32 devices in a mesh: frame: 16 (over z, y, x), space: 2 (over core).
Axes of the slice: x: 2, y: 2, z: 4, core: 2. Of those that a mesh axis runs over, the one named last changes fastest.
Arguments:
- block_input: bfloat16 [2, 4096, 768], P(None, ('frame', 'space')), may hold values from -6 to 6
- norm1_gain: float32 [768], replicated, may hold values from 0.5 to 1.5
- w_query: bfloat16 [768, 768], replicated, may hold values from -0.3125 to 0.3125
- w_key: bfloat16 [768, 768], replicated, may hold values from -0.3125 to 0.3125
- w_value: bfloat16 [768, 768], replicated, may hold values from -0.21875 to 0.21875
- w_out: bfloat16 [768, 768], replicated, may hold values from -1.75 to 1.75
- norm2_gain: float32 [768], replicated, may hold values from 0.5 to 1.5
- w_up: bfloat16 [768, 3072], replicated, may hold values from -0.21875 to 0.21875
- w_down: bfloat16 [3072, 768], replicated, may hold values from -0.109375 to 0.109375
- clip_frames: int32 [2, 4], replicated, may hold values from 0 to 16, as said below
- cotangent: bfloat16 [2, 4096, 768], P(None, ('frame', 'space')), may hold values from -6 to 6
Outputs:
- block_output: bfloat16 [2, 4096, 768], P(None, ('frame', 'space'))
- grad_input: float32 [2, 4096, 768], P(None, ('frame', 'space'))
- grad_norm1_gain: float32 [768], replicated
- grad_w_query: float32 [768, 768], replicated
- grad_w_key: float32 [768, 768], replicated
- grad_w_value: float32 [768, 768], replicated
- grad_w_out: float32 [768, 768], replicated
- grad_norm2_gain: float32 [768], replicated
- grad_w_up: float32 [768, 3072], replicated
- grad_w_down: float32 [3072, 768], replicated
The draws below stay inside these ranges and needn't reach their ends.
Inputs may be any that keep to these rules, and one draw needn't show every extreme that they name: `clip_frames`: row s lists the lengths in frames of stream s's clips in order; each row sums to 16; a length is 0 or a multiple of 4, and zeros come only after the last clip; in one stream, drawn from the seed, a single clip holds all 16 frames.
All inputs are finite; a program needn't handle non-finite values.
Results may differ from the reference program's by a relative error of at most 0.017.
Values may be sent and summed in bfloat16 or wider, within the bound.
No kernel may reach another device: no remote copies, remote signals or barrier semaphores. Data moves between devices by JAX's collectives and lax.ppermute only.
A program may use at most 320 MiB of HBM per device.

```python
import math
import jax
import jax.numpy as jnp
from jax import lax

D = 768
HEADS = 12
HEAD_DIM = 64
FF = 3072
STREAMS = 2
TPF = 256
MIN_FRAMES = 4
NF = 16
CLIPS = 4
NTOK = 4096


def draw_clip_frames(key, part):
    key = jax.random.fold_in(key, 7)
    flag_key, pick_key = jax.random.split(key)
    flags = jax.random.randint(flag_key, (STREAMS, CLIPS), 0, 2, dtype=jnp.int32)
    column = jnp.arange(CLIPS, dtype=jnp.int32)[None, :]
    stream_row = jnp.arange(STREAMS, dtype=jnp.int32)[:, None]
    chosen = jax.random.randint(pick_key, (), 0, STREAMS, dtype=jnp.int32)
    flags = jnp.where(column == 0, 1, flags)
    flags = jnp.where(stream_row == chosen, (column == 0).astype(jnp.int32), flags)
    clip_index = jnp.cumsum(flags, axis=1, dtype=jnp.int32) - 1
    matches = clip_index[:, :, None] == jnp.arange(CLIPS, dtype=jnp.int32)[None, None, :]
    return (MIN_FRAMES * jnp.sum(matches.astype(jnp.int32), axis=1, dtype=jnp.int32)).astype(jnp.int32)


def levels(rng, shape, cuts, smallest, top_value):
    def one(dim, parts):
        draws = jax.random.uniform(jax.random.fold_in(jax.random.fold_in(rng, 6), dim), (parts,), jnp.float32, smallest / len(cuts), top_value / len(cuts))
        return jnp.repeat(jnp.exp(draws), shape[dim] // parts).reshape((-1,) + (1,) * (len(shape) - dim - 1))

    level = one(*cuts[0])
    for cut in cuts[1:]:
        level = level * one(*cut)
    return level


def normal_values(stream_key, extent, scale, reach, cuts=(), held_as=jnp.bfloat16):
    loudness = levels(stream_key, extent, cuts, -0.22, 0.18) if cuts else 1.0
    values = jax.random.normal(stream_key, extent, jnp.float32) * scale * loudness
    return jnp.minimum(jnp.maximum(values, -reach), reach).astype(held_as)


def setup_inputs(seed: int = 0) -> dict:
    seeds = jax.random.split(jax.random.key(seed), 12)
    block_input = normal_values(seeds[0], (STREAMS, NTOK, D), 1.0, 6.0, ((1, 32),))
    norm1_gain = jnp.clip(1.0 + 0.1 * jax.random.normal(seeds[1], (D,), jnp.float32), 0.5, 1.5)
    w_query = normal_values(seeds[2], (D, D), (D // 2) ** -0.5, 0.3125)
    w_key = normal_values(seeds[3], (D, D), (D // 2) ** -0.5, 0.3125)
    w_value = normal_values(seeds[4], (D, D), D ** -0.5, 0.21875)
    w_out = normal_values(seeds[5], (D, D), (max(D // 64, 1)) ** -0.5, 1.75)
    norm2_gain = jnp.clip(1.0 + 0.1 * jax.random.normal(seeds[6], (D,), jnp.float32), 0.5, 1.5)
    w_up = normal_values(seeds[7], (D, FF), D ** -0.5, 0.21875)
    w_down = normal_values(seeds[8], (FF, D), FF ** -0.5, 0.109375)
    clip_frames = draw_clip_frames(jax.random.fold_in(seeds[11], 71), 0)
    cotangent = normal_values(seeds[10], (STREAMS, NTOK, D), 1.0, 6.0, ((1, 32),))
    return dict(block_input=block_input, norm1_gain=norm1_gain, w_query=w_query, w_key=w_key, w_value=w_value, w_out=w_out, norm2_gain=norm2_gain, w_up=w_up, w_down=w_down, clip_frames=clip_frames, cotangent=cotangent)


@jax.custom_vjp
def low(v):
    return lax.optimization_barrier(v.astype(jnp.bfloat16)).astype(jnp.float32)

@jax.custom_vjp
def low_back(v):
    return v

def low_keep(v):
    return (low(v), None)

def low_pass(kept, grad):
    return (grad,)

def back_keep(v):
    return (v, None)

def back_low(kept, grad):
    return (low(grad),)
low.defvjp(low_keep, low_pass)
low_back.defvjp(back_keep, back_low)

def layer_norm(values, gain_vector):
    average = lax.optimization_barrier(jnp.mean(values, axis=-1, keepdims=True))
    centred = values - average
    spread = lax.optimization_barrier(jnp.mean(centred * centred, axis=-1, keepdims=True))
    return centred * lax.rsqrt(spread + 1e-05) * gain_vector

def frame_tables(clip_frames, clip_first, frame_count):
    clip_ends = jnp.cumsum(clip_frames, axis=1, dtype=jnp.int32)
    clip_begins = clip_ends - clip_frames
    frame_index = jnp.arange(frame_count, dtype=jnp.int32)
    inside = (frame_index[None, :, None] >= clip_begins[:, None, :]) & (frame_index[None, :, None] < clip_ends[:, None, :])
    frame_begin = lax.optimization_barrier(jnp.sum(jnp.where(inside, clip_begins[:, None, :], 0), axis=2, dtype=jnp.int32))
    offsets = lax.optimization_barrier(jnp.sum(jnp.where(inside, clip_first[:, None, :] - clip_begins[:, None, :], 0), axis=2, dtype=jnp.int32))
    return (frame_begin, offsets + frame_index[None, :])

def rotate(values, cosine, sine_table):
    half_width = values.shape[-1] // 2
    turned = jnp.concatenate([-values[..., half_width:], values[..., :half_width]], axis=-1)
    return values * cosine + turned * sine_table

def matmul_high(left, right):
    return jnp.dot(left, right, precision=lax.Precision.HIGHEST, preferred_element_type=jnp.float32)

def stream_forward(stream_input, position, query_frame, query_begin, params):
    gain_one, query_weight, key_weight, value_weight, out_weight, gain_two, up_weight, down_weight = params
    normed = low(layer_norm(stream_input, gain_one))
    half_width = HEAD_DIM // 2
    frequency = jnp.exp(jnp.arange(half_width, dtype=jnp.float32) * (-2.0 * math.log(10000.0) / HEAD_DIM))
    angles = position.astype(jnp.float32)[:, None] * frequency[None, :]
    cosine = jnp.concatenate([jnp.cos(angles), jnp.cos(angles)], axis=-1)[:, None, :]
    sine_table = jnp.concatenate([jnp.sin(angles), jnp.sin(angles)], axis=-1)[:, None, :]
    queries = low(rotate(low_back(matmul_high(normed, query_weight)).reshape(NTOK, HEADS, HEAD_DIM), cosine, sine_table))
    keys_all = low(rotate(low_back(matmul_high(normed, key_weight)).reshape(NTOK, HEADS, HEAD_DIM), cosine, sine_table))
    values_all = low(low_back(matmul_high(normed, value_weight))).reshape(NTOK, HEADS, HEAD_DIM)
    block_rows = math.gcd(NTOK, 512)
    blocks = NTOK // block_rows
    key_frame = jnp.arange(NTOK, dtype=jnp.int32) // TPF
    scale_factor = 1.0 / math.sqrt(HEAD_DIM)

    def attend_block(pieces):
        query_block, frame_block, begin_block = pieces
        raw_scores = jnp.einsum('qhd,khd->hqk', query_block, keys_all, precision=lax.Precision.HIGHEST)
        scores = low_back(raw_scores) * scale_factor
        allowed = (key_frame[None, :] >= begin_block[:, None]) & (key_frame[None, :] <= frame_block[:, None])
        scores = jnp.where(allowed[None], scores, -1e+30)
        weights = jax.nn.softmax(scores, axis=-1)
        return jnp.einsum('hqk,khd->qhd', low(weights), values_all, precision=lax.Precision.HIGHEST)
    attended = lax.map(jax.checkpoint(attend_block), (queries.reshape(blocks, block_rows, HEADS, HEAD_DIM), query_frame.reshape(blocks, block_rows), query_begin.reshape(blocks, block_rows)))
    attended = low(low_back(attended.reshape(NTOK, D)))
    middle = stream_input + low_back(matmul_high(attended, out_weight))
    normed_two = low(layer_norm(middle, gain_two))
    hidden = low_back(matmul_high(normed_two, up_weight))
    activated = low(jax.nn.gelu(hidden, approximate=True))
    return middle + low_back(matmul_high(activated, down_weight))

def reference(block_input, norm1_gain, w_query, w_key, w_value, w_out, norm2_gain, w_up, w_down, clip_frames, cotangent):
    frame_begin, frame_time = frame_tables(clip_frames, jnp.zeros_like(clip_frames), NF)
    token_index = jnp.arange(NTOK, dtype=jnp.int32)
    token_frame = token_index // TPF
    query_begin = frame_begin[:, token_frame]
    position = frame_time[:, token_frame] * TPF + token_index % TPF

    def forward(inputs, gain_one, query_weight, key_weight, value_weight, out_weight, gain_two, up_weight, down_weight):
        params = (gain_one, query_weight, key_weight, value_weight, out_weight, gain_two, up_weight, down_weight)
        return jnp.stack([stream_forward(inputs[stream], position[stream], token_frame, query_begin[stream], params) for stream in range(STREAMS)])
    outputs, pullback = jax.vjp(forward, block_input.astype(jnp.float32), norm1_gain, w_query.astype(jnp.float32), w_key.astype(jnp.float32), w_value.astype(jnp.float32), w_out.astype(jnp.float32), norm2_gain, w_up.astype(jnp.float32), w_down.astype(jnp.float32))
    grads = pullback(cotangent.astype(jnp.float32))
    return (outputs.astype(jnp.bfloat16), grads[0], grads[1], grads[2], grads[3], grads[4], grads[5], grads[6], grads[7], grads[8])
```

```python
import functools
import math

import jax
import jax.numpy as jnp
from jax import lax
from jax.experimental import pallas as pl
from jax.experimental.pallas import tpu as pltpu
from jax.sharding import PartitionSpec as P

HEADS = 12
HEAD_DIM = 64

NEG=-1e30
def dotT(a,b,ca,cb):
    return lax.dot_general(a,b,(((ca,),(cb,)),((),())),preferred_element_type=jnp.float32)

def fwd_kernel(lo_ref, r_ref, o_ref, lse_ref, kn, qt, vt, s_buf, *, nf, rows, G):
    spc = r_ref.shape[0]//nf
    tpf = spc*rows
    for_ = r_ref.shape[0]
    def prep(d, _):
        kT = r_ref[d, 64:128, :]
        kn[pl.ds(pl.multiple_of(d*rows,rows), rows), :] = kT.T
        return 0
    lax.fori_loop(0, for_, prep, 0)
    def prep2(f, _):
        qt[f] = jnp.concatenate([r_ref[f*spc+j,0:64,:] for j in range(spc)],axis=1)
        vt[f] = jnp.concatenate([r_ref[f*spc+j,128:192,:] for j in range(spc)],axis=1)
        return 0
    lax.fori_loop(0, nf, prep2, 0)
    def one_frame(f, _):
        lo = lo_ref[f]
        q = qt[f]
        n = (f - lo)//G
        def scores(g0, cnt):
            return dotT(kn[pl.ds(pl.multiple_of(g0*tpf,tpf), cnt*tpf), :], q, 1, 0)
        def step(g0, cnt, s, state):
            m, l, o = state
            mn = jnp.maximum(m, jnp.max(s, axis=0, keepdims=True))
            a = jnp.exp(m-mn)
            p = jnp.exp(s-mn)
            l = l*a + jnp.sum(p,axis=0,keepdims=True)
            pb = p.astype(jnp.bfloat16)
            o = o*a
            for j in range(cnt):
                o = o + dotT(vt[g0+j], pb[j*tpf:(j+1)*tpf], 1, 0)
            return mn,l,o
        state=(jnp.full((1,tpf),NEG,jnp.float32),jnp.zeros((1,tpf),jnp.float32),jnp.zeros((64,tpf),jnp.float32))
        def body(i, st):
            g0 = lo+i*G
            return step(g0, G, scores(g0,G), st)
        state=lax.fori_loop(0,n,body,state)
        def tail(i, st):
            g0 = lo+n*G+i
            return step(g0,1,scores(g0,1),st)
        state=lax.fori_loop(0, f-lo-n*G+1, tail, state)
        m,l,o=state
        o = o/l
        for j in range(spc):
            o_ref[f*spc+j] = o[:,j*rows:(j+1)*rows]
        lse_ref[f] = m+jnp.log(l)
        return 0
    lax.fori_loop(0,nf,one_frame,0)

def attn_fwd(lo, r, nf, G=4):
    nd,_,rows=r.shape
    tpf=nd//nf*rows
    return pl.pallas_call(functools.partial(fwd_kernel,nf=nf,rows=rows,G=G),
        out_shape=(jax.ShapeDtypeStruct((nd,64,rows),jnp.float32),jax.ShapeDtypeStruct((nf,1,tpf),jnp.float32)),
        in_specs=[pl.BlockSpec(memory_space=pltpu.SMEM),pl.BlockSpec(memory_space=pltpu.VMEM)],
        out_specs=(pl.BlockSpec(memory_space=pltpu.VMEM),)*2,
        scratch_shapes=[pltpu.VMEM((nd*rows,64),jnp.bfloat16),pltpu.VMEM((nf,64,tpf),jnp.bfloat16),pltpu.VMEM((nf,64,tpf),jnp.bfloat16),pltpu.VMEM((G*tpf,tpf),jnp.float32)],
        compiler_params=pltpu.CompilerParams(vmem_limit_bytes=48*2**20),
        name="attn_fwd")(lo,r)

def bwd_kernel(hi_ref, r_ref, do_ref, o_ref, lse_ref, d_ref, kn, vn, qt, qn, don, dot_, dq, delta, *, nf, rows):
    nd=r_ref.shape[0]; spc=nd//nf; tpf=spc*rows
    def prep(f,_):
        for j in range(spc):
            d=f*spc+j
            blk=r_ref[d]
            sl=pl.ds(pl.multiple_of(d*rows,rows),rows)
            kn[sl,:]=blk[64:128].T
            vn[sl,:]=blk[128:192].T
            qn[sl,:]=blk[0:64].T
            don[sl,:]=do_ref[d].T
        qt[f]=jnp.concatenate([r_ref[f*spc+j,0:64,:] for j in range(spc)],axis=1)
        dd=jnp.concatenate([do_ref[f*spc+j] for j in range(spc)],axis=1)
        oo=jnp.concatenate([o_ref[f*spc+j] for j in range(spc)],axis=1)
        dot_[f]=dd
        delta[f]=jnp.sum(dd.astype(jnp.float32)*oo,axis=0,keepdims=True)
        dq[f]=jnp.zeros((64,tpf),jnp.float32)
        return 0
    lax.fori_loop(0,nf,prep,0)
    def one_key(kf,_):
        sl=pl.ds(pl.multiple_of(kf*tpf,tpf),tpf)
        k=kn[sl,:]; v=vn[sl,:]
        kT=jnp.concatenate([r_ref[kf*spc+j,64:128,:] for j in range(spc)],axis=1)
        def body(f, st):
            dk,dv=st
            qsl=pl.ds(pl.multiple_of(f*tpf,tpf),tpf)
            s=dotT(k,qt[f],1,0)
            p=jnp.exp(s-lse_ref[f])
            dp=dotT(v,dot_[f],1,0)
            ds=(p*(dp-delta[f])).astype(jnp.bfloat16)
            dv=dv+dotT(p.astype(jnp.bfloat16),don[qsl,:],1,0)
            dk=dk+dotT(ds,qn[qsl,:],1,0)
            dq[f]=dq[f]+dotT(kT,ds,1,0)
            return dk,dv
        z=jnp.zeros((tpf,64),jnp.float32)
        dk,dv=lax.fori_loop(kf,hi_ref[kf],body,(z,z))
        dkT=dk.T; dvT=dv.T
        for j in range(spc):
            d_ref[kf*spc+j,64:128,:]=dkT[:,j*rows:(j+1)*rows].astype(jnp.bfloat16)
            d_ref[kf*spc+j,128:192,:]=dvT[:,j*rows:(j+1)*rows].astype(jnp.bfloat16)
        return 0
    lax.fori_loop(0,nf,one_key,0)
    def fin(f,_):
        x=dq[f]
        for j in range(spc):
            d_ref[f*spc+j,0:64,:]=x[:,j*rows:(j+1)*rows].astype(jnp.bfloat16)
        return 0
    lax.fori_loop(0,nf,fin,0)

def attn_bwd(hi, r, do, o, lse, nf):
    nd,_,rows=r.shape; tpf=nd//nf*rows; n=nd*rows
    V=pltpu.VMEM
    return pl.pallas_call(functools.partial(bwd_kernel,nf=nf,rows=rows),
        out_shape=jax.ShapeDtypeStruct((nd,192,rows),jnp.bfloat16),
        in_specs=[pl.BlockSpec(memory_space=pltpu.SMEM)]+[pl.BlockSpec(memory_space=V)]*4,
        out_specs=pl.BlockSpec(memory_space=V),
        scratch_shapes=[V((n,64),jnp.bfloat16)]*2+[V((nf,64,tpf),jnp.bfloat16)]+[V((n,64),jnp.bfloat16)]*2+[V((nf,64,tpf),jnp.bfloat16),V((nf,64,tpf),jnp.float32),V((nf,1,tpf),jnp.float32)],
        compiler_params=pltpu.CompilerParams(vmem_limit_bytes=48*2**20),
        name="attn_bwd")(hi,r,do,o,lse)


def layer_norm(values, gain_vector):
    average = jnp.mean(values, axis=-1, keepdims=True)
    centred = values - average
    spread = jnp.mean(centred * centred, axis=-1, keepdims=True)
    return centred * lax.rsqrt(spread + 1e-05) * gain_vector


def frame_tables(clip_frames, frame_count):
    clip_ends = jnp.cumsum(clip_frames, axis=1, dtype=jnp.int32)
    clip_begins = clip_ends - clip_frames
    frame_index = jnp.arange(frame_count, dtype=jnp.int32)
    inside = (frame_index[None, :, None] >= clip_begins[:, None, :]) & (
        frame_index[None, :, None] < clip_ends[:, None, :]
    )
    begin = jnp.sum(jnp.where(inside, clip_begins[:, None, :], 0), axis=2, dtype=jnp.int32)
    end = jnp.sum(jnp.where(inside, clip_ends[:, None, :], 0), axis=2, dtype=jnp.int32)
    return begin, end


def dot(left, right, left_dim, right_dim):
    return lax.dot_general(
        left,
        right,
        (((left_dim,), (right_dim,)), ((), ())),
        preferred_element_type=jnp.float32,
    )


def turn(values, cosine, sine, sign):
    first, second = values[:, 0], values[:, 1]
    return jnp.stack(
        [first * cosine - sign * second * sine, second * cosine + sign * first * sine], axis=1
    )


def local(
    block_input,
    norm1_gain,
    w_query,
    w_key,
    w_value,
    w_out,
    norm2_gain,
    w_up,
    w_down,
    clip_frames,
    cotangent,
):
    streams, rows, width = block_input.shape
    heads, head_width = HEADS, HEAD_DIM
    half = head_width // 2
    frames = lax.axis_size("frame")
    spaces = lax.axis_size("space")
    devices = frames * spaces
    pairs = streams * heads
    per_frame = rows * spaces
    tokens = streams * rows
    axes = ("frame", "space")
    frame_place = lax.axis_index("frame")
    space_place = lax.axis_index("space")
    low = jnp.bfloat16

    begin, end = frame_tables(clip_frames, frames)
    frame_ids = jnp.arange(frames, dtype=jnp.int32)
    my_time = jnp.sum(
        jnp.where(frame_ids[None, :] == frame_place, frame_ids[None, :] - begin, 0), axis=1
    )
    within = space_place * rows + jnp.arange(rows, dtype=jnp.int32)
    position = (my_time[:, None] * per_frame + within[None, :]).astype(jnp.float32)
    frequency = jnp.exp(
        jnp.arange(half, dtype=jnp.float32) * (-2.0 * math.log(10000.0) / head_width)
    )
    angles = frequency[:, None, None] * position[None]
    cosine, sine = jnp.cos(angles), jnp.sin(angles)

    mine = frame_place * spaces + space_place
    my_stream = jnp.minimum(mine // heads, streams - 1)
    idle = mine >= pairs
    picked = jnp.arange(streams, dtype=jnp.int32)[:, None] == my_stream
    lo = jnp.where(idle, frame_ids, jnp.sum(jnp.where(picked, begin, 0), axis=0))
    hi = jnp.where(idle, frame_ids, jnp.sum(jnp.where(picked, end, 0), axis=0))

    def to_heads(parts):
        whole = jnp.stack(parts, axis=1).transpose(3, 0, 1, 2, 4)
        whole = whole.reshape(pairs, len(parts) * head_width, rows)
        whole = jnp.pad(whole, ((0, devices - pairs), (0, 0), (0, 0)))
        return lax.all_to_all(whole, axes, 0, 0, tiled=True)

    def to_tokens(whole, count):
        back = lax.all_to_all(whole, axes, 0, 0, tiled=True)[:pairs]
        back = back.reshape(streams, heads, count, head_width, rows)
        return back.transpose(2, 1, 3, 0, 4)

    input_flat = block_input.astype(jnp.float32).reshape(tokens, width)
    normed = layer_norm(input_flat, norm1_gain).astype(low)

    def project(weight):
        return dot(weight, normed, 0, 1)

    def rope(value):
        value = value.reshape(heads, 2, half, streams, rows)
        return turn(value, cosine, sine, 1.0).reshape(heads, head_width, streams, rows)

    scale = 1.0 / math.sqrt(head_width)
    query = (rope(project(w_query)) * scale).astype(low)
    key = rope(project(w_key)).astype(low)
    value = project(w_value).astype(low).reshape(heads, head_width, streams, rows)
    packed = to_heads([query, key, value])
    attended_own, lse = attn_fwd(lo, packed, frames)
    attended = to_tokens(attended_own.astype(low), 1)[0].reshape(width, tokens)

    middle = input_flat + dot(attended, w_out, 0, 0)
    normed_two = layer_norm(middle, norm2_gain).astype(low)
    hidden = dot(normed_two, w_up, 1, 0)
    activated, gelu_back = jax.vjp(lambda inner: jax.nn.gelu(inner, approximate=True), hidden)
    activated_low = activated.astype(low)
    block_output = (middle + dot(activated_low, w_down, 1, 0)).astype(low)
    cot_flat = cotangent.reshape(tokens, width)
    d_activated = dot(cot_flat, w_down, 1, 1)
    d_hidden = gelu_back(d_activated)[0].astype(low)
    d_normed_two = dot(d_hidden, w_up, 1, 1)
    unused_two, norm_two_back = jax.vjp(layer_norm, middle, norm2_gain)
    d_middle_norm, grad_gain_two = norm_two_back(d_normed_two)
    d_middle = cot_flat.astype(jnp.float32) + d_middle_norm
    d_branch = d_middle.astype(low)
    d_attended = dot(w_out, d_branch, 1, 1).astype(low)
    d_own = to_heads([d_attended.reshape(heads, head_width, streams, rows)])

    grad_down = dot(activated_low, cot_flat, 0, 0)
    grad_up = dot(normed_two, d_hidden, 0, 0)
    grad_out = dot(attended, d_branch, 1, 0)
    early = lax.psum((grad_down.astype(low), grad_up.astype(low), grad_out.astype(low)), axes)

    grads_own = attn_bwd(hi, packed, d_own, attended_own, lse, frames)
    d_three = to_tokens(grads_own, 3)

    def rope_back(value):
        value = value.astype(jnp.float32).reshape(heads, 2, half, streams, rows)
        return turn(value, cosine, sine, -1.0).reshape(width, tokens)

    d_query = (rope_back(d_three[0]) * scale).astype(low)
    d_key = rope_back(d_three[1]).astype(low)
    d_value = d_three[2].reshape(width, tokens)
    grad_query = dot(normed, d_query, 0, 1)
    grad_key = dot(normed, d_key, 0, 1)
    grad_value = dot(normed, d_value, 0, 1)
    d_normed = (
        dot(d_query, w_query, 0, 1) + dot(d_key, w_key, 0, 1) + dot(d_value, w_value, 0, 1)
    )
    unused_one, norm_one_back = jax.vjp(layer_norm, input_flat, norm1_gain)
    d_input_norm, grad_gain_one = norm_one_back(d_normed)
    grad_input = (d_middle + d_input_norm).reshape(streams, rows, width)
    late = lax.psum(
        (grad_query.astype(low), grad_key.astype(low), grad_value.astype(low)), axes
    )
    gains = lax.psum((grad_gain_one, grad_gain_two), axes)
    wide = lambda member: member.astype(jnp.float32)
    return (
        block_output.reshape(streams, rows, width),
        grad_input,
        gains[0],
        wide(late[0]),
        wide(late[1]),
        wide(late[2]),
        wide(early[2]),
        gains[1],
        wide(early[1]),
        wide(early[0]),
    )


def solution(mesh):
    spread = P(None, ("frame", "space"), None)
    in_specs = (spread,) + (P(),) * 9 + (spread,)
    out_specs = (spread, spread) + (P(),) * 8
    return jax.shard_map(local, mesh=mesh, in_specs=in_specs, out_specs=out_specs, check_vma=False)
```

```python
import functools
import math

import jax
import jax.numpy as jnp
from jax import lax
from jax.experimental import pallas as pl
from jax.experimental.pallas import tpu as pltpu
from jax.sharding import PartitionSpec as P

HEADS = 12
HEAD_DIM = 64

NEG=-1e30
def dotT(a,b,ca,cb):
    return lax.dot_general(a,b,(((ca,),(cb,)),((),())),preferred_element_type=jnp.float32)

def fwd_kernel(lo_ref, r_ref, o_ref, lse_ref, kn, qt, vt, s_buf, *, nf, rows, G):
    spc = r_ref.shape[0]//nf
    tpf = spc*rows
    for_ = r_ref.shape[0]
    def prep(d, _):
        kT = r_ref[d, 64:128, :]
        kn[pl.ds(pl.multiple_of(d*rows,rows), rows), :] = kT.T
        return 0
    lax.fori_loop(0, for_, prep, 0)
    def prep2(f, _):
        qt[f] = jnp.concatenate([r_ref[f*spc+j,0:64,:] for j in range(spc)],axis=1)
        vt[f] = jnp.concatenate([r_ref[f*spc+j,128:192,:] for j in range(spc)],axis=1)
        return 0
    lax.fori_loop(0, nf, prep2, 0)
    def one_frame(f, _):
        lo = lo_ref[f]
        q = qt[f]
        n = (f - lo)//G
        def scores(g0, cnt):
            return dotT(kn[pl.ds(pl.multiple_of(g0*tpf,tpf), cnt*tpf), :], q, 1, 0)
        def step(g0, cnt, s, state):
            m, l, o = state
            mn = jnp.maximum(m, jnp.max(s, axis=0, keepdims=True))
            a = jnp.exp(m-mn)
            p = jnp.exp(s-mn)
            l = l*a + jnp.sum(p,axis=0,keepdims=True)
            pb = p.astype(jnp.bfloat16)
            o = o*a
            for j in range(cnt):
                o = o + dotT(vt[g0+j], pb[j*tpf:(j+1)*tpf], 1, 0)
            return mn,l,o
        state=(jnp.full((1,tpf),NEG,jnp.float32),jnp.zeros((1,tpf),jnp.float32),jnp.zeros((64,tpf),jnp.float32))
        def body(i, st):
            g0 = lo+i*G
            return step(g0, G, scores(g0,G), st)
        state=lax.fori_loop(0,n,body,state)
        def tail(i, st):
            g0 = lo+n*G+i
            return step(g0,1,scores(g0,1),st)
        state=lax.fori_loop(0, f-lo-n*G+1, tail, state)
        m,l,o=state
        o = o/l
        for j in range(spc):
            o_ref[f*spc+j] = o[:,j*rows:(j+1)*rows]
        lse_ref[f] = m+jnp.log(l)
        return 0
    lax.fori_loop(0,nf,one_frame,0)

def attn_fwd(lo, r, nf, G=4):
    nd,_,rows=r.shape
    tpf=nd//nf*rows
    return pl.pallas_call(functools.partial(fwd_kernel,nf=nf,rows=rows,G=G),
        out_shape=(jax.ShapeDtypeStruct((nd,64,rows),jnp.float32),jax.ShapeDtypeStruct((nf,1,tpf),jnp.float32)),
        in_specs=[pl.BlockSpec(memory_space=pltpu.SMEM),pl.BlockSpec(memory_space=pltpu.VMEM)],
        out_specs=(pl.BlockSpec(memory_space=pltpu.VMEM),)*2,
        scratch_shapes=[pltpu.VMEM((nd*rows,64),jnp.bfloat16),pltpu.VMEM((nf,64,tpf),jnp.bfloat16),pltpu.VMEM((nf,64,tpf),jnp.bfloat16),pltpu.VMEM((G*tpf,tpf),jnp.float32)],
        compiler_params=pltpu.CompilerParams(vmem_limit_bytes=48*2**20),
        name="attn_fwd")(lo,r)

def bwd_kernel(hi_ref, r_ref, do_ref, o_ref, lse_ref, d_ref, kn, vn, qt, qn, don, dot_, dq, delta, *, nf, rows):
    nd=r_ref.shape[0]; spc=nd//nf; tpf=spc*rows
    def prep(f,_):
        for j in range(spc):
            d=f*spc+j
            blk=r_ref[d]
            sl=pl.ds(pl.multiple_of(d*rows,rows),rows)
            kn[sl,:]=blk[64:128].T
            vn[sl,:]=blk[128:192].T
            qn[sl,:]=blk[0:64].T
            don[sl,:]=do_ref[d].T
        qt[f]=jnp.concatenate([r_ref[f*spc+j,0:64,:] for j in range(spc)],axis=1)
        dd=jnp.concatenate([do_ref[f*spc+j] for j in range(spc)],axis=1)
        oo=jnp.concatenate([o_ref[f*spc+j] for j in range(spc)],axis=1)
        dot_[f]=dd
        delta[f]=jnp.sum(dd.astype(jnp.float32)*oo,axis=0,keepdims=True)
        dq[f]=jnp.zeros((64,tpf),jnp.float32)
        return 0
    lax.fori_loop(0,nf,prep,0)
    def one_key(kf,_):
        sl=pl.ds(pl.multiple_of(kf*tpf,tpf),tpf)
        k=kn[sl,:]; v=vn[sl,:]
        kT=jnp.concatenate([r_ref[kf*spc+j,64:128,:] for j in range(spc)],axis=1)
        def body(f, st):
            dk,dv=st
            qsl=pl.ds(pl.multiple_of(f*tpf,tpf),tpf)
            s=dotT(k,qt[f],1,0)
            p=jnp.exp(s-lse_ref[f])
            dp=dotT(v,dot_[f],1,0)
            ds=(p*(dp-delta[f])).astype(jnp.bfloat16)
            dv=dv+dotT(p.astype(jnp.bfloat16),don[qsl,:],1,0)
            dk=dk+dotT(ds,qn[qsl,:],1,0)
            dq[f]=dq[f]+dotT(kT,ds,1,0)
            return dk,dv
        z=jnp.zeros((tpf,64),jnp.float32)
        dk,dv=lax.fori_loop(kf,hi_ref[kf],body,(z,z))
        dkT=dk.T; dvT=dv.T
        for j in range(spc):
            d_ref[kf*spc+j,64:128,:]=dkT[:,j*rows:(j+1)*rows].astype(jnp.bfloat16)
            d_ref[kf*spc+j,128:192,:]=dvT[:,j*rows:(j+1)*rows].astype(jnp.bfloat16)
        return 0
    lax.fori_loop(0,nf,one_key,0)
    def fin(f,_):
        x=dq[f]
        for j in range(spc):
            d_ref[f*spc+j,0:64,:]=x[:,j*rows:(j+1)*rows].astype(jnp.bfloat16)
        return 0
    lax.fori_loop(0,nf,fin,0)

def attn_bwd(hi, r, do, o, lse, nf):
    nd,_,rows=r.shape; tpf=nd//nf*rows; n=nd*rows
    V=pltpu.VMEM
    return pl.pallas_call(functools.partial(bwd_kernel,nf=nf,rows=rows),
        out_shape=jax.ShapeDtypeStruct((nd,192,rows),jnp.bfloat16),
        in_specs=[pl.BlockSpec(memory_space=pltpu.SMEM)]+[pl.BlockSpec(memory_space=V)]*4,
        out_specs=pl.BlockSpec(memory_space=V),
        scratch_shapes=[V((n,64),jnp.bfloat16)]*2+[V((nf,64,tpf),jnp.bfloat16)]+[V((n,64),jnp.bfloat16)]*2+[V((nf,64,tpf),jnp.bfloat16),V((nf,64,tpf),jnp.float32),V((nf,1,tpf),jnp.float32)],
        compiler_params=pltpu.CompilerParams(vmem_limit_bytes=48*2**20),
        name="attn_bwd")(hi,r,do,o,lse)


def layer_norm(values, gain_vector):
    average = jnp.mean(values, axis=-1, keepdims=True)
    centred = values - average
    spread = jnp.mean(centred * centred, axis=-1, keepdims=True)
    return centred * lax.rsqrt(spread + 1e-05) * gain_vector


def frame_tables(clip_frames, frame_count):
    clip_ends = jnp.cumsum(clip_frames, axis=1, dtype=jnp.int32)
    clip_begins = clip_ends - clip_frames
    frame_index = jnp.arange(frame_count, dtype=jnp.int32)
    inside = (frame_index[None, :, None] >= clip_begins[:, None, :]) & (
        frame_index[None, :, None] < clip_ends[:, None, :]
    )
    begin = jnp.sum(jnp.where(inside, clip_begins[:, None, :], 0), axis=2, dtype=jnp.int32)
    end = jnp.sum(jnp.where(inside, clip_ends[:, None, :], 0), axis=2, dtype=jnp.int32)
    return begin, end


def dot(left, right, left_dim, right_dim):
    return lax.dot_general(
        left,
        right,
        (((left_dim,), (right_dim,)), ((), ())),
        preferred_element_type=jnp.float32,
    )


def turn(values, cosine, sine, sign):
    first, second = values[:, 0], values[:, 1]
    return jnp.stack(
        [first * cosine - sign * second * sine, second * cosine + sign * first * sine], axis=1
    )


class Ring:
    def __init__(self):
        self.frames = lax.axis_size("frame")
        self.spaces = lax.axis_size("space")
        self.planes = self.frames // 4
        frame = lax.axis_index("frame")
        self.core = lax.axis_index("space")
        self.plane = frame // 4
        self.spot = frame % 4
        self.bits = (frame % 2, (frame // 2) % 2)
        self.first_bit = jnp.where(self.core == 0, self.bits[0], self.bits[1])
        self.second_bit = jnp.where(self.core == 0, self.bits[1], self.bits[0])

    def send(self, value, target):
        moves = []
        for frame in range(self.frames):
            for core in range(self.spaces):
                to_frame, to_core = target(frame, core)
                moves.append((frame * self.spaces + core, to_frame * self.spaces + to_core))
        return lax.ppermute(value, ("frame", "space"), moves)

    def first(self, value):
        return self.send(value, lambda frame, core: (frame ^ (1 if core == 0 else 2), core))

    def second(self, value):
        return self.send(value, lambda frame, core: (frame ^ (2 if core == 0 else 1), core))

    def across(self, value):
        return self.send(value, lambda frame, core: (frame, 1 - core))

    def up(self, value, step):
        size = self.frames
        return self.send(value, lambda frame, core: ((frame + 4 * step) % size, core))

    def plane_sum(self, value):
        count = self.planes
        rows, columns = value.shape
        cut = value.reshape(count, rows // count, columns)
        pick = lambda index: lax.dynamic_index_in_dim(cut, index % count, 0, keepdims=False)
        total = pick(self.plane)
        for step in range(1, count):
            piece = pick(self.plane + step).astype(jnp.bfloat16)
            total = total + self.up(piece, step).astype(jnp.float32)
        total = total.astype(jnp.bfloat16)
        parts = [total] + [self.up(total, step) for step in range(1, count)]
        twice = jnp.stack(parts[::-1] * 2)
        start = (count - 1 - self.plane) % count
        whole = lax.dynamic_slice_in_dim(twice, start, count, 0)
        return whole.reshape(rows, columns)

    def plane_gather(self, value):
        one = self.second(value)
        pair = jnp.stack([value, one])
        two = self.first(pair)
        mine = jnp.concatenate([pair, two], axis=0)
        return mine, self.across(mine)

    def gather_spots(self):
        near = jnp.where(self.core == 0, 2, 1)
        own = jnp.stack([self.spot, self.spot ^ near, self.spot ^ (3 - near), self.spot ^ 3])
        other = jnp.stack([self.spot, self.spot ^ (3 - near), self.spot ^ near, self.spot ^ 3])
        cores = jnp.repeat(jnp.stack([self.core, 1 - self.core]), 4)
        return jnp.concatenate([own, other]), cores

    def half_sums(self, value):
        for bit, exchange in ((self.first_bit, self.first), (self.second_bit, self.second)):
            rows, columns = value.shape
            cut = value.reshape(2, rows // 2, columns)
            keep = lax.dynamic_index_in_dim(cut, bit, 0, keepdims=False)
            give = lax.dynamic_index_in_dim(cut, 1 - bit, 0, keepdims=False)
            value = keep + exchange(give.astype(jnp.bfloat16)).astype(jnp.float32)
        return value


def quarter_rows(spots, cores):
    return jnp.where(cores == 1, spots, (spots % 2) * 2 + spots // 2)


def place(mine, other, block_of, out_shape, cuts):
    count, rows, columns = mine.shape
    width = columns // cuts

    def body(where, mine_ref, other_ref, *outs):
        step = pl.program_id(0)

        def put(ref):
            for index, out in enumerate(outs):
                out[...] = ref[0, :, index * width : (index + 1) * width].astype(jnp.float32)

        @pl.when(step < count)
        def _():
            put(mine_ref)

        @pl.when(step >= count)
        def _():
            put(other_ref)

    spec = pl.BlockSpec((rows, width), lambda i, where: (where[0, i], where[1, i]))
    return pl.pallas_call(
        body,
        grid_spec=pltpu.PrefetchScalarGridSpec(
            num_scalar_prefetch=1,
            grid=(2 * count,),
            in_specs=[
                pl.BlockSpec((1, rows, columns), lambda i, where: (jnp.minimum(i, count - 1), 0, 0)),
                pl.BlockSpec((1, rows, columns), lambda i, where: (jnp.maximum(i - count, 0), 0, 0)),
            ],
            out_specs=[spec] * cuts,
        ),
        out_shape=[jax.ShapeDtypeStruct(out_shape, jnp.float32)] * cuts,
        compiler_params=pltpu.CompilerParams(vmem_limit_bytes=40 * 2**20),
        name="place",
    )(block_of, mine, other)


def local(
    block_input,
    norm1_gain,
    w_query,
    w_key,
    w_value,
    w_out,
    norm2_gain,
    w_up,
    w_down,
    clip_frames,
    cotangent,
):
    streams, rows, width = block_input.shape
    heads, head_width = HEADS, HEAD_DIM
    half = head_width // 2
    frames = lax.axis_size("frame")
    spaces = lax.axis_size("space")
    devices = frames * spaces
    pairs = streams * heads
    per_frame = rows * spaces
    tokens = streams * rows
    axes = ("frame", "space")
    frame_place = lax.axis_index("frame")
    space_place = lax.axis_index("space")
    low = jnp.bfloat16

    begin, end = frame_tables(clip_frames, frames)
    frame_ids = jnp.arange(frames, dtype=jnp.int32)
    my_time = jnp.sum(
        jnp.where(frame_ids[None, :] == frame_place, frame_ids[None, :] - begin, 0), axis=1
    )
    within = space_place * rows + jnp.arange(rows, dtype=jnp.int32)
    position = (my_time[:, None] * per_frame + within[None, :]).astype(jnp.float32)
    frequency = jnp.exp(
        jnp.arange(half, dtype=jnp.float32) * (-2.0 * math.log(10000.0) / head_width)
    )
    angles = frequency[:, None, None] * position[None]
    cosine, sine = jnp.cos(angles), jnp.sin(angles)

    ring = Ring()
    spots, cores = ring.gather_spots()
    slots = 4 * spaces
    hidden_width = w_up.shape[1]
    part = hidden_width // slots
    my_part = (ring.spot * spaces + ring.core) * part

    def plane_tokens(value):
        mine, other = ring.plane_gather(value)
        return jnp.concatenate([mine, other], axis=0).reshape(slots * tokens, width)

    cot_flat = cotangent.reshape(tokens, width)
    cot_plane = plane_tokens(cot_flat)
    up_part = lax.dynamic_slice_in_dim(w_up, my_part, part, 1)
    down_part = lax.dynamic_slice_in_dim(w_down, my_part, part, 0)

    mine = frame_place * spaces + space_place
    my_stream = jnp.minimum(mine // heads, streams - 1)
    idle = mine >= pairs
    picked = jnp.arange(streams, dtype=jnp.int32)[:, None] == my_stream
    lo = jnp.where(idle, frame_ids, jnp.sum(jnp.where(picked, begin, 0), axis=0))
    hi = jnp.where(idle, frame_ids, jnp.sum(jnp.where(picked, end, 0), axis=0))

    def to_heads(parts):
        whole = jnp.stack(parts, axis=1).transpose(3, 0, 1, 2, 4)
        whole = whole.reshape(pairs, len(parts) * head_width, rows)
        whole = jnp.pad(whole, ((0, devices - pairs), (0, 0), (0, 0)))
        return lax.all_to_all(whole, axes, 0, 0, tiled=True)

    def to_tokens(whole, count):
        back = lax.all_to_all(whole, axes, 0, 0, tiled=True)[:pairs]
        back = back.reshape(streams, heads, count, head_width, rows)
        return back.transpose(2, 1, 3, 0, 4)

    input_flat = block_input.astype(jnp.float32).reshape(tokens, width)
    normed = layer_norm(input_flat, norm1_gain).astype(low)
    normed_pair = jnp.concatenate([normed, ring.across(normed)], axis=0)

    def project(weight):
        return dot(weight, normed, 0, 1)

    def rope(value):
        value = value.reshape(heads, 2, half, streams, rows)
        return turn(value, cosine, sine, 1.0).reshape(heads, head_width, streams, rows)

    scale = 1.0 / math.sqrt(head_width)
    query = (rope(project(w_query)) * scale).astype(low)
    key = rope(project(w_key)).astype(low)
    value = project(w_value).astype(low).reshape(heads, head_width, streams, rows)
    packed = to_heads([query, key, value])
    attended_own, lse = attn_fwd(lo, packed, frames)
    attended = to_tokens(attended_own.astype(low), 1)[0].reshape(width, tokens)

    attended_other = ring.across(attended)
    middle = input_flat + dot(attended, w_out, 0, 0)
    normed_two = layer_norm(middle, norm2_gain).astype(low)
    two_plane = plane_tokens(normed_two)
    gelu = lambda inner: jax.nn.gelu(inner, approximate=True)

    def feed(rows_two, rows_cot, up_weight, down_weight):
        activated, gelu_back = jax.vjp(gelu, dot(rows_two, up_weight, 1, 0))
        d_hidden = gelu_back(dot(rows_cot, down_weight, 1, 1))[0].astype(low)
        return activated.astype(low), d_hidden

    activated_low, d_hidden = feed(normed_two, cot_flat, w_up, w_down)
    d_normed_two = dot(d_hidden, w_up, 1, 1)
    unused_two, norm_two_back = jax.vjp(layer_norm, middle, norm2_gain)
    d_middle_norm, grad_gain_two = norm_two_back(d_normed_two)
    d_middle = cot_flat.astype(jnp.float32) + d_middle_norm
    d_branch = d_middle.astype(low)
    d_attended = dot(w_out, d_branch, 1, 1).astype(low)
    d_own = to_heads([d_attended.reshape(heads, head_width, streams, rows)])
    block_output = (middle + dot(activated_low, w_down, 1, 0)).astype(low)

    part_active, part_hidden = feed(two_plane, cot_plane, up_part, down_part)
    grad_up = ring.plane_sum(dot(two_plane, part_hidden, 0, 0))
    grad_down = ring.plane_sum(dot(part_active, cot_plane, 0, 0))
    parts_of = spots * spaces + cores
    zeros = jnp.zeros_like(parts_of)
    (grad_up,) = place(
        *ring.plane_gather(grad_up), jnp.stack([zeros, parts_of]), w_up.shape, 1
    )
    (grad_down,) = place(
        *ring.plane_gather(grad_down), jnp.stack([parts_of, zeros]), w_down.shape, 1
    )
    quarters = jnp.stack([quarter_rows(spots, cores), cores])
    half_columns = width // spaces

    def my_half(value, axis, core):
        return lax.dynamic_slice_in_dim(value, core * half_columns, half_columns, axis)

    branch_other = ring.across(my_half(d_branch, 1, 1 - ring.core))
    grad_out = dot(attended, my_half(d_branch, 1, ring.core), 1, 0) + dot(
        attended_other, branch_other, 1, 0
    )
    grad_out = ring.plane_sum(ring.half_sums(grad_out))
    (grad_out,) = place(*ring.plane_gather(grad_out), quarters, w_out.shape, 1)

    grads_own = attn_bwd(hi, packed, d_own, attended_own, lse, frames)
    d_three = to_tokens(grads_own, 3)

    def rope_back(value):
        value = value.astype(jnp.float32).reshape(heads, 2, half, streams, rows)
        return turn(value, cosine, sine, -1.0).reshape(width, tokens)

    d_query = (rope_back(d_three[0]) * scale).astype(low)
    d_key = rope_back(d_three[1]).astype(low)
    d_value = d_three[2].reshape(width, tokens)
    d_three = jnp.stack([d_query, d_key, d_value])
    three_other = ring.across(my_half(d_three, 1, 1 - ring.core))
    three_pair = jnp.concatenate([my_half(d_three, 1, ring.core), three_other], axis=2)
    grad_three = dot(normed_pair, three_pair.reshape(3 * half_columns, spaces * tokens), 0, 1)
    grad_three = ring.plane_sum(ring.half_sums(grad_three))
    grad_query, grad_key, grad_value = place(
        *ring.plane_gather(grad_three), quarters, w_query.shape, 3
    )
    d_normed = (
        dot(d_query, w_query, 0, 1) + dot(d_key, w_key, 0, 1) + dot(d_value, w_value, 0, 1)
    )
    unused_one, norm_one_back = jax.vjp(layer_norm, input_flat, norm1_gain)
    d_input_norm, grad_gain_one = norm_one_back(d_normed)
    grad_input = (d_middle + d_input_norm).reshape(streams, rows, width)
    gain_sum = lambda value: jnp.sum(lax.all_gather(value, axes), axis=0)
    return (
        block_output.reshape(streams, rows, width),
        grad_input,
        gain_sum(grad_gain_one),
        grad_query,
        grad_key,
        grad_value,
        grad_out,
        gain_sum(grad_gain_two),
        grad_up,
        grad_down,
    )


def solution(mesh):
    spread = P(None, ("frame", "space"), None)
    in_specs = (spread,) + (P(),) * 9 + (spread,)
    out_specs = (spread, spread) + (P(),) * 8
    return jax.shard_map(local, mesh=mesh, in_specs=in_specs, out_specs=out_specs, check_vma=False)
```

```python
import math

import jax
import jax.numpy as jnp
import numpy as np
from jax import lax
from jax.experimental import pallas as pl
from jax.experimental.pallas import tpu as pltpu
from jax.sharding import PartitionSpec as P

HEADS = 12
HEAD_DIM = 64
VMEM = pl.BlockSpec(memory_space=pltpu.VMEM)
SMEM = pl.BlockSpec(memory_space=pltpu.SMEM)
LIMIT = pltpu.CompilerParams(vmem_limit_bytes=56 * 2**20)


def dot(left, right, left_dim, right_dim):
    return lax.dot_general(
        left,
        right,
        (((left_dim,), (right_dim,)), ((), ())),
        preferred_element_type=jnp.float32,
    )


def normalize(values):
    average = jnp.mean(values, axis=-1, keepdims=True)
    centred = values - average
    root = lax.rsqrt(jnp.mean(centred * centred, axis=-1, keepdims=True) + 1e-05)
    return centred * root, root


def normalize_back(d_scaled, unit, root, gain):
    d_unit = d_scaled * gain
    mean_one = jnp.mean(d_unit, axis=-1, keepdims=True)
    mean_two = jnp.mean(d_unit * unit, axis=-1, keepdims=True)
    return root * (d_unit - mean_one - unit * mean_two), jnp.sum(
        d_scaled * unit, axis=0, keepdims=True
    )


def angles_of(frame, first_row, clips_ref, stream, rows, per_frame, frequency):
    begin = jnp.int32(0)
    running = jnp.int32(0)
    for clip in range(clips_ref.shape[1]):
        length = clips_ref[stream, clip]
        begin = jnp.where((frame >= running) & (frame < running + length), running, begin)
        running = running + length
    row = lax.broadcasted_iota(jnp.int32, (HEAD_DIM // 2, rows), 1)
    position = ((frame - begin) * per_frame + first_row + row).astype(jnp.float32)
    return position * frequency


def turned(value, cosine, sine, sign):
    half = HEAD_DIM // 2
    first, second = value[:half], value[half:]
    return jnp.concatenate(
        [first * cosine - sign * second * sine, second * cosine + sign * first * sine], axis=0
    )


def project(place, clips, block_input, gain, w_query, w_key, w_value, devices, per_frame):
    streams, rows, width = block_input.shape
    half = HEAD_DIM // 2
    low = jnp.bfloat16
    scale = 1.0 / math.sqrt(HEAD_DIM)

    def body(place_ref, clips_ref, freq_ref, x_ref, gain_ref, wq, wk, wv, out, normed_out, table):
        frame, first_row = place_ref[0], place_ref[1]
        frequency = freq_ref[...]
        for stream in range(streams):
            angles = angles_of(frame, first_row, clips_ref, stream, rows, per_frame, frequency)
            table[0, stream] = jnp.cos(angles)
            table[1, stream] = jnp.sin(angles)
        values = x_ref[...].astype(jnp.float32).reshape(streams * rows, width)
        unit, _ = normalize(values)
        normed = (unit * gain_ref[...]).astype(low)
        normed_out[...] = normed
        for kind, weight in enumerate((wq, wk, wv)):
            product = dot(normed, weight[...], 1, 0).T
            for stream in range(streams):
                columns = slice(stream * rows, (stream + 1) * rows)
                for head in range(HEADS):
                    piece = product[head * HEAD_DIM : (head + 1) * HEAD_DIM, columns]
                    if kind < 2:
                        piece = turned(piece, table[0, stream], table[1, stream], 1.0)
                    if kind == 0:
                        piece = piece * scale
                    out[
                        stream * HEADS + head, kind * HEAD_DIM : (kind + 1) * HEAD_DIM, :
                    ] = piece.astype(low)
        for spare in range(streams * HEADS, devices):
            out[spare] = jnp.zeros((3 * HEAD_DIM, rows), low)

    frequency = np.exp(np.arange(half) * (-2.0 * math.log(10000.0) / HEAD_DIM))
    frequency = jnp.asarray(np.broadcast_to(frequency[:, None], (half, rows)), jnp.float32)
    return pl.pallas_call(
        body,
        out_shape=(
            jax.ShapeDtypeStruct((devices, 3 * HEAD_DIM, rows), low),
            jax.ShapeDtypeStruct((streams * rows, width), low),
            jax.ShapeDtypeStruct((2, streams, half, rows), jnp.float32),
        ),
        in_specs=[SMEM, SMEM] + [VMEM] * 6,
        out_specs=(VMEM, VMEM, VMEM),
        compiler_params=LIMIT,
        name="project",
    )(place, clips, frequency, block_input, gain[None, :], w_query, w_key, w_value)


GELU = math.sqrt(2.0 / math.pi)


def gelu_pair(value):
    square = value * value
    bent = jnp.tanh(GELU * value * (1.0 + 0.044715 * square))
    side = 0.5 * (1.0 + bent)
    slope = side + 0.5 * value * (1.0 - bent * bent) * (GELU * (1.0 + 3 * 0.044715 * square))
    return value * side, slope


def attention_out(attended, block_input, w_out, gain):
    _, _, rows = attended.shape
    streams, _, width = block_input.shape
    low = jnp.bfloat16

    def body(att, x_ref, wo, gain_ref, middle, two_ref):
        for stream in range(streams):
            rows_of = slice(stream * rows, (stream + 1) * rows)
            flat = att[stream * HEADS : (stream + 1) * HEADS].reshape(width, rows)
            values = x_ref[stream].astype(jnp.float32) + dot(flat.T, wo[...], 1, 0)
            middle[rows_of] = values
            two_ref[rows_of] = (normalize(values)[0] * gain_ref[...]).astype(low)

    return pl.pallas_call(
        body,
        out_shape=(
            jax.ShapeDtypeStruct((streams * rows, width), jnp.float32),
            jax.ShapeDtypeStruct((streams * rows, width), low),
        ),
        in_specs=[VMEM] * 4,
        out_specs=(VMEM, VMEM),
        compiler_params=LIMIT,
        name="attention_out",
    )(attended, block_input, w_out, gain[None, :])


def feed_forward(core, attended, middle, two, cotangent, w_out, gain, w_up, w_down, chunk):
    devices, head_width, rows = attended.shape
    streams, _, width = cotangent.shape
    tokens = streams * rows
    pairs = streams * HEADS
    half = width // 2
    steps = w_up.shape[1] // chunk
    low = jnp.bfloat16
    f32 = jnp.float32

    def body(
        core_ref, att, middle, two_ref, cot, wo, gain_ref, up, down,
        result_ref, d_middle_ref, d_own, gain_out, keep, give,
        result, d_two,
    ):
        step = pl.program_id(0)
        cot_flat = cot[...].reshape(tokens, width)
        active, slope = gelu_pair(dot(two_ref[...], up[...], 1, 0))
        d_hidden = (dot(cot_flat, down[...], 1, 1) * slope).astype(low)
        forward = dot(active.astype(low), down[...], 1, 0)
        backward = dot(d_hidden, up[...], 1, 1)

        @pl.when(step == 0)
        def _():
            result[...] = forward
            d_two[...] = backward

        @pl.when(step > 0)
        def _():
            result[...] += forward
            d_two[...] += backward

        @pl.when(step == steps - 1)
        def _():
            result_ref[...] = (middle[...] + result[...]).astype(low).reshape(streams, rows, width)
            unit, root = normalize(middle[...])
            d_values, gain_terms = normalize_back(d_two[...], unit, root, gain_ref[...])
            gain_out[...] = gain_terms
            d_middle = cot_flat.astype(f32) + d_values
            d_middle_ref[...] = d_middle
            branch = d_middle.astype(low)
            d_att = dot(branch, wo[...], 1, 1).T.astype(low)
            total = jnp.zeros((width, width), f32)
            for stream in range(streams):
                rows_of = slice(stream * rows, (stream + 1) * rows)
                for head in range(HEADS):
                    d_own[stream * HEADS + head] = d_att[
                        head * HEAD_DIM : (head + 1) * HEAD_DIM, rows_of
                    ]
                flat = att[stream * HEADS : (stream + 1) * HEADS].reshape(width, rows)
                total += dot(flat, branch[rows_of], 1, 0)
            for spare in range(pairs, devices):
                d_own[spare] = jnp.zeros((head_width, rows), low)
            first = core_ref[0] == 0
            keep[...] = jnp.where(first, total[:, :half], total[:, half:])
            give[...] = jnp.where(first, total[:, half:], total[:, :half]).astype(low)

    whole = lambda shape: pl.BlockSpec(shape, lambda i: (0,) * len(shape))
    shapes = (
        ((streams, rows, width), low),
        ((tokens, width), f32),
        ((devices, head_width, rows), low),
        ((1, width), f32),
        ((width, half), f32),
        ((width, half), low),
    )
    return pl.pallas_call(
        body,
        grid=(steps,),
        out_shape=tuple(jax.ShapeDtypeStruct(*entry) for entry in shapes),
        in_specs=[
            SMEM, whole(attended.shape), whole(middle.shape), whole(two.shape),
            whole(cotangent.shape), whole(w_out.shape), whole((1, width)),
            pl.BlockSpec((width, chunk), lambda i: (0, i)),
            pl.BlockSpec((chunk, width), lambda i: (i, 0)),
        ],
        out_specs=tuple(whole(shape) for shape, _ in shapes),
        scratch_shapes=[pltpu.VMEM((tokens, width), f32), pltpu.VMEM((tokens, width), f32)],
        compiler_params=LIMIT,
        name="feed_forward",
    )(core, attended, middle, two, cotangent, w_out, gain[None, :], w_up, w_down)


def hidden_gradients(where, two_mine, two_other, cot_mine, cot_other, w_up, w_down, slots, planes):
    pieces, tokens, width = two_mine.shape
    hidden = w_up.shape[1] // slots
    rows = width // planes
    low = jnp.bfloat16

    def body(where_ref, two_a, two_b, cot_a, cot_b, up, down, *rest):
        outs, (up_sum, down_sum) = rest[:planes], rest[planes:]
        step = pl.program_id(0)

        def run(two, cot):
            active, slope = gelu_pair(dot(two, up[...], 1, 0))
            d_hidden = (dot(cot, down[...], 1, 1) * slope).astype(low)
            up_term = dot(two, d_hidden, 0, 0)
            down_term = dot(active.astype(low), cot, 0, 0)

            @pl.when(step == 0)
            def _():
                up_sum[...] = up_term
                down_sum[:hidden] = down_term[:, :hidden]
                down_sum[hidden:] = down_term[:, hidden:]

            @pl.when(step > 0)
            def _():
                up_sum[...] += up_term
                down_sum[:hidden] += down_term[:, :hidden]
                down_sum[hidden:] += down_term[:, hidden:]

        @pl.when(step < pieces // 2)
        def _():
            run(two_a[...].reshape(2 * tokens, width), cot_a[...].reshape(2 * tokens, width))

        @pl.when(step >= pieces // 2)
        def _():
            run(two_b[...].reshape(2 * tokens, width), cot_b[...].reshape(2 * tokens, width))

        @pl.when(step == pieces - 1)
        def _():
            for index, out in enumerate(outs):
                plane = lax.rem(where_ref[1] + index, planes)
                rows_of = pl.ds(pl.multiple_of(plane * rows, rows), rows)
                out[0] = up_sum[rows_of, :].astype(low)
                out[1] = down_sum[rows_of, :].astype(low)

    near = pl.BlockSpec(
        (2, tokens, width), lambda i, where: (jnp.minimum(i, pieces // 2 - 1), 0, 0)
    )
    far = pl.BlockSpec((2, tokens, width), lambda i, where: (jnp.maximum(i - pieces // 2, 0), 0, 0))
    return pl.pallas_call(
        body,
        grid_spec=pltpu.PrefetchScalarGridSpec(
            num_scalar_prefetch=1,
            grid=(pieces,),
            in_specs=[
                near, far, near, far,
                pl.BlockSpec((width, hidden), lambda i, where: (0, where[0])),
                pl.BlockSpec((hidden, width), lambda i, where: (where[0], 0)),
            ],
            out_specs=[pl.BlockSpec((2, rows, hidden), lambda i, where: (0, 0, 0))] * planes,
            scratch_shapes=[pltpu.VMEM((width, hidden), jnp.float32)] * 2,
        ),
        out_shape=[jax.ShapeDtypeStruct((2, rows, hidden), low)] * planes,
        compiler_params=LIMIT,
        name="hidden_gradients",
    )(where, two_mine, two_other, cot_mine, cot_other, w_up, w_down)


def unrope(core, grads, table, spaces):
    devices, _, rows = grads.shape
    streams = table.shape[1]
    width = HEADS * HEAD_DIM
    half = width // spaces
    low = jnp.bfloat16
    scale = 1.0 / math.sqrt(HEAD_DIM)

    def body(core_ref, grads_ref, table_ref, full, give):
        core = core_ref[0]
        for stream in range(streams):
            rows_of = slice(stream * rows, (stream + 1) * rows)
            cosine, sine = table_ref[0, stream], table_ref[1, stream]
            for kind in range(3):
                pieces = []
                for head in range(HEADS):
                    piece = grads_ref[
                        stream * HEADS + head, kind * HEAD_DIM : (kind + 1) * HEAD_DIM, :
                    ].astype(jnp.float32)
                    if kind < 2:
                        piece = turned(piece, cosine, sine, -1.0)
                    if kind == 0:
                        piece = piece * scale
                    pieces.append(piece)
                flat = jnp.concatenate(pieces, axis=0).T.astype(low)
                full[kind, rows_of] = flat
                give[kind, rows_of] = jnp.where(core == 0, flat[:, half:], flat[:, :half])

    return pl.pallas_call(
        body,
        out_shape=(
            jax.ShapeDtypeStruct((3, streams * rows, width), low),
            jax.ShapeDtypeStruct((3, streams * rows, half), low),
        ),
        in_specs=[SMEM, VMEM, VMEM],
        out_specs=(VMEM, VMEM),
        compiler_params=LIMIT,
        name="unrope",
    )(core, grads, table)


def input_gradient(d_three, weights, block_input, gain, d_middle):
    _, tokens, width = d_three.shape

    def body(d_ref, wq, wk, wv, x_ref, gain_ref, d_middle_ref, out, gain_out):
        d_normed = dot(d_ref[0], wq[...], 1, 1)
        d_normed += dot(d_ref[1], wk[...], 1, 1)
        d_normed += dot(d_ref[2], wv[...], 1, 1)
        unit, root = normalize(x_ref[...].astype(jnp.float32).reshape(tokens, width))
        d_values, gain_terms = normalize_back(d_normed, unit, root, gain_ref[...])
        out[...] = (d_middle_ref[...] + d_values).reshape(out.shape)
        gain_out[...] = gain_terms

    return pl.pallas_call(
        body,
        out_shape=(
            jax.ShapeDtypeStruct(block_input.shape, jnp.float32),
            jax.ShapeDtypeStruct((1, width), jnp.float32),
        ),
        in_specs=[VMEM] * 7,
        out_specs=(VMEM, VMEM),
        compiler_params=LIMIT,
        name="input_gradient",
    )(d_three, *weights, block_input, gain[None, :], d_middle)


def projection_gradients(where, normed, normed_other, d_three, d_other):
    tokens, width = normed.shape
    half = d_other.shape[2]
    low = jnp.bfloat16

    def body(where_ref, a_ref, b_ref, d_ref, o_ref, keep, give):
        core, bit = where_ref[0], where_ref[1]
        left = jnp.concatenate([a_ref[...], b_ref[...]], axis=0)
        for kind in range(3):
            flat = d_ref[kind]
            mine = jnp.where(core == 0, flat[:, :half], flat[:, half:])
            right = jnp.concatenate([mine, o_ref[kind]], axis=0)
            total = dot(left, right, 0, 0)
            columns = slice(kind * half, (kind + 1) * half)
            top, bottom = total[: width // 2], total[width // 2 :]
            keep[:, columns] = jnp.where(bit == 0, top, bottom)
            give[:, columns] = jnp.where(bit == 0, bottom, top).astype(low)

    return pl.pallas_call(
        body,
        out_shape=(
            jax.ShapeDtypeStruct((width // 2, 3 * half), jnp.float32),
            jax.ShapeDtypeStruct((width // 2, 3 * half), low),
        ),
        in_specs=[SMEM] + [VMEM] * 4,
        out_specs=(VMEM, VMEM),
        compiler_params=LIMIT,
        name="projection_gradients",
    )(where, normed, normed_other, d_three, d_other)


CLIP = 4


def wide(ref, frame, spaces, first, last, count=1):
    return jnp.concatenate(
        [ref[frame * spaces + j, first:last, :] for j in range(spaces * count)], axis=1
    )


def attend(lo, packed, frames):
    devices, _, rows = packed.shape
    spaces = devices // frames
    per_frame = rows * spaces
    dim = HEAD_DIM

    def body(lo_ref, r_ref, o_ref, low_ref, lse_ref, kv, top, total, summed):
        def turn_keys(device, _):
            kv[pl.ds(pl.multiple_of(device * rows, rows), rows), :] = r_ref[device, dim:, :].T
            return 0

        lax.fori_loop(0, devices, turn_keys, 0, unroll=4)

        def group(queries, _):
            first = queries * CLIP
            query = [wide(r_ref, first + i, spaces, 0, dim) for i in range(CLIP)]

            def update(i, keys, count, fresh):
                base = pl.multiple_of(keys * CLIP * per_frame, per_frame)
                scores = dot(kv[pl.ds(base, count * per_frame), :dim], query[i], 1, 0)
                new_top = jnp.max(scores, axis=0, keepdims=True)
                if not fresh:
                    old_top = top[i]
                    new_top = jnp.maximum(old_top, new_top)
                weights = jnp.exp(scores - new_top)
                new_total = jnp.sum(weights, axis=0, keepdims=True)
                values = wide(r_ref, keys * CLIP, spaces, 2 * dim, 3 * dim, count)
                new_sum = dot(values, weights.astype(jnp.bfloat16), 1, 0)
                if not fresh:
                    factor = jnp.exp(old_top - new_top)
                    new_total += total[i] * factor
                    new_sum += summed[i] * factor
                top[i] = new_top
                total[i] = new_total
                summed[i] = new_sum

            for i in range(CLIP):
                update(i, queries, i + 1, True)

            def earlier(keys, _):
                for i in range(CLIP):
                    update(i, keys, CLIP, False)
                return 0

            lax.fori_loop(lo_ref[first] // CLIP, queries, earlier, 0)
            for i in range(CLIP):
                out = summed[i] / total[i]
                for j in range(spaces):
                    piece = out[:, j * rows : (j + 1) * rows]
                    o_ref[(first + i) * spaces + j] = piece
                    low_ref[(first + i) * spaces + j] = piece.astype(jnp.bfloat16)
                lse_ref[first + i] = top[i] + jnp.log(total[i])
            return 0

        lax.fori_loop(0, frames // CLIP, group, 0)

    f32 = jnp.float32
    return pl.pallas_call(
        body,
        out_shape=(
            jax.ShapeDtypeStruct((devices, dim, rows), f32),
            jax.ShapeDtypeStruct((devices, dim, rows), jnp.bfloat16),
            jax.ShapeDtypeStruct((frames, 1, per_frame), f32),
            jax.ShapeDtypeStruct((devices * rows, 2 * dim), jnp.bfloat16),
        ),
        in_specs=[SMEM, VMEM],
        out_specs=(VMEM,) * 4,
        scratch_shapes=[
            pltpu.VMEM((CLIP, 1, per_frame), f32),
            pltpu.VMEM((CLIP, 1, per_frame), f32),
            pltpu.VMEM((CLIP, dim, per_frame), f32),
        ],
        compiler_params=LIMIT,
        name="attend",
    )(lo, packed)


def attend_back_ready(packed, d_own, out, frames):
    devices, _, rows = packed.shape
    spaces = devices // frames
    dim = HEAD_DIM

    def body(r_ref, d_ref, o_ref, qd, delta):
        def turn_frame(frame, _):
            for j in range(spaces):
                device = frame * spaces + j
                both = jnp.concatenate([r_ref[device, :dim, :], d_ref[device]], axis=0)
                qd[pl.ds(pl.multiple_of(device * rows, rows), rows), :] = both.T
                delta[frame, :, j * rows : (j + 1) * rows] = jnp.sum(
                    d_ref[device].astype(jnp.float32) * o_ref[device], axis=0, keepdims=True
                )
            return 0

        lax.fori_loop(0, frames, turn_frame, 0, unroll=2)

    return pl.pallas_call(
        body,
        out_shape=(
            jax.ShapeDtypeStruct((devices * rows, 2 * dim), jnp.bfloat16),
            jax.ShapeDtypeStruct((frames, 1, spaces * rows), jnp.float32),
        ),
        in_specs=[VMEM] * 3,
        out_specs=(VMEM, VMEM),
        compiler_params=LIMIT,
        name="attend_back_ready",
    )(packed, d_own, out)


def attend_back(hi, packed, d_own, lse, delta, kv, qd, d_query, earlier, frames, start, stop):
    devices, _, rows = packed.shape
    spaces = devices // frames
    per_frame = rows * spaces
    dim = HEAD_DIM
    last = stop * CLIP == frames
    f32 = jnp.float32
    shift = dim if last else 0
    base = 0 if last else start * CLIP * spaces

    def body(hi_ref, r_ref, d_ref, lse_ref, delta_ref, kv_ref, qd_ref, *rest):
        rest = list(rest)
        before = rest.pop(0) if start else None
        pieces = [rest.pop(0) for _ in earlier] if last else []
        out = rest.pop(0)
        d_query_ref, acc, left = rest

        def begin(frame, _):
            d_query_ref[frame] = before[frame] if start else jnp.zeros((dim, per_frame), f32)
            return 0

        lax.fori_loop(0, frames, begin, 0)
        done = 0
        for piece in pieces:
            out[done : done + piece.shape[0], dim:, :] = piece[...]
            done += piece.shape[0]
        first_half = lax.broadcasted_iota(jnp.int32, (per_frame, 2 * dim), 1) < dim

        def group(keys, _):
            first = keys * CLIP
            for i in range(CLIP):
                rows_of = pl.ds(pl.multiple_of((first + i) * per_frame, per_frame), per_frame)
                both = kv_ref[rows_of, :]
                zero = jnp.zeros_like(both)
                left[i, :per_frame] = jnp.where(first_half, both, zero)
                left[i, per_frame:] = jnp.where(first_half, zero, both)

            def block(i, frame, count, fresh):
                own = [d_ref[frame * spaces + j] for j in range(spaces * count)]
                right = jnp.concatenate(
                    [wide(r_ref, frame, spaces, 0, dim, count), jnp.concatenate(own, axis=1)],
                    axis=0,
                )
                both = dot(left[i], right, 1, 0)
                row = lambda ref: jnp.concatenate([ref[frame + j] for j in range(count)], axis=1)
                weights = jnp.exp(both[:per_frame] - row(lse_ref))
                d_scores = (weights * (both[per_frame:] - row(delta_ref))).astype(jnp.bfloat16)
                pair = jnp.concatenate([weights.astype(jnp.bfloat16), d_scores], axis=0)
                tokens = pl.ds(pl.multiple_of(frame * per_frame, per_frame), count * per_frame)
                term = dot(pair, qd_ref[tokens, :], 1, 0)
                if fresh:
                    acc[i] = term
                else:
                    acc[i] += term
                key_rows = wide(r_ref, first + i, spaces, dim, 2 * dim)
                change = dot(key_rows, d_scores, 1, 0)
                for j in range(count):
                    d_query_ref[frame + j] += change[:, j * per_frame : (j + 1) * per_frame]

            for i in range(CLIP):
                block(i, first + i, CLIP - i, True)

            def later(queries, _):
                for i in range(CLIP):
                    block(i, queries * CLIP, CLIP, False)
                return 0

            lax.fori_loop(keys + 1, hi_ref[first] // CLIP, later, 0)
            for i in range(CLIP):
                total = acc[i]
                d_key = total[per_frame:].T[:dim].astype(jnp.bfloat16)
                d_value = total[:per_frame].T[dim:].astype(jnp.bfloat16)
                for j in range(spaces):
                    device = (first + i) * spaces + j - base
                    columns = slice(j * rows, (j + 1) * rows)
                    out[device, shift : shift + dim, :] = d_key[:, columns]
                    out[device, shift + dim : shift + 2 * dim, :] = d_value[:, columns]
            return 0

        lax.fori_loop(start, stop, group, 0)
        if last:

            def finish(frame, _):
                whole = d_query_ref[frame].astype(jnp.bfloat16)
                for j in range(spaces):
                    out[frame * spaces + j, :dim, :] = whole[:, j * rows : (j + 1) * rows]
                return 0

            lax.fori_loop(0, frames, finish, 0)

    if last:
        out_shape = (devices, 3 * dim, rows)
    else:
        out_shape = ((stop - start) * CLIP * spaces, 2 * dim, rows)
    inputs = [hi, packed, d_own, lse, delta, kv, qd]
    inputs += [d_query] if start else []
    inputs += list(earlier) if last else []
    return pl.pallas_call(
        body,
        out_shape=(
            jax.ShapeDtypeStruct(out_shape, jnp.bfloat16),
            jax.ShapeDtypeStruct((frames, dim, per_frame), f32),
        ),
        in_specs=[SMEM] + [VMEM] * (len(inputs) - 1),
        out_specs=(VMEM, VMEM),
        scratch_shapes=[
            pltpu.VMEM((CLIP, 2 * per_frame, 2 * dim), f32),
            pltpu.VMEM((CLIP, 2 * per_frame, 2 * dim), jnp.bfloat16),
        ],
        compiler_params=LIMIT,
        name="attend_back",
    )(*inputs)


def after(value, *others):
    return lax.optimization_barrier((value, *others))[0]


class Ring:
    def __init__(self):
        self.frames = lax.axis_size("frame")
        self.spaces = lax.axis_size("space")
        self.planes = self.frames // 4
        self.frame = lax.axis_index("frame")
        self.core = lax.axis_index("space")
        self.plane = self.frame // 4
        self.spot = self.frame % 4
        bits = (self.frame % 2, (self.frame // 2) % 2)
        self.first_bit = jnp.where(self.core == 0, bits[0], bits[1])
        self.second_bit = jnp.where(self.core == 0, bits[1], bits[0])

    def send(self, value, target):
        moves = []
        for frame in range(self.frames):
            for core in range(self.spaces):
                to_frame, to_core = target(frame, core)
                moves.append((frame * self.spaces + core, to_frame * self.spaces + to_core))
        return lax.ppermute(value, ("frame", "space"), moves)

    def first(self, value):
        return self.send(value, lambda frame, core: (frame ^ (1 if core == 0 else 2), core))

    def second(self, value):
        return self.send(value, lambda frame, core: (frame ^ (2 if core == 0 else 1), core))

    def across(self, value):
        return self.send(value, lambda frame, core: (frame, 1 - core))

    def up(self, value, step):
        size = self.frames
        return self.send(value, lambda frame, core: ((frame + 4 * step) % size, core))

    def spread_planes(self, pieces):
        total = pieces[0].astype(jnp.float32)
        for step, piece in enumerate(pieces[1:], 1):
            total = total + self.up(piece, step).astype(jnp.float32)
        total = total.astype(jnp.bfloat16)
        return jnp.stack([total] + [self.up(total, step) for step in range(1, len(pieces))])

    def gather_spots(self):
        near = jnp.where(self.core == 0, 2, 1)
        own = jnp.stack([self.spot, self.spot ^ near, self.spot ^ (3 - near), self.spot ^ 3])
        other = jnp.stack([self.spot, self.spot ^ (3 - near), self.spot ^ near, self.spot ^ 3])
        cores = jnp.repeat(jnp.stack([self.core, 1 - self.core]), 4)
        return jnp.concatenate([own, other]), cores

    def gather(self, value):
        pair = jnp.stack([value, self.second(value)])
        return jnp.concatenate([pair, self.first(pair)], axis=0)

    def halve(self, value, bit, exchange):
        rows, columns = value.shape
        cut = value.reshape(2, rows // 2, columns)
        keep = lax.dynamic_index_in_dim(cut, bit, 0, keepdims=False)
        give = lax.dynamic_index_in_dim(cut, 1 - bit, 0, keepdims=False)
        return keep + exchange(give.astype(jnp.bfloat16)).astype(jnp.float32)

    def plane_sum(self, value):
        rows, columns = value.shape
        size = rows // self.planes
        if size % 16:
            groups = [list(range(spot, self.frames, 4)) for spot in range(4)]
            low = value.astype(jnp.bfloat16)
            return lax.psum(low, "frame", axis_index_groups=groups)[None]
        cut = value.reshape(self.planes, size, columns).astype(jnp.bfloat16)
        pick = lambda index: lax.dynamic_index_in_dim(cut, index % self.planes, 0, keepdims=False)
        return self.spread_planes([pick(self.plane + step) for step in range(self.planes)])

    def total(self, value):
        step = 1
        while step < self.frames:
            value = value + self.send(value, lambda frame, core, s=step: (frame ^ s, core))
            step *= 2
        return value + self.across(value)


def quarter_rows(spots, cores):
    return jnp.where(cores == 1, spots, (spots % 2) * 2 + spots // 2)


def place(mine, other, blocks, out_shapes, cuts):
    spots, parts = mine.shape[:2]
    inner = mine.shape[2:]
    half_steps = spots * parts
    count = len(out_shapes)

    def body(where, mine_ref, other_ref, *outs):
        step = pl.program_id(0)

        @pl.when(step < half_steps)
        def _():
            for out, piece in zip(outs, cuts(mine_ref[0])):
                out[...] = piece.astype(jnp.float32)

        @pl.when(step >= half_steps)
        def _():
            for out, piece in zip(outs, cuts(other_ref[0])):
                out[...] = piece.astype(jnp.float32)

    zeros = (0,) * len(inner)
    sizes = [piece.shape for piece in jax.eval_shape(cuts, jax.ShapeDtypeStruct(inner, mine.dtype))]

    def out_spec(index):
        return pl.BlockSpec(sizes[index], lambda i, where: (where[index, 0, i], where[index, 1, i]))

    return pl.pallas_call(
        body,
        grid_spec=pltpu.PrefetchScalarGridSpec(
            num_scalar_prefetch=1,
            grid=(2 * half_steps,),
            in_specs=[
                pl.BlockSpec(
                    (1,) + inner, lambda i, where: (jnp.minimum(i, half_steps - 1),) + zeros
                ),
                pl.BlockSpec((1,) + inner, lambda i, where: (jnp.maximum(i - half_steps, 0),) + zeros),
            ],
            out_specs=[out_spec(index) for index in range(count)],
        ),
        out_shape=[jax.ShapeDtypeStruct(shape, jnp.float32) for shape in out_shapes],
        compiler_params=LIMIT,
        name="place",
    )(blocks, mine.reshape((half_steps,) + inner), other.reshape((half_steps,) + inner))


def frame_limits(clip_frames, frames):
    ends = jnp.cumsum(clip_frames, axis=1, dtype=jnp.int32)
    begins = ends - clip_frames
    index = jnp.arange(frames, dtype=jnp.int32)[None, :, None]
    inside = (index >= begins[:, None, :]) & (index < ends[:, None, :])
    pick = lambda table: jnp.sum(jnp.where(inside, table[:, None, :], 0), axis=2, dtype=jnp.int32)
    return pick(begins), pick(ends)


def local(
    block_input,
    norm1_gain,
    w_query,
    w_key,
    w_value,
    w_out,
    norm2_gain,
    w_up,
    w_down,
    clip_frames,
    cotangent,
):
    streams, rows, width = block_input.shape
    ring = Ring()
    frames, spaces, planes = ring.frames, ring.spaces, ring.planes
    devices = frames * spaces
    per_frame = rows * spaces
    tokens = streams * rows
    axes = ("frame", "space")
    low = jnp.bfloat16
    core = jnp.reshape(ring.core, (1,))
    spots, cores = ring.gather_spots()
    slots = 4 * spaces

    begin, end = frame_limits(clip_frames, frames)
    frame_ids = jnp.arange(frames, dtype=jnp.int32)
    mine = ring.frame * spaces + ring.core
    idle = mine >= streams * HEADS
    picked = jnp.arange(streams, dtype=jnp.int32)[:, None] == mine // HEADS
    lo = jnp.where(idle, frame_ids, jnp.sum(jnp.where(picked, begin, 0), axis=0))
    hi = jnp.where(idle, frame_ids, jnp.sum(jnp.where(picked, end, 0), axis=0))

    def swap(value):
        return lax.all_to_all(value, axes, 0, 0, tiled=True)

    spot_of = jnp.stack([ring.frame, ring.core * rows])
    sent, normed, table = project(
        spot_of, clip_frames, block_input, norm1_gain, w_query, w_key, w_value, devices, per_frame
    )
    packed = swap(sent)
    cot_flat = cotangent.reshape(tokens, width)
    cot_one = ring.second(after(cot_flat, packed))
    normed_other = ring.across(after(normed, packed))
    out, out_low, lse, kv = attend(lo, packed, frames)
    attended = swap(out_low)
    cot_pair = after(jnp.stack([cot_flat, cot_one]), out_low)
    cot_mine = jnp.concatenate([cot_pair, ring.first(cot_pair)], axis=0)

    middle, two = attention_out(attended, block_input, w_out, norm2_gain)
    cot_other = ring.across(after(cot_mine, middle))
    two_mine = ring.gather(two)
    two_other = ring.across(two_mine)
    block_output, d_middle, d_sent, gain_two, out_keep, out_give = feed_forward(
        core, attended, middle, two, cotangent, w_out, norm2_gain, w_up, w_down, 512
    )
    d_own = swap(d_sent)
    out_other = ring.across(out_give)
    pieces = hidden_gradients(
        jnp.stack([ring.spot * spaces + ring.core, ring.plane]),
        two_mine, two_other, cot_mine, cot_other, w_up, w_down, slots, planes,
    )

    qd, delta = attend_back_ready(packed, after(d_own, pieces[0]), out, frames)
    groups = frames // CLIP
    cuts = [0, groups // 4, groups // 2, groups]
    d_query, earlier = None, []
    for start, stop in zip(cuts[:-1], cuts[1:]):
        result, d_query = attend_back(
            hi, packed, d_own, lse, delta, kv, qd, d_query, earlier, frames, start, stop
        )
        earlier.append(result)
    back = swap(result)
    hidden_sum = ring.spread_planes(pieces)
    hidden_mine = ring.gather(hidden_sum)
    hidden_other = ring.across(hidden_mine)
    out_sum = out_keep + out_other.astype(jnp.float32)
    out_sum = ring.halve(out_sum, ring.first_bit, ring.first)
    out_sum = ring.plane_sum(ring.halve(out_sum, ring.second_bit, ring.second))
    out_mine = ring.gather(out_sum)
    out_other_sum = ring.across(out_mine)

    def order(parts):
        steps = jnp.arange(parts, dtype=jnp.int32)
        return (ring.plane - steps) % parts

    def blocks(parts, where):
        part = jnp.tile(order(parts), 2 * 4)
        spot = jnp.repeat(spots, parts)
        side = jnp.repeat(cores, parts)
        return jnp.stack([jnp.stack(pair) for pair in where(part, spot, side)]).astype(jnp.int32)

    def hidden_blocks(part, spot, side):
        unit = spot * spaces + side
        units = w_up.shape[1] // slots
        size = width // planes
        row = part * size
        return (
            (part, unit),
            ((unit * units + row % units) // size, row // units),
        )

    grad_up, grad_down = place(
        hidden_mine, hidden_other, blocks(planes, hidden_blocks), (w_up.shape, w_down.shape),
        lambda piece: (piece[0], piece[1]),
    )

    def square_blocks(count):
        def where(part, spot, side):
            parts = out_sum.shape[0]
            return ((quarter_rows(spot, side) * parts + part, side),) * count

        return blocks(out_sum.shape[0], where)

    (grad_out,) = place(
        out_mine, out_other_sum, square_blocks(1), (w_out.shape,), lambda piece: (piece,)
    )

    d_three, d_give = unrope(core, back, table, spaces)
    d_other = ring.across(d_give)
    keep, give = projection_gradients(
        jnp.stack([ring.core, ring.first_bit]), normed, normed_other, d_three, d_other
    )
    three = keep + ring.first(give).astype(jnp.float32)
    grad_input, gain_one = input_gradient(
        after(d_three, give), (w_query, w_key, w_value), block_input, norm1_gain, d_middle
    )
    three = ring.plane_sum(ring.halve(three, ring.second_bit, ring.second))
    three_mine = ring.gather(three)
    three_other = ring.across(three_mine)
    half = width // spaces
    grad_query, grad_key, grad_value = place(
        three_mine, three_other, square_blocks(3), (w_query.shape,) * 3,
        lambda piece: tuple(piece[:, i * half : (i + 1) * half] for i in range(3)),
    )
    gains = ring.total(jnp.concatenate([gain_one, gain_two], axis=0))
    return (
        block_output,
        grad_input,
        gains[0],
        grad_query,
        grad_key,
        grad_value,
        grad_out,
        gains[1],
        grad_up,
        grad_down,
    )


def solution(mesh):
    spread = P(None, ("frame", "space"), None)
    in_specs = (spread,) + (P(),) * 9 + (spread,)
    out_specs = (spread, spread) + (P(),) * 8
    return jax.shard_map(local, mesh=mesh, in_specs=in_specs, out_specs=out_specs, check_vma=False)
```

```python
import math

import jax
import jax.numpy as jnp
import numpy as np
from jax import lax
from jax.experimental import pallas as pl
from jax.experimental.pallas import tpu as pltpu
from jax.sharding import PartitionSpec as P

HEADS = 12
HEAD_DIM = 64
VMEM = pl.BlockSpec(memory_space=pltpu.VMEM)
SMEM = pl.BlockSpec(memory_space=pltpu.SMEM)
LIMIT = pltpu.CompilerParams(vmem_limit_bytes=56 * 2**20)
CLIP = 4


def dot(left, right, left_dim, right_dim):
    return lax.dot_general(
        left,
        right,
        (((left_dim,), (right_dim,)), ((), ())),
        preferred_element_type=jnp.float32,
    )


def head_owners(frames, spaces):
    planes = frames // 4
    share = -(-HEADS // planes)
    return [
        [
            ((head // share) * 4 + (head % share) // spaces * 2 + stream) * spaces
            + (head % share) % spaces
            for head in range(HEADS)
        ]
        for stream in range(2)
    ]


def normalize(values):
    average = jnp.mean(values, axis=-1, keepdims=True)
    centred = values - average
    root = lax.rsqrt(jnp.mean(centred * centred, axis=-1, keepdims=True) + 1e-05)
    return centred * root, root


def normalize_back(d_scaled, unit, root, gain):
    d_unit = d_scaled * gain
    mean_one = jnp.mean(d_unit, axis=-1, keepdims=True)
    mean_two = jnp.mean(d_unit * unit, axis=-1, keepdims=True)
    return root * (d_unit - mean_one - unit * mean_two)


def frequencies(columns):
    half = HEAD_DIM // 2
    values = np.exp(np.arange(half) * (-2.0 * math.log(10000.0) / HEAD_DIM))
    return jnp.asarray(np.broadcast_to(values[:, None], (half, columns)), jnp.float32)


def turned(value, cosine, sine, sign):
    half = HEAD_DIM // 2
    first, second = value[:half], value[half:]
    return jnp.concatenate(
        [first * cosine - sign * second * sine, second * cosine + sign * first * sine], axis=0
    )


def project(place, clips, block_input, gain, w_query, w_key, w_value, owners, devices, per_frame):
    streams, rows, width = block_input.shape
    half = HEAD_DIM // 2
    low = jnp.bfloat16
    scale = 1.0 / math.sqrt(HEAD_DIM)
    owned = {device for row in owners for device in row}

    def body(place_ref, clips_ref, freq_ref, x_ref, gain_ref, wq, wk, wv, out, normed_out, table):
        frame, first_row = place_ref[0], place_ref[1]
        for stream in range(streams):
            begin = jnp.int32(0)
            running = jnp.int32(0)
            for clip in range(clips_ref.shape[1]):
                length = clips_ref[stream, clip]
                begin = jnp.where((frame >= running) & (frame < running + length), running, begin)
                running = running + length
            row = lax.broadcasted_iota(jnp.int32, (half, rows), 1)
            position = ((frame - begin) * per_frame + first_row + row).astype(jnp.float32)
            angles = position * freq_ref[...]
            table[0, stream] = jnp.cos(angles)
            table[1, stream] = jnp.sin(angles)
        values = x_ref[...].astype(jnp.float32).reshape(streams * rows, width)
        normed = (normalize(values)[0] * gain_ref[...]).astype(low)
        normed_out[...] = normed.reshape(streams, rows, width)
        for kind, weight in enumerate((wq, wk, wv)):
            product = dot(normed, weight[...], 1, 0).T
            for stream in range(streams):
                columns = slice(stream * rows, (stream + 1) * rows)
                for head in range(HEADS):
                    piece = product[head * HEAD_DIM : (head + 1) * HEAD_DIM, columns]
                    if kind < 2:
                        piece = turned(piece, table[0, stream], table[1, stream], 1.0)
                    if kind == 0:
                        piece = piece * scale
                    out[
                        owners[stream][head], kind * HEAD_DIM : (kind + 1) * HEAD_DIM, :
                    ] = piece.astype(low)
        for spare in range(devices):
            if spare not in owned:
                out[spare] = jnp.zeros((3 * HEAD_DIM, rows), low)

    return pl.pallas_call(
        body,
        out_shape=(
            jax.ShapeDtypeStruct((devices, 3 * HEAD_DIM, rows), low),
            jax.ShapeDtypeStruct((streams, rows, width), low),
        ),
        in_specs=[SMEM, SMEM] + [VMEM] * 6,
        out_specs=(VMEM, VMEM),
        scratch_shapes=[pltpu.VMEM((2, streams, half, rows), jnp.float32)],
        compiler_params=LIMIT,
        name="project",
    )(place, clips, frequencies(rows), block_input, gain[None, :], w_query, w_key, w_value)


def rope_tables(lo, frames, per_frame):
    half = HEAD_DIM // 2

    def body(lo_ref, freq_ref, out):
        def one(frame, _):
            row = lax.broadcasted_iota(jnp.int32, (half, per_frame), 1)
            position = ((frame - lo_ref[frame]) * per_frame + row).astype(jnp.float32)
            angles = position * freq_ref[...]
            out[frame, 0] = jnp.cos(angles)
            out[frame, 1] = jnp.sin(angles)
            return 0

        lax.fori_loop(0, frames, one, 0)

    return pl.pallas_call(
        body,
        out_shape=jax.ShapeDtypeStruct((frames, 2, half, per_frame), jnp.float32),
        in_specs=[SMEM, VMEM],
        out_specs=VMEM,
        compiler_params=LIMIT,
        name="rope_tables",
    )(lo, frequencies(per_frame))


GELU = math.sqrt(2.0 / math.pi)


def gelu_pair(value):
    square = value * value
    bent = jnp.tanh(GELU * value * (1.0 + 0.044715 * square))
    side = 0.5 * (1.0 + bent)
    slope = side + 0.5 * value * (1.0 - bent * bent) * (GELU * (1.0 + 3 * 0.044715 * square))
    return value * side, slope


def attention_out(attended, block_input, w_out, gain, owners):
    streams, rows, width = block_input.shape
    low = jnp.bfloat16

    def body(att, x_ref, wo, gain_ref, middle, two_ref):
        for stream in range(streams):
            rows_of = slice(stream * rows, (stream + 1) * rows)
            flat = jnp.concatenate([att[owner] for owner in owners[stream]], axis=0)
            values = x_ref[stream].astype(jnp.float32) + dot(flat.T, wo[...], 1, 0)
            middle[rows_of] = values
            two_ref[rows_of] = (normalize(values)[0] * gain_ref[...]).astype(low)

    return pl.pallas_call(
        body,
        out_shape=(
            jax.ShapeDtypeStruct((streams * rows, width), jnp.float32),
            jax.ShapeDtypeStruct((streams * rows, width), low),
        ),
        in_specs=[VMEM] * 4,
        out_specs=(VMEM, VMEM),
        compiler_params=LIMIT,
        name="attention_out",
    )(attended, block_input, w_out, gain[None, :])


def whole(shape):
    return pl.BlockSpec(shape, lambda *indices: (0,) * len(shape))


def feed_first(two, cotangent, w_up, w_down, chunk, steps):
    tokens, width = two.shape
    low = jnp.bfloat16

    def body(two_ref, cot, up, down, result, d_two):
        cot_flat = cot[...].reshape(tokens, width)
        active, slope = gelu_pair(dot(two_ref[...], up[...], 1, 0))
        d_hidden = (dot(cot_flat, down[...], 1, 1) * slope).astype(low)
        forward = dot(active.astype(low), down[...], 1, 0)
        backward = dot(d_hidden, up[...], 1, 1)

        @pl.when(pl.program_id(0) == 0)
        def _():
            result[...] = forward
            d_two[...] = backward

        @pl.when(pl.program_id(0) > 0)
        def _():
            result[...] += forward
            d_two[...] += backward

    return pl.pallas_call(
        body,
        grid=(steps,),
        out_shape=(jax.ShapeDtypeStruct((tokens, width), jnp.float32),) * 2,
        in_specs=[
            whole(two.shape), whole(cotangent.shape),
            pl.BlockSpec((width, chunk), lambda i: (0, i)),
            pl.BlockSpec((chunk, width), lambda i: (i, 0)),
        ],
        out_specs=(whole((tokens, width)),) * 2,
        compiler_params=LIMIT,
        name="feed_first",
    )(two, cotangent, w_up, w_down)


def feed_rest(core, so_far, attended, middle, two, cotangent, w_out, gain, w_up, w_down, chunk, skip, owners):
    devices, head_width, rows = attended.shape
    streams, _, width = cotangent.shape
    tokens = streams * rows
    half = width // 2
    steps = w_up.shape[1] // chunk - skip
    low = jnp.bfloat16
    f32 = jnp.float32
    owned = {device for row in owners for device in row}

    def body(
        core_ref, first_result, first_two, att, middle, two_ref, cot, wo, gain_ref, up, down,
        result_ref, d_middle_ref, d_own, keep, give,
        result, d_two,
    ):
        step = pl.program_id(0)
        cot_flat = cot[...].reshape(tokens, width)
        active, slope = gelu_pair(dot(two_ref[...], up[...], 1, 0))
        d_hidden = (dot(cot_flat, down[...], 1, 1) * slope).astype(low)
        forward = dot(active.astype(low), down[...], 1, 0)
        backward = dot(d_hidden, up[...], 1, 1)

        @pl.when(step == 0)
        def _():
            result[...] = first_result[...] + forward
            d_two[...] = first_two[...] + backward

        @pl.when(step > 0)
        def _():
            result[...] += forward
            d_two[...] += backward

        @pl.when(step == steps - 1)
        def _():
            result_ref[...] = (middle[...] + result[...]).astype(low).reshape(streams, rows, width)
            unit, root = normalize(middle[...])
            d_middle = cot_flat.astype(f32) + normalize_back(
                d_two[...], unit, root, gain_ref[...]
            )
            d_middle_ref[...] = d_middle
            branch = d_middle.astype(low)
            d_att = dot(branch, wo[...], 1, 1).T.astype(low)
            total = jnp.zeros((width, width), f32)
            for stream in range(streams):
                rows_of = slice(stream * rows, (stream + 1) * rows)
                for head, owner in enumerate(owners[stream]):
                    d_own[owner] = d_att[head * HEAD_DIM : (head + 1) * HEAD_DIM, rows_of]
                flat = jnp.concatenate([att[owner] for owner in owners[stream]], axis=0)
                total += dot(flat, branch[rows_of], 1, 0)
            for spare in range(devices):
                if spare not in owned:
                    d_own[spare] = jnp.zeros((head_width, rows), low)
            first = core_ref[0] == 0
            keep[...] = jnp.where(first, total[:, :half], total[:, half:])
            give[...] = jnp.where(first, total[:, half:], total[:, :half]).astype(low)

    shapes = (
        ((streams, rows, width), low),
        ((tokens, width), f32),
        ((devices, head_width, rows), low),
        ((width, half), f32),
        ((width, half), low),
    )
    return pl.pallas_call(
        body,
        grid=(steps,),
        out_shape=tuple(jax.ShapeDtypeStruct(*entry) for entry in shapes),
        in_specs=[
            SMEM, whole((tokens, width)), whole((tokens, width)),
            whole(attended.shape), whole(middle.shape), whole(two.shape),
            whole(cotangent.shape), whole(w_out.shape), whole((1, width)),
            pl.BlockSpec((width, chunk), lambda i: (0, i + skip)),
            pl.BlockSpec((chunk, width), lambda i: (i + skip, 0)),
        ],
        out_specs=tuple(whole(shape) for shape, _ in shapes),
        scratch_shapes=[pltpu.VMEM((tokens, width), f32), pltpu.VMEM((tokens, width), f32)],
        compiler_params=LIMIT,
        name="feed_rest",
    )(core, *so_far, attended, middle, two, cotangent, w_out, gain[None, :], w_up, w_down)


def out_rows(width, planes):
    return -(-(width // 4) // (16 * planes)) * 16


def hidden_gradients(
    where, two_mine, two_other, cot_mine, cot_other, w_up, w_down, out_quarter, slots, planes
):
    pieces, tokens, width = two_mine.shape
    hidden = w_up.shape[1] // slots
    rows = width // planes
    extra = out_rows(width, planes)
    quarter = out_quarter.shape[0]
    height = 2 * rows + extra
    low = jnp.bfloat16

    def body(where_ref, two_a, two_b, cot_a, cot_b, up, down, quarter_ref, *rest):
        outs, (up_sum, down_sum, out_sum) = rest[:planes], rest[planes:]
        step = pl.program_id(0)

        def run(two, cot):
            active, slope = gelu_pair(dot(two, up[...], 1, 0))
            d_hidden = (dot(cot, down[...], 1, 1) * slope).astype(low)
            up_term = dot(two, d_hidden, 0, 0)
            down_term = dot(active.astype(low), cot, 0, 0)

            @pl.when(step == 0)
            def _():
                up_sum[...] = up_term
                down_sum[:hidden] = down_term[:, :hidden]
                down_sum[hidden:] = down_term[:, hidden:]

            @pl.when(step > 0)
            def _():
                up_sum[...] += up_term
                down_sum[:hidden] += down_term[:, :hidden]
                down_sum[hidden:] += down_term[:, hidden:]

        @pl.when(step < pieces // 2)
        def _():
            run(two_a[...].reshape(2 * tokens, width), cot_a[...].reshape(2 * tokens, width))

        @pl.when(step >= pieces // 2)
        def _():
            run(two_b[...].reshape(2 * tokens, width), cot_b[...].reshape(2 * tokens, width))

        @pl.when(step == pieces - 1)
        def _():
            out_sum[...] = jnp.zeros_like(out_sum)
            out_sum[:quarter] = quarter_ref[...]
            for index, out in enumerate(outs):
                plane = lax.rem(where_ref[1] + index, planes)
                rows_of = pl.ds(pl.multiple_of(plane * rows, rows), rows)
                out[:rows] = up_sum[rows_of, :].astype(low)
                out[rows : 2 * rows] = down_sum[rows_of, :].astype(low)
                out[2 * rows :] = out_sum[
                    pl.ds(pl.multiple_of(plane * extra, extra), extra), :
                ].astype(low)

    near = pl.BlockSpec(
        (2, tokens, width), lambda i, where: (jnp.minimum(i, pieces // 2 - 1), 0, 0)
    )
    far = pl.BlockSpec((2, tokens, width), lambda i, where: (jnp.maximum(i - pieces // 2, 0), 0, 0))
    return pl.pallas_call(
        body,
        grid_spec=pltpu.PrefetchScalarGridSpec(
            num_scalar_prefetch=1,
            grid=(pieces,),
            in_specs=[
                near, far, near, far,
                pl.BlockSpec((width, hidden), lambda i, where: (0, where[0])),
                pl.BlockSpec((hidden, width), lambda i, where: (where[0], 0)),
                whole(out_quarter.shape),
            ],
            out_specs=[whole((height, hidden))] * planes,
            scratch_shapes=[
                pltpu.VMEM((width, hidden), jnp.float32),
                pltpu.VMEM((width, hidden), jnp.float32),
                pltpu.VMEM((extra * planes, hidden), jnp.float32),
            ],
        ),
        out_shape=[jax.ShapeDtypeStruct((height, hidden), low)] * planes,
        compiler_params=LIMIT,
        name="hidden_gradients",
    )(where, two_mine, two_other, cot_mine, cot_other, w_up, w_down, out_quarter)


def place_hidden(where, mine, other, w_up, w_out, gain, slots):
    spots, planes, height, hidden = mine.shape
    width = w_up.shape[0]
    rows = width // planes
    extra = out_rows(width, planes)
    quarter = width // 4
    f32 = jnp.float32

    def body(where_ref, mine_ref, other_ref, up_ref, gain_ref, up_out, down_out, out, gain_out, low):
        step = pl.program_id(0)

        def put(ref):
            for index in range(planes):
                plane = lax.rem(where_ref[3, 0] + planes - index, planes)
                rows_of = pl.ds(pl.multiple_of(plane * rows, rows), rows)
                up_out[rows_of, :] = ref[0, index, :rows].astype(f32)
                low[rows_of, :] = ref[0, index, rows : 2 * rows].astype(f32)
                row = where_ref[1, step] * quarter + plane * extra
                rows_of = pl.ds(pl.multiple_of(row, 16), extra)
                piece = ref[0, index, 2 * rows :].astype(f32)

                @pl.when((plane * extra < quarter) & (where_ref[2, step] == 0))
                def _():
                    out[rows_of, :hidden] = piece

                @pl.when((plane * extra < quarter) & (where_ref[2, step] == 1))
                def _():
                    out[rows_of, hidden:] = piece

        @pl.when(step < spots)
        def _():
            put(mine_ref)

        @pl.when(step >= spots)
        def _():
            put(other_ref)

        down_out[:, :hidden] = low[:hidden]
        down_out[:, hidden:] = low[hidden:]
        terms = jnp.sum(up_out[...] * up_ref[...].astype(f32), axis=1, keepdims=True)

        @pl.when(step == 0)
        def _():
            gain_out[...] = terms

        @pl.when(step > 0)
        def _():
            gain_out[...] += terms

        @pl.when(step == slots - 1)
        def _():
            gain_out[...] /= gain_ref[...]

    return pl.pallas_call(
        body,
        grid_spec=pltpu.PrefetchScalarGridSpec(
            num_scalar_prefetch=1,
            grid=(slots,),
            in_specs=[
                pl.BlockSpec(
                    (1, planes, height, hidden),
                    lambda i, where: (jnp.minimum(i, spots - 1), 0, 0, 0),
                ),
                pl.BlockSpec(
                    (1, planes, height, hidden),
                    lambda i, where: (jnp.maximum(i - spots, 0), 0, 0, 0),
                ),
                pl.BlockSpec((width, hidden), lambda i, where: (0, where[0, i])),
                whole((width, 1)),
            ],
            out_specs=[
                pl.BlockSpec((width, hidden), lambda i, where: (0, where[0, i])),
                pl.BlockSpec((hidden, width), lambda i, where: (where[0, i], 0)),
                whole((width, width)),
                whole((width, 1)),
            ],
            scratch_shapes=[pltpu.VMEM((width, hidden), f32)],
        ),
        out_shape=[
            jax.ShapeDtypeStruct(w_up.shape, f32),
            jax.ShapeDtypeStruct(w_up.shape[::-1], f32),
            jax.ShapeDtypeStruct(w_out.shape, f32),
            jax.ShapeDtypeStruct((width, 1), f32),
        ],
        compiler_params=LIMIT,
        name="place_hidden",
    )(where, mine, other, w_up, gain[:, None])


def head_products(where, grads, mine, other):
    devices, height, rows = grads.shape
    frames, _, width = mine.shape
    half = width // 2

    def body(where_ref, d_ref, a_ref, b_ref, keep, give, total):
        core = where_ref[0]
        total[...] = jnp.zeros_like(total)

        def one(pair, _):
            lefts, rights = [], []
            for frame in (2 * pair, 2 * pair + 1):
                lefts += [d_ref[2 * frame + core], d_ref[2 * frame + 1 - core]]
                rights += [a_ref[frame], b_ref[frame]]
            total[...] += dot(
                jnp.concatenate(lefts, axis=1), jnp.concatenate(rights, axis=0), 1, 0
            )
            return 0

        lax.fori_loop(0, frames // 2, one, 0)
        first = where_ref[1] == 0
        keep[...] = jnp.where(first, total[:, :half], total[:, half:])
        give[...] = jnp.where(first, total[:, half:], total[:, :half]).astype(jnp.bfloat16)

    return pl.pallas_call(
        body,
        out_shape=(
            jax.ShapeDtypeStruct((height, half), jnp.float32),
            jax.ShapeDtypeStruct((height, half), jnp.bfloat16),
        ),
        in_specs=[SMEM] + [VMEM] * 3,
        out_specs=(VMEM, VMEM),
        scratch_shapes=[pltpu.VMEM((height, width), jnp.float32)],
        compiler_params=LIMIT,
        name="head_products",
    )(where, grads, mine, other)


def place_heads(where, mine, other, weights, gain, owners):
    _, height, half = mine.shape
    width = 2 * half
    f32 = jnp.float32

    def body(where_ref, mine_ref, other_ref, wq, wk, wv, gain_ref, dq, dk, dv, gain_out):
        for side in range(2):
            blocks = []
            for head in range(HEADS):
                entry = where_ref[side, head]
                own = where_ref[2, 0] == owners[0][head] % 2
                blocks.append(jnp.where(own, mine_ref[entry], other_ref[entry]))
            rows_of = slice(side * half, (side + 1) * half)
            terms = jnp.zeros((half, 1), f32)
            for kind, (weight, out) in enumerate(((wq, dq), (wk, dk), (wv, dv))):
                rows = slice(kind * HEAD_DIM, (kind + 1) * HEAD_DIM)
                flat = jnp.concatenate([block[rows] for block in blocks], axis=0)
                grad = flat.T.astype(f32)
                out[rows_of] = grad
                terms += jnp.sum(grad * weight[rows_of].astype(f32), axis=1, keepdims=True)
            gain_out[rows_of] = terms / gain_ref[rows_of]

    return pl.pallas_call(
        body,
        out_shape=[jax.ShapeDtypeStruct((width, width), f32)] * 3
        + [jax.ShapeDtypeStruct((width, 1), f32)],
        in_specs=[SMEM] + [VMEM] * 6,
        out_specs=[VMEM] * 4,
        compiler_params=LIMIT,
        name="place_heads",
    )(where, mine, other, *weights, gain[:, None])


def input_gradient(grads, weights, block_input, gain, d_middle, owners):
    streams, rows, width = block_input.shape

    def body(d_ref, wq, wk, wv, x_ref, gain_ref, d_middle_ref, out):
        for stream in range(streams):
            d_normed = jnp.zeros((rows, width), jnp.float32)
            for kind, weight in enumerate((wq, wk, wv)):
                rows_of = slice(kind * HEAD_DIM, (kind + 1) * HEAD_DIM)
                flat = jnp.concatenate([d_ref[owner, rows_of] for owner in owners[stream]], axis=0)
                d_normed += dot(flat.T, weight[...], 1, 1)
            unit, root = normalize(x_ref[stream].astype(jnp.float32))
            d_values = normalize_back(d_normed, unit, root, gain_ref[...])
            out[stream] = d_middle_ref[stream * rows : (stream + 1) * rows] + d_values

    return pl.pallas_call(
        body,
        out_shape=jax.ShapeDtypeStruct(block_input.shape, jnp.float32),
        in_specs=[VMEM] * 7,
        out_specs=VMEM,
        compiler_params=LIMIT,
        name="input_gradient",
    )(grads, *weights, block_input, gain[None, :], d_middle)


def wide(ref, frame, spaces, first, last, count=1):
    return jnp.concatenate(
        [ref[frame * spaces + j, first:last, :] for j in range(spaces * count)], axis=1
    )


def attend(lo, packed, frames):
    devices, _, rows = packed.shape
    spaces = devices // frames
    per_frame = rows * spaces
    dim = HEAD_DIM

    def body(lo_ref, r_ref, o_ref, low_ref, lse_ref, kv, top, total, summed):
        def turn_keys(device, _):
            kv[pl.ds(pl.multiple_of(device * rows, rows), rows), :] = r_ref[device, dim:, :].T
            return 0

        lax.fori_loop(0, devices, turn_keys, 0, unroll=4)

        def group(queries, _):
            first = queries * CLIP
            query = [wide(r_ref, first + i, spaces, 0, dim) for i in range(CLIP)]

            def update(i, keys, count, fresh):
                base = pl.multiple_of(keys * CLIP * per_frame, per_frame)
                scores = dot(kv[pl.ds(base, count * per_frame), :dim], query[i], 1, 0)
                new_top = jnp.max(scores, axis=0, keepdims=True)
                if not fresh:
                    old_top = top[i]
                    new_top = jnp.maximum(old_top, new_top)
                weights = jnp.exp(scores - new_top)
                new_total = jnp.sum(weights, axis=0, keepdims=True)
                values = wide(r_ref, keys * CLIP, spaces, 2 * dim, 3 * dim, count)
                new_sum = dot(values, weights.astype(jnp.bfloat16), 1, 0)
                if not fresh:
                    factor = jnp.exp(old_top - new_top)
                    new_total += total[i] * factor
                    new_sum += summed[i] * factor
                top[i] = new_top
                total[i] = new_total
                summed[i] = new_sum

            for i in range(CLIP):
                update(i, queries, i + 1, True)

            def earlier(keys, _):
                for i in range(CLIP):
                    update(i, keys, CLIP, False)
                return 0

            lax.fori_loop(lo_ref[first] // CLIP, queries, earlier, 0)
            for i in range(CLIP):
                out = summed[i] / total[i]
                for j in range(spaces):
                    piece = out[:, j * rows : (j + 1) * rows]
                    o_ref[(first + i) * spaces + j] = piece
                    low_ref[(first + i) * spaces + j] = piece.astype(jnp.bfloat16)
                lse_ref[first + i] = top[i] + jnp.log(total[i])
            return 0

        lax.fori_loop(0, frames // CLIP, group, 0)

    f32 = jnp.float32
    return pl.pallas_call(
        body,
        out_shape=(
            jax.ShapeDtypeStruct((devices, dim, rows), f32),
            jax.ShapeDtypeStruct((devices, dim, rows), jnp.bfloat16),
            jax.ShapeDtypeStruct((frames, 1, per_frame), f32),
            jax.ShapeDtypeStruct((devices * rows, 2 * dim), jnp.bfloat16),
        ),
        in_specs=[SMEM, VMEM],
        out_specs=(VMEM,) * 4,
        scratch_shapes=[
            pltpu.VMEM((CLIP, 1, per_frame), f32),
            pltpu.VMEM((CLIP, 1, per_frame), f32),
            pltpu.VMEM((CLIP, dim, per_frame), f32),
        ],
        compiler_params=LIMIT,
        name="attend",
    )(lo, packed)


def attend_back_ready(packed, d_own, out, frames):
    devices, _, rows = packed.shape
    spaces = devices // frames
    dim = HEAD_DIM

    def body(r_ref, d_ref, o_ref, qd, delta):
        def turn_frame(frame, _):
            for j in range(spaces):
                device = frame * spaces + j
                both = jnp.concatenate([r_ref[device, :dim, :], d_ref[device]], axis=0)
                qd[pl.ds(pl.multiple_of(device * rows, rows), rows), :] = both.T
                delta[frame, :, j * rows : (j + 1) * rows] = jnp.sum(
                    d_ref[device].astype(jnp.float32) * o_ref[device], axis=0, keepdims=True
                )
            return 0

        lax.fori_loop(0, frames, turn_frame, 0, unroll=2)

    return pl.pallas_call(
        body,
        out_shape=(
            jax.ShapeDtypeStruct((devices * rows, 2 * dim), jnp.bfloat16),
            jax.ShapeDtypeStruct((frames, 1, spaces * rows), jnp.float32),
        ),
        in_specs=[VMEM] * 3,
        out_specs=(VMEM, VMEM),
        compiler_params=LIMIT,
        name="attend_back_ready",
    )(packed, d_own, out)


def attend_back(hi, packed, d_own, lse, delta, kv, qd, tables, d_query, earlier, frames, start, stop):
    devices, _, rows = packed.shape
    spaces = devices // frames
    per_frame = rows * spaces
    dim = HEAD_DIM
    last = stop * CLIP == frames
    f32 = jnp.float32
    shift = dim if last else 0
    base = 0 if last else start * CLIP * spaces

    def body(hi_ref, r_ref, d_ref, lse_ref, delta_ref, kv_ref, qd_ref, table_ref, *rest):
        rest = list(rest)
        before = rest.pop(0) if start else None
        pieces = [rest.pop(0) for _ in earlier] if last else []
        out = rest.pop(0)
        d_query_ref, acc, left = rest

        def begin(frame, _):
            d_query_ref[frame] = before[frame] if start else jnp.zeros((dim, per_frame), f32)
            return 0

        lax.fori_loop(0, frames, begin, 0)
        done = 0
        for piece in pieces:
            out[done : done + piece.shape[0], dim:, :] = piece[...]
            done += piece.shape[0]
        first_half = lax.broadcasted_iota(jnp.int32, (per_frame, 2 * dim), 1) < dim

        def group(keys, _):
            first = keys * CLIP
            for i in range(CLIP):
                rows_of = pl.ds(pl.multiple_of((first + i) * per_frame, per_frame), per_frame)
                both = kv_ref[rows_of, :]
                zero = jnp.zeros_like(both)
                left[i, :per_frame] = jnp.where(first_half, both, zero)
                left[i, per_frame:] = jnp.where(first_half, zero, both)

            def block(i, frame, count, fresh):
                own = [d_ref[frame * spaces + j] for j in range(spaces * count)]
                right = jnp.concatenate(
                    [wide(r_ref, frame, spaces, 0, dim, count), jnp.concatenate(own, axis=1)],
                    axis=0,
                )
                both = dot(left[i], right, 1, 0)
                row = lambda ref: jnp.concatenate([ref[frame + j] for j in range(count)], axis=1)
                weights = jnp.exp(both[:per_frame] - row(lse_ref))
                d_scores = (weights * (both[per_frame:] - row(delta_ref))).astype(jnp.bfloat16)
                pair = jnp.concatenate([weights.astype(jnp.bfloat16), d_scores], axis=0)
                tokens = pl.ds(pl.multiple_of(frame * per_frame, per_frame), count * per_frame)
                term = dot(pair, qd_ref[tokens, :], 1, 0)
                if fresh:
                    acc[i] = term
                else:
                    acc[i] += term
                key_rows = wide(r_ref, first + i, spaces, dim, 2 * dim)
                change = dot(key_rows, d_scores, 1, 0)
                for j in range(count):
                    d_query_ref[frame + j] += change[:, j * per_frame : (j + 1) * per_frame]

            for i in range(CLIP):
                block(i, first + i, CLIP - i, True)

            def later(queries, _):
                for i in range(CLIP):
                    block(i, queries * CLIP, CLIP, False)
                return 0

            lax.fori_loop(keys + 1, hi_ref[first] // CLIP, later, 0)
            for i in range(CLIP):
                total = acc[i]
                d_key = total[per_frame:].T[:dim]
                d_key = turned(d_key, table_ref[first + i, 0], table_ref[first + i, 1], -1.0)
                d_key = d_key.astype(jnp.bfloat16)
                d_value = total[:per_frame].T[dim:].astype(jnp.bfloat16)
                for j in range(spaces):
                    device = (first + i) * spaces + j - base
                    columns = slice(j * rows, (j + 1) * rows)
                    out[device, shift : shift + dim, :] = d_key[:, columns]
                    out[device, shift + dim : shift + 2 * dim, :] = d_value[:, columns]
            return 0

        lax.fori_loop(start, stop, group, 0)
        if last:

            def finish(frame, _):
                whole_query = d_query_ref[frame] * (1.0 / math.sqrt(dim))
                whole_query = turned(whole_query, table_ref[frame, 0], table_ref[frame, 1], -1.0)
                whole_query = whole_query.astype(jnp.bfloat16)
                for j in range(spaces):
                    out[frame * spaces + j, :dim, :] = whole_query[:, j * rows : (j + 1) * rows]
                return 0

            lax.fori_loop(0, frames, finish, 0)

    if last:
        out_shape = (devices, 3 * dim, rows)
    else:
        out_shape = ((stop - start) * CLIP * spaces, 2 * dim, rows)
    inputs = [hi, packed, d_own, lse, delta, kv, qd, tables]
    inputs += [d_query] if start else []
    inputs += list(earlier) if last else []
    return pl.pallas_call(
        body,
        out_shape=(
            jax.ShapeDtypeStruct(out_shape, jnp.bfloat16),
            jax.ShapeDtypeStruct((frames, dim, per_frame), f32),
        ),
        in_specs=[SMEM] + [VMEM] * (len(inputs) - 1),
        out_specs=(VMEM, VMEM),
        scratch_shapes=[
            pltpu.VMEM((CLIP, 2 * per_frame, 2 * dim), f32),
            pltpu.VMEM((CLIP, 2 * per_frame, 2 * dim), jnp.bfloat16),
        ],
        compiler_params=LIMIT,
        name="attend_back",
    )(*inputs)


def after(value, *others):
    return lax.optimization_barrier((value, *others))[0]


class Ring:
    def __init__(self):
        self.frames = lax.axis_size("frame")
        self.spaces = lax.axis_size("space")
        self.planes = self.frames // 4
        self.frame = lax.axis_index("frame")
        self.core = lax.axis_index("space")
        self.plane = self.frame // 4
        self.spot = self.frame % 4
        bits = (self.frame % 2, (self.frame // 2) % 2)
        self.first_bit = jnp.where(self.core == 0, bits[0], bits[1])
        self.second_bit = jnp.where(self.core == 0, bits[1], bits[0])

    def send(self, value, target):
        moves = []
        for frame in range(self.frames):
            for core in range(self.spaces):
                to_frame, to_core = target(frame, core)
                moves.append((frame * self.spaces + core, to_frame * self.spaces + to_core))
        return lax.ppermute(value, ("frame", "space"), moves)

    def first(self, value):
        return self.send(value, lambda frame, core: (frame ^ (1 if core == 0 else 2), core))

    def second(self, value):
        return self.send(value, lambda frame, core: (frame ^ (2 if core == 0 else 1), core))

    def across(self, value):
        return self.send(value, lambda frame, core: (frame, 1 - core))

    def up(self, value, step):
        size = self.frames
        return self.send(value, lambda frame, core: ((frame + 4 * step) % size, core))

    def reduce_planes(self, pieces):
        total = pieces[0].astype(jnp.float32)
        for step, piece in enumerate(pieces[1:], 1):
            total = total + self.up(piece, step).astype(jnp.float32)
        return total.astype(jnp.bfloat16)

    def spread_planes(self, value, count):
        return jnp.stack([value] + [self.up(value, step) for step in range(1, count)])

    def gather_spots(self):
        near = jnp.where(self.core == 0, 2, 1)
        own = jnp.stack([self.spot, self.spot ^ near, self.spot ^ (3 - near), self.spot ^ 3])
        other = jnp.stack([self.spot, self.spot ^ (3 - near), self.spot ^ near, self.spot ^ 3])
        cores = jnp.repeat(jnp.stack([self.core, 1 - self.core]), 4)
        return jnp.concatenate([own, other]), cores

    def gather(self, value):
        pair = jnp.stack([value, self.second(value)])
        return jnp.concatenate([pair, self.first(pair)], axis=0)

    def halve(self, value, bit, exchange):
        rows, columns = value.shape
        cut = value.reshape(2, rows // 2, columns)
        keep = lax.dynamic_index_in_dim(cut, bit, 0, keepdims=False)
        give = lax.dynamic_index_in_dim(cut, 1 - bit, 0, keepdims=False)
        return keep + exchange(give.astype(jnp.bfloat16)).astype(jnp.float32)


def quarter_rows(spots, cores):
    return jnp.where(cores == 1, spots, (spots % 2) * 2 + spots // 2)


def frame_limits(clip_frames, frames):
    ends = jnp.cumsum(clip_frames, axis=1, dtype=jnp.int32)
    begins = ends - clip_frames
    index = jnp.arange(frames, dtype=jnp.int32)[None, :, None]
    inside = (index >= begins[:, None, :]) & (index < ends[:, None, :])
    pick = lambda table: jnp.sum(jnp.where(inside, table[:, None, :], 0), axis=2, dtype=jnp.int32)
    return pick(begins), pick(ends)


def local(
    block_input,
    norm1_gain,
    w_query,
    w_key,
    w_value,
    w_out,
    norm2_gain,
    w_up,
    w_down,
    clip_frames,
    cotangent,
):
    streams, rows, width = block_input.shape
    ring = Ring()
    frames, spaces, planes = ring.frames, ring.spaces, ring.planes
    devices = frames * spaces
    per_frame = rows * spaces
    tokens = streams * rows
    axes = ("frame", "space")
    low = jnp.bfloat16
    core = jnp.reshape(ring.core, (1,))
    spots, cores = ring.gather_spots()
    slots = 4 * spaces

    owners = head_owners(frames, spaces)
    w_projections = (w_query, w_key, w_value)

    begin, end = frame_limits(clip_frames, frames)
    frame_ids = jnp.arange(frames, dtype=jnp.int32)
    mine = ring.frame * spaces + ring.core
    idle = ~jnp.any(mine == jnp.asarray(owners))
    side = ring.frame % 2
    lo = jnp.where(idle, frame_ids, jnp.where(side == 0, begin[0], begin[1]))
    hi = jnp.where(idle, frame_ids, jnp.where(side == 0, end[0], end[1]))

    def swap(value):
        return lax.all_to_all(value, axes, 0, 0, tiled=True)

    spot_of = jnp.stack([ring.frame, ring.core * rows])
    sent, normed = project(
        spot_of, clip_frames, block_input, norm1_gain, *w_projections, owners, devices, per_frame
    )
    packed = swap(sent)
    tables = rope_tables(after(lo, sent), frames, per_frame)
    neighbour = lambda value: ring.send(value, lambda frame, core: (frame ^ 1, core))
    normed_later = after(normed, packed)
    stream_near = neighbour(lax.dynamic_index_in_dim(normed_later, 1 - side, 0))
    stream_own = lax.dynamic_index_in_dim(normed_later, side, 0)
    stream_pair = jnp.where(
        side == 0,
        jnp.concatenate([stream_own, stream_near]),
        jnp.concatenate([stream_near, stream_own]),
    )
    same_side = [list(range(start, frames, 2)) for start in range(2)]
    stream_mine = lax.all_gather(
        stream_pair, "frame", axis=0, tiled=True, axis_index_groups=same_side
    )
    cot_flat = cotangent.reshape(tokens, width)
    cot_one = ring.second(after(cot_flat, packed))
    out, out_low, lse, kv = attend(lo, packed, frames)
    attended = swap(out_low)
    cot_pair = after(jnp.stack([cot_flat, cot_one]), out_low)
    cot_mine = jnp.concatenate([cot_pair, ring.first(cot_pair)], axis=0)

    middle, two = attention_out(attended, block_input, w_out, norm2_gain, owners)
    cot_other = ring.across(after(cot_mine, middle))
    chunk, skip = 512, 3
    so_far = feed_first(two, cotangent, w_up, w_down, chunk, skip)
    two_pair = jnp.stack([two, ring.second(two)])
    so_far = after(so_far, two_pair)
    two_mine = jnp.concatenate([two_pair, ring.first(two_pair)], axis=0)
    block_output, d_middle, d_sent, out_keep, out_give = feed_rest(
        core, so_far, attended, middle, two, cotangent, w_out, norm2_gain, w_up, w_down,
        chunk, skip, owners,
    )
    d_own = swap(d_sent)
    two_other = ring.across(two_mine)
    out_sum = out_keep + ring.across(out_give).astype(jnp.float32)
    out_sum = ring.halve(out_sum, ring.first_bit, ring.first)
    out_sum = ring.halve(out_sum, ring.second_bit, ring.second)
    pieces = hidden_gradients(
        jnp.stack([ring.spot * spaces + ring.core, ring.plane]),
        two_mine, two_other, cot_mine, cot_other, w_up, w_down, out_sum, slots, planes,
    )

    total = ring.reduce_planes(pieces)
    stream_other = ring.across(stream_mine)
    qd, delta = attend_back_ready(packed, after(d_own, pieces[0]), out, frames)
    groups = frames // CLIP
    cuts = [0, groups // 4, groups // 2, groups]
    d_query, earlier = None, []
    for start, stop in zip(cuts[:-1], cuts[1:]):
        delta_now = after(delta, total) if stop == groups else delta
        result, d_query = attend_back(
            hi, packed, d_own, lse, delta_now, kv, qd, tables, d_query, earlier, frames, start, stop
        )
        earlier.append(result)
    hidden_mine = ring.gather(ring.spread_planes(total, planes))
    back = swap(result)
    hidden_other = ring.across(hidden_mine)
    unit_slots = spots * spaces + cores
    where = jnp.stack(
        [unit_slots, quarter_rows(spots, cores), cores, jnp.broadcast_to(ring.plane, cores.shape)]
    )
    grad_up, grad_down, grad_out, gain_two = place_hidden(
        where, hidden_mine, hidden_other, w_up, w_out, norm2_gain, slots
    )

    keep, give = head_products(jnp.stack([ring.core, side]), result, stream_mine, stream_other)
    heads_sum = (keep + neighbour(give).astype(jnp.float32)).astype(low)
    heads_mine = ring.gather(ring.spread_planes(heads_sum, planes))
    heads_other = ring.across(heads_mine)
    owner_of = jnp.asarray([[owners[stream][head] for head in range(HEADS)] for stream in range(2)])
    owner_plane, owner_spot = owner_of // (4 * spaces), owner_of // spaces % 4
    owner_core = owner_of % spaces
    list_of = jnp.where(owner_core == ring.core, 0, 1)
    entries = jnp.stack([spots[:4], spots[4:]])[list_of] == owner_spot[..., None]
    entry = jnp.sum(jnp.where(entries, jnp.arange(4), 0), axis=-1)
    entry = entry * planes + (ring.plane - owner_plane) % planes
    where = jnp.concatenate([entry, jnp.broadcast_to(ring.core, (1, HEADS))]).astype(jnp.int32)
    flat = lambda value: value.reshape((-1,) + value.shape[2:])
    grad_query, grad_key, grad_value, gain_one = place_heads(
        where, flat(heads_mine), flat(heads_other), w_projections, norm1_gain, owners
    )
    grad_input = input_gradient(back, w_projections, block_input, norm1_gain, d_middle, owners)
    return (
        block_output,
        grad_input,
        gain_one.reshape(width),
        grad_query,
        grad_key,
        grad_value,
        grad_out,
        gain_two.reshape(width),
        grad_up,
        grad_down,
    )


def solution(mesh):
    spread = P(None, ("frame", "space"), None)
    in_specs = (spread,) + (P(),) * 9 + (spread,)
    out_specs = (spread, spread) + (P(),) * 8
    return jax.shard_map(local, mesh=mesh, in_specs=in_specs, out_specs=out_specs, check_vma=False)
```

```python
import math

import jax
import jax.numpy as jnp
import numpy as np
from jax import lax
from jax.experimental import pallas as pl
from jax.experimental.pallas import tpu as pltpu
from jax.sharding import PartitionSpec as P

HEADS = 12
HEAD_DIM = 64
VMEM = pl.BlockSpec(memory_space=pltpu.VMEM)
ANY = pl.BlockSpec(memory_space=pl.ANY)
SMEM = pl.BlockSpec(memory_space=pltpu.SMEM)
LIMIT = pltpu.CompilerParams(vmem_limit_bytes=56 * 2**20)
FLOPS = 1.15e9


def busy(microseconds):
    return pl.CostEstimate(flops=int(microseconds * FLOPS), transcendentals=0, bytes_accessed=0)


CLIP = 4


def dot(left, right, left_dim, right_dim):
    return lax.dot_general(
        left,
        right,
        (((left_dim,), (right_dim,)), ((), ())),
        preferred_element_type=jnp.float32,
    )


def head_owners(frames, spaces):
    planes = frames // 4
    share = -(-HEADS // planes)
    return [
        [
            ((head // share) * 4 + (head % share) // spaces * 2 + stream) * spaces
            + (head % share) % spaces
            for head in range(HEADS)
        ]
        for stream in range(2)
    ]


def normalize(values):
    average = jnp.mean(values, axis=-1, keepdims=True)
    centred = values - average
    root = lax.rsqrt(jnp.mean(centred * centred, axis=-1, keepdims=True) + 1e-05)
    return centred * root, root


def normalize_back(d_scaled, unit, root, gain):
    d_unit = d_scaled * gain
    mean_one = jnp.mean(d_unit, axis=-1, keepdims=True)
    mean_two = jnp.mean(d_unit * unit, axis=-1, keepdims=True)
    return root * (d_unit - mean_one - unit * mean_two)


def frequencies(columns):
    half = HEAD_DIM // 2
    values = np.exp(np.arange(half) * (-2.0 * math.log(10000.0) / HEAD_DIM))
    return jnp.asarray(np.broadcast_to(values[:, None], (half, columns)), jnp.float32)


def turned(value, cosine, sine, sign):
    half = HEAD_DIM // 2
    first, second = value[:half], value[half:]
    return jnp.concatenate(
        [first * cosine - sign * second * sine, second * cosine + sign * first * sine], axis=0
    )


def project(place, clips, block_input, gain, w_query, w_key, w_value, owners, devices, per_frame):
    streams, rows, width = block_input.shape
    half = HEAD_DIM // 2
    low = jnp.bfloat16
    scale = 1.0 / math.sqrt(HEAD_DIM)
    owned = {device for row in owners for device in row}

    def body(place_ref, clips_ref, freq_ref, x_ref, gain_ref, wq, wk, wv, out, normed_out, table):
        frame, first_row = place_ref[0], place_ref[1]
        for stream in range(streams):
            begin = jnp.int32(0)
            running = jnp.int32(0)
            for clip in range(clips_ref.shape[1]):
                length = clips_ref[stream, clip]
                begin = jnp.where((frame >= running) & (frame < running + length), running, begin)
                running = running + length
            row = lax.broadcasted_iota(jnp.int32, (half, rows), 1)
            position = ((frame - begin) * per_frame + first_row + row).astype(jnp.float32)
            angles = position * freq_ref[...]
            table[0, stream] = jnp.cos(angles)
            table[1, stream] = jnp.sin(angles)
        values = x_ref[...].astype(jnp.float32).reshape(streams * rows, width)
        normed = (normalize(values)[0] * gain_ref[...]).astype(low)
        normed_out[...] = normed.reshape(streams, rows, width)
        for kind, weight in enumerate((wq, wk, wv)):
            product = dot(normed, weight[...], 1, 0).T
            for stream in range(streams):
                columns = slice(stream * rows, (stream + 1) * rows)
                for head in range(HEADS):
                    piece = product[head * HEAD_DIM : (head + 1) * HEAD_DIM, columns]
                    if kind < 2:
                        piece = turned(piece, table[0, stream], table[1, stream], 1.0)
                    if kind == 0:
                        piece = piece * scale
                    out[
                        owners[stream][head], kind * HEAD_DIM : (kind + 1) * HEAD_DIM, :
                    ] = piece.astype(low)
        for spare in range(devices):
            if spare not in owned:
                out[spare] = jnp.zeros((3 * HEAD_DIM, rows), low)

    return pl.pallas_call(
        body,
        out_shape=(
            jax.ShapeDtypeStruct((devices, 3 * HEAD_DIM, rows), low),
            jax.ShapeDtypeStruct((streams, rows, width), low),
        ),
        in_specs=[SMEM, SMEM] + [VMEM] * 6,
        out_specs=(VMEM, VMEM),
        scratch_shapes=[pltpu.VMEM((2, streams, half, rows), jnp.float32)],
        compiler_params=LIMIT,
        cost_estimate=busy(5),
        name="project",
    )(place, clips, frequencies(rows), block_input, gain[None, :], w_query, w_key, w_value)


def rope_tables(lo, frames, per_frame):
    half = HEAD_DIM // 2

    def body(lo_ref, freq_ref, out):
        def one(frame, _):
            row = lax.broadcasted_iota(jnp.int32, (half, per_frame), 1)
            position = ((frame - lo_ref[frame]) * per_frame + row).astype(jnp.float32)
            angles = position * freq_ref[...]
            out[frame, 0] = jnp.cos(angles)
            out[frame, 1] = jnp.sin(angles)
            return 0

        lax.fori_loop(0, frames, one, 0)

    return pl.pallas_call(
        body,
        out_shape=jax.ShapeDtypeStruct((frames, 2, half, per_frame), jnp.float32),
        in_specs=[SMEM, VMEM],
        out_specs=VMEM,
        compiler_params=LIMIT,
        cost_estimate=busy(4),
        name="rope_tables",
    )(lo, frequencies(per_frame))


GELU = math.sqrt(2.0 / math.pi)


def gelu_pair(value):
    square = value * value
    bent = jnp.tanh(GELU * value * (1.0 + 0.044715 * square))
    side = 0.5 * (1.0 + bent)
    slope = side + 0.5 * value * (1.0 - bent * bent) * (GELU * (1.0 + 3 * 0.044715 * square))
    return value * side, slope


def attention_out(attended, block_input, w_out, gain, owners):
    streams, rows, width = block_input.shape
    low = jnp.bfloat16

    def body(att, x_ref, wo, gain_ref, middle, two_ref):
        for stream in range(streams):
            rows_of = slice(stream * rows, (stream + 1) * rows)
            flat = jnp.concatenate([att[owner] for owner in owners[stream]], axis=0)
            values = x_ref[stream].astype(jnp.float32) + dot(flat.T, wo[...], 1, 0)
            middle[rows_of] = values
            two_ref[rows_of] = (normalize(values)[0] * gain_ref[...]).astype(low)

    return pl.pallas_call(
        body,
        out_shape=(
            jax.ShapeDtypeStruct((streams * rows, width), jnp.float32),
            jax.ShapeDtypeStruct((streams * rows, width), low),
        ),
        in_specs=[VMEM] * 4,
        out_specs=(VMEM, VMEM),
        compiler_params=LIMIT,
        cost_estimate=busy(3),
        name="attention_out",
    )(attended, block_input, w_out, gain[None, :])


def as_row(column):
    return jnp.broadcast_to(column, (column.shape[0], 128)).T[:1]


def whole(shape):
    return pl.BlockSpec(shape, lambda *indices: (0,) * len(shape))


def feed_first(two, cotangent, w_up, w_down, chunk, steps):
    tokens, width = two.shape
    low = jnp.bfloat16

    def body(two_ref, cot, up, down, result, d_two):
        cot_flat = cot[...].reshape(tokens, width)
        active, slope = gelu_pair(dot(two_ref[...], up[...], 1, 0))
        d_hidden = (dot(cot_flat, down[...], 1, 1) * slope).astype(low)
        forward = dot(active.astype(low), down[...], 1, 0)
        backward = dot(d_hidden, up[...], 1, 1)

        @pl.when(pl.program_id(0) == 0)
        def _():
            result[...] = forward
            d_two[...] = backward

        @pl.when(pl.program_id(0) > 0)
        def _():
            result[...] += forward
            d_two[...] += backward

    return pl.pallas_call(
        body,
        grid=(steps,),
        out_shape=(jax.ShapeDtypeStruct((tokens, width), jnp.float32),) * 2,
        in_specs=[
            whole(two.shape), whole(cotangent.shape),
            pl.BlockSpec((width, chunk), lambda i: (0, i)),
            pl.BlockSpec((chunk, width), lambda i: (i, 0)),
        ],
        out_specs=(whole((tokens, width)),) * 2,
        compiler_params=LIMIT,
        cost_estimate=busy(7),
        name="feed_first",
    )(two, cotangent, w_up, w_down)


def feed_rest(core, so_far, attended, middle, two, cotangent, w_out, gain, w_up, w_down, chunk, skip, owners):
    devices, head_width, rows = attended.shape
    streams, _, width = cotangent.shape
    tokens = streams * rows
    half = width // 2
    steps = w_up.shape[1] // chunk - skip
    low = jnp.bfloat16
    f32 = jnp.float32
    owned = {device for row in owners for device in row}

    def body(
        core_ref, first_result, first_two, att, middle, two_ref, cot, wo, gain_ref, up, down,
        result_ref, d_middle_ref, d_own, keep, give,
        result, d_two,
    ):
        step = pl.program_id(0)
        cot_flat = cot[...].reshape(tokens, width)
        active, slope = gelu_pair(dot(two_ref[...], up[...], 1, 0))
        d_hidden = (dot(cot_flat, down[...], 1, 1) * slope).astype(low)
        forward = dot(active.astype(low), down[...], 1, 0)
        backward = dot(d_hidden, up[...], 1, 1)

        @pl.when(step == 0)
        def _():
            result[...] = first_result[...] + forward
            d_two[...] = first_two[...] + backward

        @pl.when(step > 0)
        def _():
            result[...] += forward
            d_two[...] += backward

        @pl.when(step == steps - 1)
        def _():
            result_ref[...] = (middle[...] + result[...]).astype(low).reshape(streams, rows, width)
            unit, root = normalize(middle[...])
            d_middle = cot_flat.astype(f32) + normalize_back(
                d_two[...], unit, root, gain_ref[...]
            )
            d_middle_ref[...] = d_middle
            branch = d_middle.astype(low)
            d_att = dot(branch, wo[...], 1, 1).T.astype(low)
            total = jnp.zeros((width, width), f32)
            for stream in range(streams):
                rows_of = slice(stream * rows, (stream + 1) * rows)
                for head, owner in enumerate(owners[stream]):
                    d_own[owner] = d_att[head * HEAD_DIM : (head + 1) * HEAD_DIM, rows_of]
                flat = jnp.concatenate([att[owner] for owner in owners[stream]], axis=0)
                total += dot(flat, branch[rows_of], 1, 0)
            for spare in range(devices):
                if spare not in owned:
                    d_own[spare] = jnp.zeros((head_width, rows), low)
            first = core_ref[0] == 0
            keep[...] = jnp.where(first, total[:, :half], total[:, half:])
            give[...] = jnp.where(first, total[:, half:], total[:, :half]).astype(low)

    shapes = (
        ((streams, rows, width), low),
        ((tokens, width), f32),
        ((devices, head_width, rows), low),
        ((width, half), f32),
        ((width, half), low),
    )
    return pl.pallas_call(
        body,
        grid=(steps,),
        out_shape=tuple(jax.ShapeDtypeStruct(*entry) for entry in shapes),
        in_specs=[
            SMEM, whole((tokens, width)), whole((tokens, width)),
            whole(attended.shape), whole(middle.shape), whole(two.shape),
            whole(cotangent.shape), whole(w_out.shape), whole((1, width)),
            pl.BlockSpec((width, chunk), lambda i: (0, i + skip)),
            pl.BlockSpec((chunk, width), lambda i: (i + skip, 0)),
        ],
        out_specs=tuple(whole(shape) for shape, _ in shapes),
        scratch_shapes=[pltpu.VMEM((tokens, width), f32), pltpu.VMEM((tokens, width), f32)],
        compiler_params=LIMIT,
        cost_estimate=busy(10),
        name="feed_rest",
    )(core, *so_far, attended, middle, two, cotangent, w_out, gain[None, :], w_up, w_down)


def hidden_gradients(
    where, two_mine, two_other, cot_mine, cot_other, w_up, w_down, slots, planes
):
    pieces, tokens, width = two_mine.shape
    hidden = w_up.shape[1] // slots
    rows = width // planes
    height = 2 * rows
    low = jnp.bfloat16

    def body(where_ref, two_a, two_b, cot_a, cot_b, up, down, *rest):
        outs, (up_sum, down_sum) = rest[:planes], rest[planes:]
        step = pl.program_id(0)

        def run(two, cot):
            active, slope = gelu_pair(dot(two, up[...], 1, 0))
            d_hidden = (dot(cot, down[...], 1, 1) * slope).astype(low)
            up_term = dot(two, d_hidden, 0, 0)
            down_term = dot(active.astype(low), cot, 0, 0)

            @pl.when(step == 0)
            def _():
                up_sum[...] = up_term
                down_sum[:hidden] = down_term[:, :hidden]
                down_sum[hidden:] = down_term[:, hidden:]

            @pl.when(step > 0)
            def _():
                up_sum[...] += up_term
                down_sum[:hidden] += down_term[:, :hidden]
                down_sum[hidden:] += down_term[:, hidden:]

        @pl.when(step < pieces // 2)
        def _():
            run(two_a[...].reshape(2 * tokens, width), cot_a[...].reshape(2 * tokens, width))

        @pl.when(step >= pieces // 2)
        def _():
            run(two_b[...].reshape(2 * tokens, width), cot_b[...].reshape(2 * tokens, width))

        @pl.when(step == pieces - 1)
        def _():
            for index, out in enumerate(outs):
                plane = lax.rem(where_ref[1] + index, planes)
                rows_of = pl.ds(pl.multiple_of(plane * rows, rows), rows)
                out[:rows] = up_sum[rows_of, :].astype(low)
                out[rows:] = down_sum[rows_of, :].astype(low)

    near = pl.BlockSpec(
        (2, tokens, width), lambda i, where: (jnp.minimum(i, pieces // 2 - 1), 0, 0)
    )
    far = pl.BlockSpec((2, tokens, width), lambda i, where: (jnp.maximum(i - pieces // 2, 0), 0, 0))
    return pl.pallas_call(
        body,
        grid_spec=pltpu.PrefetchScalarGridSpec(
            num_scalar_prefetch=1,
            grid=(pieces,),
            in_specs=[
                near, far, near, far,
                pl.BlockSpec((width, hidden), lambda i, where: (0, where[0])),
                pl.BlockSpec((hidden, width), lambda i, where: (where[0], 0)),
            ],
            out_specs=[whole((height, hidden))] * planes,
            scratch_shapes=[
                pltpu.VMEM((width, hidden), jnp.float32),
                pltpu.VMEM((width, hidden), jnp.float32),
            ],
        ),
        out_shape=[jax.ShapeDtypeStruct((height, hidden), low)] * planes,
        compiler_params=LIMIT,
        cost_estimate=busy(12),
        name="hidden_gradients",
    )(where, two_mine, two_other, cot_mine, cot_other, w_up, w_down)


def place_hidden(where, pieces, placed, w_up, gain, planes):
    spots, height, hidden = pieces.shape
    width = w_up.shape[0]
    rows = width // planes
    f32 = jnp.float32
    second = placed is not None

    def body(where_ref, ref, up_ref, gain_ref, *rest):
        gain_before = rest[2] if second else None
        up_out, down_out, gain_out, low, sums = rest[3:] if second else rest
        step = pl.program_id(0)
        for index in range(planes):
            plane = lax.rem(where_ref[1, 0] + planes - index, planes)
            rows_of = pl.ds(pl.multiple_of(plane * rows, rows), rows)
            first = 2 * rows * index
            up_out[rows_of, :] = ref[0, first : first + rows].astype(f32)
            low[rows_of, :] = ref[0, first + rows : first + 2 * rows].astype(f32)
        down_out[:, :hidden] = low[:hidden]
        down_out[:, hidden:] = low[hidden:]
        terms = jnp.sum(up_out[...] * up_ref[...].astype(f32), axis=1, keepdims=True)

        @pl.when(step == 0)
        def _():
            sums[...] = terms

        @pl.when(step > 0)
        def _():
            sums[...] += terms

        @pl.when(step == spots - 1)
        def _():
            row = as_row(sums[...])
            gain_out[...] = (row + gain_before[...]) / gain_ref[...] if second else row

    unused = [pl.BlockSpec(memory_space=pl.ANY)] * 2 + [whole((1, width))]
    return pl.pallas_call(
        body,
        grid_spec=pltpu.PrefetchScalarGridSpec(
            num_scalar_prefetch=1,
            grid=(spots,),
            in_specs=[
                pl.BlockSpec((1, height, hidden), lambda i, where: (i, 0, 0)),
                pl.BlockSpec((width, hidden), lambda i, where: (0, where[0, i])),
                whole((1, width)),
            ]
            + (unused if second else []),
            out_specs=[
                pl.BlockSpec((width, hidden), lambda i, where: (0, where[0, i])),
                pl.BlockSpec((hidden, width), lambda i, where: (where[0, i], 0)),
                whole((1, width)),
            ],
            scratch_shapes=[pltpu.VMEM((width, hidden), f32), pltpu.VMEM((width, 1), f32)],
        ),
        out_shape=[
            jax.ShapeDtypeStruct(w_up.shape, f32),
            jax.ShapeDtypeStruct(w_up.shape[::-1], f32),
            jax.ShapeDtypeStruct((1, width), f32),
        ],
        input_output_aliases={4: 0, 5: 1} if second else {},
        compiler_params=LIMIT,
        cost_estimate=busy(8),
        name="place_hidden",
    )(where, pieces, w_up, gain[None, :], *(placed or []))


def place_heads(pieces, weights, gain, owners):
    _, height, half = pieces.shape
    width = 2 * half
    quarter = width // 4
    size = height - 3 * HEAD_DIM
    f32 = jnp.float32

    def body(ref, wq, wk, wv, gain_ref, dq, dk, dv, out, gain_out):
        for spot in range(4):
            for core in range(2):
                first = (spot if core else spot % 2 * 2 + spot // 2) * quarter
                columns = slice(core * half, (core + 1) * half)
                for plane in range(quarter // size):
                    piece = ref[(plane * 4 + spot) * 2 + core, 3 * HEAD_DIM :]
                    out[first + plane * size : first + (plane + 1) * size, columns] = piece.astype(f32)
        for side in range(2):
            rows_of = slice(side * half, (side + 1) * half)
            terms = jnp.zeros((half, 1), f32)
            for kind, (weight, out) in enumerate(((wq, dq), (wk, dk), (wv, dv))):
                rows = slice(kind * HEAD_DIM, (kind + 1) * HEAD_DIM)
                flat = jnp.concatenate([ref[owner, rows] for owner in owners[side]], axis=0)
                grad = flat.T.astype(f32)
                out[rows_of] = grad
                terms += jnp.sum(grad * weight[rows_of].astype(f32), axis=1, keepdims=True)
            gain_out[:, rows_of] = as_row(terms) / gain_ref[:, rows_of]

    return pl.pallas_call(
        body,
        out_shape=[jax.ShapeDtypeStruct((width, width), f32)] * 4
        + [jax.ShapeDtypeStruct((1, width), f32)],
        in_specs=[VMEM] * 5,
        out_specs=[VMEM] * 5,
        compiler_params=LIMIT,
        cost_estimate=busy(7),
        name="place_heads",
    )(pieces, *weights, gain[None, :])


def input_gradient(grads, weights, block_input, gain, d_middle, owners):
    streams, rows, width = block_input.shape

    def body(d_ref, wq, wk, wv, x_ref, gain_ref, d_middle_ref, out):
        for stream in range(streams):
            d_normed = jnp.zeros((rows, width), jnp.float32)
            for kind, weight in enumerate((wq, wk, wv)):
                rows_of = slice(kind * HEAD_DIM, (kind + 1) * HEAD_DIM)
                flat = jnp.concatenate([d_ref[owner, rows_of] for owner in owners[stream]], axis=0)
                d_normed += dot(flat.T, weight[...], 1, 1)
            unit, root = normalize(x_ref[stream].astype(jnp.float32))
            d_values = normalize_back(d_normed, unit, root, gain_ref[...])
            out[stream] = d_middle_ref[stream * rows : (stream + 1) * rows] + d_values

    return pl.pallas_call(
        body,
        out_shape=jax.ShapeDtypeStruct(block_input.shape, jnp.float32),
        in_specs=[VMEM] * 7,
        out_specs=VMEM,
        compiler_params=LIMIT,
        cost_estimate=busy(6),
        name="input_gradient",
    )(grads, *weights, block_input, gain[None, :], d_middle)


def wide(ref, frame, spaces, first, last, count=1):
    return jnp.concatenate(
        [ref[frame * spaces + j, first:last, :] for j in range(spaces * count)], axis=1
    )


def attend(lo, packed, frames):
    devices, _, rows = packed.shape
    spaces = devices // frames
    per_frame = rows * spaces
    dim = HEAD_DIM

    def body(lo_ref, r_ref, o_ref, low_ref, lse_ref, kv, top, total, summed):
        def turn_keys(device, _):
            kv[pl.ds(pl.multiple_of(device * rows, rows), rows), :] = r_ref[device, dim:, :].T
            return 0

        lax.fori_loop(0, devices, turn_keys, 0, unroll=4)

        def group(queries, _):
            first = queries * CLIP
            query = [wide(r_ref, first + i, spaces, 0, dim) for i in range(CLIP)]

            def update(i, keys, count, fresh):
                base = pl.multiple_of(keys * CLIP * per_frame, per_frame)
                scores = dot(kv[pl.ds(base, count * per_frame), :dim], query[i], 1, 0)
                new_top = jnp.max(scores, axis=0, keepdims=True)
                if not fresh:
                    old_top = top[i]
                    new_top = jnp.maximum(old_top, new_top)
                weights = jnp.exp(scores - new_top)
                new_total = jnp.sum(weights, axis=0, keepdims=True)
                values = wide(r_ref, keys * CLIP, spaces, 2 * dim, 3 * dim, count)
                new_sum = dot(values, weights.astype(jnp.bfloat16), 1, 0)
                if not fresh:
                    factor = jnp.exp(old_top - new_top)
                    new_total += total[i] * factor
                    new_sum += summed[i] * factor
                top[i] = new_top
                total[i] = new_total
                summed[i] = new_sum

            for i in range(CLIP):
                update(i, queries, i + 1, True)

            def earlier(keys, _):
                for i in range(CLIP):
                    update(i, keys, CLIP, False)
                return 0

            lax.fori_loop(lo_ref[first] // CLIP, queries, earlier, 0)
            for i in range(CLIP):
                out = summed[i] / total[i]
                for j in range(spaces):
                    piece = out[:, j * rows : (j + 1) * rows]
                    o_ref[(first + i) * spaces + j] = piece
                    low_ref[(first + i) * spaces + j] = piece.astype(jnp.bfloat16)
                lse_ref[first + i] = top[i] + jnp.log(total[i])
            return 0

        lax.fori_loop(0, frames // CLIP, group, 0)

    f32 = jnp.float32
    return pl.pallas_call(
        body,
        out_shape=(
            jax.ShapeDtypeStruct((devices, dim, rows), f32),
            jax.ShapeDtypeStruct((devices, dim, rows), jnp.bfloat16),
            jax.ShapeDtypeStruct((frames, 1, per_frame), f32),
            jax.ShapeDtypeStruct((devices * rows, 2 * dim), jnp.bfloat16),
        ),
        in_specs=[SMEM, VMEM],
        out_specs=(VMEM,) * 4,
        scratch_shapes=[
            pltpu.VMEM((CLIP, 1, per_frame), f32),
            pltpu.VMEM((CLIP, 1, per_frame), f32),
            pltpu.VMEM((CLIP, dim, per_frame), f32),
        ],
        compiler_params=LIMIT,
        cost_estimate=busy(28),
        name="attend",
    )(lo, packed)


def attend_back_ready(packed, d_own, out, frames):
    devices, _, rows = packed.shape
    spaces = devices // frames
    dim = HEAD_DIM

    def body(r_ref, d_ref, o_ref, qd, delta):
        def turn_frame(frame, _):
            for j in range(spaces):
                device = frame * spaces + j
                both = jnp.concatenate([r_ref[device, :dim, :], d_ref[device]], axis=0)
                qd[pl.ds(pl.multiple_of(device * rows, rows), rows), :] = both.T
                delta[frame, :, j * rows : (j + 1) * rows] = jnp.sum(
                    d_ref[device].astype(jnp.float32) * o_ref[device], axis=0, keepdims=True
                )
            return 0

        lax.fori_loop(0, frames, turn_frame, 0, unroll=2)

    return pl.pallas_call(
        body,
        out_shape=(
            jax.ShapeDtypeStruct((devices * rows, 2 * dim), jnp.bfloat16),
            jax.ShapeDtypeStruct((frames, 1, spaces * rows), jnp.float32),
        ),
        in_specs=[VMEM] * 3,
        out_specs=(VMEM, VMEM),
        compiler_params=LIMIT,
        cost_estimate=busy(4),
        name="attend_back_ready",
    )(packed, d_own, out)


def attend_back(hi, packed, d_own, lse, delta, kv, qd, tables, d_query, rest, frames, start, stop):
    devices, _, rows = packed.shape
    spaces = devices // frames
    per_frame = rows * spaces
    dim = HEAD_DIM
    last = stop * CLIP == frames
    f32 = jnp.float32
    shift = dim if last else 0
    base = 0 if last else start * CLIP * spaces

    def body(hi_ref, r_ref, d_ref, lse_ref, delta_ref, kv_ref, qd_ref, table_ref, *rest):
        if last:
            before, piece, where_ref, near_ref, far_ref, out, keep, give, acc, left, d_query_ref, product, near, far, sems = rest
        else:
            out, d_query_ref, acc, left = rest

        def begin(frame, _):
            d_query_ref[frame] = jnp.zeros((dim, per_frame), f32)
            return 0

        def fetch(pair, slot):
            return [
                pltpu.make_async_copy(source.at[pl.ds(2 * pair, 2)], target.at[slot], sems.at[slot, i])
                for i, (source, target) in enumerate(((near_ref, near), (far_ref, far)))
            ]

        if last:
            for copy in fetch(0, 0):
                copy.start()
            pltpu.sync_copy(before, d_query_ref)
        else:
            lax.fori_loop(0, frames, begin, 0)
        if last:
            out[: piece.shape[0], dim:, :] = piece[...]
        first_half = lax.broadcasted_iota(jnp.int32, (per_frame, 2 * dim), 1) < dim

        def group(keys, _):
            first = keys * CLIP
            for i in range(CLIP):
                rows_of = pl.ds(pl.multiple_of((first + i) * per_frame, per_frame), per_frame)
                both = kv_ref[rows_of, :]
                zero = jnp.zeros_like(both)
                left[i, :per_frame] = jnp.where(first_half, both, zero)
                left[i, per_frame:] = jnp.where(first_half, zero, both)

            def block(i, frame, count, fresh):
                own = [d_ref[frame * spaces + j] for j in range(spaces * count)]
                right = jnp.concatenate(
                    [wide(r_ref, frame, spaces, 0, dim, count), jnp.concatenate(own, axis=1)],
                    axis=0,
                )
                both = dot(left[i], right, 1, 0)
                row = lambda ref: jnp.concatenate([ref[frame + j] for j in range(count)], axis=1)
                weights = jnp.exp(both[:per_frame] - row(lse_ref))
                d_scores = (weights * (both[per_frame:] - row(delta_ref))).astype(jnp.bfloat16)
                pair = jnp.concatenate([weights.astype(jnp.bfloat16), d_scores], axis=0)
                tokens = pl.ds(pl.multiple_of(frame * per_frame, per_frame), count * per_frame)
                term = dot(pair, qd_ref[tokens, :], 1, 0)
                if fresh:
                    acc[i] = term
                else:
                    acc[i] += term
                key_rows = wide(r_ref, first + i, spaces, dim, 2 * dim)
                change = dot(key_rows, d_scores, 1, 0)
                for j in range(count):
                    d_query_ref[frame + j] += change[:, j * per_frame : (j + 1) * per_frame]

            for i in range(CLIP):
                block(i, first + i, CLIP - i, True)

            def later(queries, _):
                for i in range(CLIP):
                    block(i, queries * CLIP, CLIP, False)
                return 0

            lax.fori_loop(keys + 1, hi_ref[first] // CLIP, later, 0)
            for i in range(CLIP):
                total = acc[i]
                d_key = total[per_frame:].T[:dim]
                d_key = turned(d_key, table_ref[first + i, 0], table_ref[first + i, 1], -1.0)
                d_key = d_key.astype(jnp.bfloat16)
                d_value = total[:per_frame].T[dim:].astype(jnp.bfloat16)
                for j in range(spaces):
                    device = (first + i) * spaces + j - base
                    columns = slice(j * rows, (j + 1) * rows)
                    out[device, shift : shift + dim, :] = d_key[:, columns]
                    out[device, shift + dim : shift + 2 * dim, :] = d_value[:, columns]
            return 0

        lax.fori_loop(start, stop, group, 0)
        if last:

            def finish(frame, _):
                whole_query = d_query_ref[frame] * (1.0 / math.sqrt(dim))
                whole_query = turned(whole_query, table_ref[frame, 0], table_ref[frame, 1], -1.0)
                whole_query = whole_query.astype(jnp.bfloat16)
                for j in range(spaces):
                    out[frame * spaces + j, :dim, :] = whole_query[:, j * rows : (j + 1) * rows]
                return 0

            lax.fori_loop(0, frames, finish, 0)

            core = where_ref[0]
            product[...] = jnp.zeros_like(product)

            def multiply(pair, _):
                slot = lax.rem(pair, 2)

                @pl.when(pair + 1 < frames // 2)
                def _():
                    for copy in fetch(pair + 1, 1 - slot):
                        copy.start()

                for copy in fetch(pair, slot):
                    copy.wait()
                lefts, rights = [], []
                for index in range(2):
                    frame = 2 * pair + index
                    lefts += [out[spaces * frame + core], out[spaces * frame + 1 - core]]
                    rights += [near[slot, index], far[slot, index]]
                product[...] += dot(
                    jnp.concatenate(lefts, axis=1), jnp.concatenate(rights, axis=0), 1, 0
                )
                return 0

            lax.fori_loop(0, frames // 2, multiply, 0)
            half = product.shape[1] // 2
            first = where_ref[1] == 0
            keep[...] = jnp.where(first, product[:, :half], product[:, half:])
            give[...] = jnp.where(first, product[:, half:], product[:, :half]).astype(jnp.bfloat16)

    inputs = [hi, packed, d_own, lse, delta, kv, qd, tables]
    in_specs = [SMEM] + [VMEM] * 7
    query_sum = jax.ShapeDtypeStruct((frames, dim, per_frame), f32)
    scratch = [
        pltpu.VMEM((CLIP, 2 * per_frame, 2 * dim), f32),
        pltpu.VMEM((CLIP, 2 * per_frame, 2 * dim), jnp.bfloat16),
    ]
    if last:
        width = rest[2].shape[2]
        inputs += [d_query, *rest]
        in_specs += [ANY, VMEM, SMEM, ANY, ANY]
        out_shape = (
            jax.ShapeDtypeStruct((devices, 3 * dim, rows), jnp.bfloat16),
            jax.ShapeDtypeStruct((3 * dim, width // 2), f32),
            jax.ShapeDtypeStruct((3 * dim, width // 2), jnp.bfloat16),
        )
        scratch += [
            pltpu.VMEM((frames, dim, per_frame), f32),
            pltpu.VMEM((3 * dim, width), f32),
            pltpu.VMEM((2, 2, rows, width), jnp.bfloat16),
            pltpu.VMEM((2, 2, rows, width), jnp.bfloat16),
            pltpu.SemaphoreType.DMA((2, 2)),
        ]
    else:
        shape = ((stop - start) * CLIP * spaces, 2 * dim, rows)
        out_shape = (jax.ShapeDtypeStruct(shape, jnp.bfloat16), query_sum)
    return pl.pallas_call(
        body,
        out_shape=out_shape,
        in_specs=in_specs,
        out_specs=(VMEM,) * len(out_shape),
        scratch_shapes=scratch,
        compiler_params=LIMIT,
        cost_estimate=busy(20),
        name="attend_back",
    )(*inputs)


def after(value, *others):
    return lax.optimization_barrier((value, *others))[0]


class Ring:
    def __init__(self):
        self.frames = lax.axis_size("frame")
        self.spaces = lax.axis_size("space")
        self.planes = self.frames // 4
        self.frame = lax.axis_index("frame")
        self.core = lax.axis_index("space")
        self.plane = self.frame // 4
        self.spot = self.frame % 4
        bits = (self.frame % 2, (self.frame // 2) % 2)
        self.first_bit = jnp.where(self.core == 0, bits[0], bits[1])
        self.second_bit = jnp.where(self.core == 0, bits[1], bits[0])

    def send(self, value, target):
        moves = []
        for frame in range(self.frames):
            for core in range(self.spaces):
                to_frame, to_core = target(frame, core)
                moves.append((frame * self.spaces + core, to_frame * self.spaces + to_core))
        return lax.ppermute(value, ("frame", "space"), moves)

    def first(self, value):
        return self.send(value, lambda frame, core: (frame ^ (1 if core == 0 else 2), core))

    def second(self, value):
        return self.send(value, lambda frame, core: (frame ^ (2 if core == 0 else 1), core))

    def across(self, value):
        return self.send(value, lambda frame, core: (frame, 1 - core))

    def up(self, value, step):
        size = self.frames
        return self.send(value, lambda frame, core: ((frame + 4 * step) % size, core))

    def send_planes(self, pieces):
        return [self.up(piece, step) for step, piece in enumerate(pieces[1:], 1)]

    def plane_part(self, value):
        groups = [list(range(spot, self.frames, 4)) for spot in range(4)]
        if value.shape[0] % (16 * self.planes):
            return lax.psum(value, "frame", axis_index_groups=groups)
        return lax.psum_scatter(
            value, "frame", scatter_dimension=0, axis_index_groups=groups, tiled=True
        )

    def add_planes(self, own, arrived):
        total = own.astype(jnp.float32)
        for piece in arrived:
            total = total + piece.astype(jnp.float32)
        return total.astype(jnp.bfloat16)

    def spread_planes(self, value, count):
        return [self.up(value, step) for step in range(1, count)]

    def gather_spots(self):
        near = jnp.where(self.core == 0, 2, 1)
        own = jnp.stack([self.spot, self.spot ^ near, self.spot ^ (3 - near), self.spot ^ 3])
        other = jnp.stack([self.spot, self.spot ^ (3 - near), self.spot ^ near, self.spot ^ 3])
        cores = jnp.repeat(jnp.stack([self.core, 1 - self.core]), 4)
        return jnp.concatenate([own, other]), cores

    def gather(self, value, *others):
        pair = jnp.stack([value, after(self.second(value), *others)])
        return jnp.concatenate([pair, self.first(pair)], axis=0)

    def halves(self, value, bit):
        rows, columns = value.shape
        cut = value.reshape(2, rows // 2, columns)
        pick = lambda index: lax.dynamic_index_in_dim(cut, index, 0, keepdims=False)
        return pick(bit), pick(1 - bit).astype(jnp.bfloat16)


def frame_limits(clip_frames, frames):
    ends = jnp.cumsum(clip_frames, axis=1, dtype=jnp.int32)
    begins = ends - clip_frames
    index = jnp.arange(frames, dtype=jnp.int32)[None, :, None]
    inside = (index >= begins[:, None, :]) & (index < ends[:, None, :])
    pick = lambda table: jnp.sum(jnp.where(inside, table[:, None, :], 0), axis=2, dtype=jnp.int32)
    return pick(begins), pick(ends)


def local(
    block_input,
    norm1_gain,
    w_query,
    w_key,
    w_value,
    w_out,
    norm2_gain,
    w_up,
    w_down,
    clip_frames,
    cotangent,
):
    streams, rows, width = block_input.shape
    ring = Ring()
    frames, spaces, planes = ring.frames, ring.spaces, ring.planes
    devices = frames * spaces
    per_frame = rows * spaces
    tokens = streams * rows
    axes = ("frame", "space")
    low = jnp.bfloat16
    core = jnp.reshape(ring.core, (1,))
    spots, cores = ring.gather_spots()
    slots = 4 * spaces

    owners = head_owners(frames, spaces)
    w_projections = (w_query, w_key, w_value)
    side = ring.frame % 2

    def swap(value):
        return lax.all_to_all(value, axes, 0, 0, tiled=True)

    spot_of = jnp.stack([ring.frame, ring.core * rows])
    sent, normed = project(
        spot_of, clip_frames, block_input, norm1_gain, *w_projections, owners, devices, per_frame
    )
    packed = swap(sent)

    begin, end = frame_limits(after(clip_frames, sent), frames)
    frame_ids = jnp.arange(frames, dtype=jnp.int32)
    mine = ring.frame * spaces + ring.core
    idle = ~jnp.any(mine == jnp.asarray(owners))
    lo = jnp.where(idle, frame_ids, jnp.where(side == 0, begin[0], begin[1]))
    hi = jnp.where(idle, frame_ids, jnp.where(side == 0, end[0], end[1]))

    neighbour = lambda value: ring.send(value, lambda frame, core: (frame ^ 1, core))
    stream_near = neighbour(lax.dynamic_index_in_dim(normed, 1 - side, 0))
    stream_own = lax.dynamic_index_in_dim(normed, side, 0)
    stream_pair = jnp.where(
        side == 0,
        jnp.concatenate([stream_own, stream_near]),
        jnp.concatenate([stream_near, stream_own]),
    )
    same_side = [list(range(start, frames, 2)) for start in range(2)]
    stream_mine = lax.all_gather(
        stream_pair, "frame", axis=0, tiled=True, axis_index_groups=same_side
    )
    cot_flat = cotangent.reshape(tokens, width)
    cot_one = ring.second(cot_flat)
    out, out_low, lse, kv = attend(lo, after(packed, stream_pair), frames)
    cot_pair = jnp.stack([cot_flat, after(cot_one, out_low)])
    attended = swap(after(out_low, cot_pair))
    cot_far = ring.first(cot_pair)

    middle, two = attention_out(attended, block_input, w_out, norm2_gain, owners)
    chunk, skip = 512, 3
    cot_mine = jnp.concatenate([cot_pair, after(cot_far, middle)], axis=0)
    cot_other = ring.across(cot_mine)
    so_far = feed_first(two, cotangent, w_up, w_down, chunk, skip)
    two_pair = jnp.stack([two, ring.second(two)])
    so_far = after(so_far, two_pair, stream_mine)
    two_far = ring.first(two_pair)
    block_output, d_middle, d_sent, out_keep, out_give = feed_rest(
        core, so_far, attended, middle, two, cotangent, w_out, norm2_gain, w_up, w_down,
        chunk, skip, owners,
    )
    d_own = swap(d_sent)
    tables = rope_tables(after(lo, d_sent), frames, per_frame)
    two_mine = jnp.concatenate([two_pair, after(two_far, d_sent)], axis=0)
    two_other = ring.across(two_mine)
    out_other = ring.across(out_give)
    pieces = hidden_gradients(
        jnp.stack([ring.spot * spaces + ring.core, ring.plane]),
        two_mine, two_other, cot_mine, cot_other, w_up, w_down, slots, planes,
    )

    arrived = ring.send_planes(pieces)
    out_sum = out_keep + after(out_other, pieces[0]).astype(jnp.float32)
    out_keep, out_give = ring.halves(out_sum, ring.first_bit)
    out_other = ring.first(out_give)
    qd, delta = attend_back_ready(packed, d_own, out, frames)
    out_sum = out_keep + after(out_other, qd).astype(jnp.float32)
    out_keep, out_give = ring.halves(out_sum, ring.second_bit)
    out_sum = (out_keep + ring.second(out_give).astype(jnp.float32)).astype(low)
    delta = after(delta, out_sum)
    out_sum = ring.plane_part(out_sum)
    groups = frames // CLIP
    first_part, d_query = attend_back(
        hi, packed, d_own, lse, delta, kv, qd, tables, None, None, frames, 0, groups // 2
    )
    total = ring.add_planes(pieces[0], after(arrived, first_part))
    stream_other = ring.across(stream_mine)
    grads, keep, give = attend_back(
        hi, packed, d_own, lse, after(delta, total), kv, qd, tables, d_query,
        (first_part, jnp.stack([ring.core, side]), stream_mine, stream_other),
        frames, groups // 2, groups,
    )
    spread = after(ring.spread_planes(total, planes), keep)
    back = swap(after(grads, spread))
    heads_sum = (keep + neighbour(give).astype(jnp.float32)).astype(low)
    heads_all = lax.all_gather(jnp.concatenate([heads_sum, out_sum]), axes)
    hidden_mine = ring.gather(after(jnp.concatenate([total, *spread]), heads_sum), back)
    hidden_other = ring.across(hidden_mine)
    grad_input = input_gradient(back, w_projections, block_input, norm1_gain, d_middle, owners)
    unit_slots = spots * spaces + cores
    where = jnp.stack([unit_slots, jnp.broadcast_to(ring.plane, cores.shape)])
    placed = place_hidden(where[:, :4], hidden_mine, None, w_up, norm2_gain, planes)
    grad_up, grad_down, gain_two = place_hidden(
        where[:, 4:], after(hidden_other, placed[0], grad_input), placed, w_up, norm2_gain, planes
    )
    grad_query, grad_key, grad_value, grad_out, gain_one = place_heads(
        after(heads_all, grad_up), w_projections, norm1_gain, owners
    )
    return (
        block_output,
        grad_input,
        gain_one[0],
        grad_query,
        grad_key,
        grad_value,
        grad_out,
        gain_two[0],
        grad_up,
        grad_down,
    )


def solution(mesh):
    spread = P(None, ("frame", "space"), None)
    in_specs = (spread,) + (P(),) * 9 + (spread,)
    out_specs = (spread, spread) + (P(),) * 8
    return jax.shard_map(local, mesh=mesh, in_specs=in_specs, out_specs=out_specs, check_vma=False)
```

```python
import functools
import math

import jax
import jax.numpy as jnp
import numpy as np
from jax import lax
from jax.experimental import pallas as pl
from jax.experimental.pallas import tpu as pltpu
from jax.sharding import PartitionSpec as P

HEADS = 12
HEAD_DIM = 64
VMEM = pl.BlockSpec(memory_space=pltpu.VMEM)
ANY = pl.BlockSpec(memory_space=pl.ANY)
SMEM = pl.BlockSpec(memory_space=pltpu.SMEM)
LIMIT = pltpu.CompilerParams(vmem_limit_bytes=56 * 2**20)
FLOPS = 1.15e9


def busy(microseconds):
    return pl.CostEstimate(flops=int(microseconds * FLOPS), transcendentals=0, bytes_accessed=0)


CLIP = 4


def dot(left, right, left_dim, right_dim):
    return lax.dot_general(
        left,
        right,
        (((left_dim,), (right_dim,)), ((), ())),
        preferred_element_type=jnp.float32,
    )


def head_owners(frames, spaces):
    planes = frames // 4
    share = -(-HEADS // planes)
    return [
        [
            ((head // share) * 4 + (head % share) // spaces * 2 + stream) * spaces
            + (head % share) % spaces
            for head in range(HEADS)
        ]
        for stream in range(2)
    ]


def normalize(values):
    average = jnp.mean(values, axis=-1, keepdims=True)
    centred = values - average
    root = lax.rsqrt(jnp.mean(centred * centred, axis=-1, keepdims=True) + 1e-05)
    return centred * root, root


def normalize_back(d_scaled, unit, root, gain):
    d_unit = d_scaled * gain
    mean_one = jnp.mean(d_unit, axis=-1, keepdims=True)
    mean_two = jnp.mean(d_unit * unit, axis=-1, keepdims=True)
    return root * (d_unit - mean_one - unit * mean_two)


def frequencies(columns):
    half = HEAD_DIM // 2
    values = np.exp(np.arange(half) * (-2.0 * math.log(10000.0) / HEAD_DIM))
    return jnp.asarray(np.broadcast_to(values[:, None], (half, columns)), jnp.float32)


def turned(value, cosine, sine, sign):
    half = HEAD_DIM // 2
    first, second = value[:half], value[half:]
    return jnp.concatenate(
        [first * cosine - sign * second * sine, second * cosine + sign * first * sine], axis=0
    )


def project(place, clips, block_input, gain, w_query, w_key, w_value, owners, devices, per_frame):
    streams, rows, width = block_input.shape
    half = HEAD_DIM // 2
    low = jnp.bfloat16
    scale = 1.0 / math.sqrt(HEAD_DIM)
    owned = {device for row in owners for device in row}

    def body(place_ref, clips_ref, freq_ref, x_ref, gain_ref, wq, wk, wv, out, normed_out, table):
        frame, first_row = place_ref[0], place_ref[1]
        for stream in range(streams):
            begin = jnp.int32(0)
            running = jnp.int32(0)
            for clip in range(clips_ref.shape[1]):
                length = clips_ref[stream, clip]
                begin = jnp.where((frame >= running) & (frame < running + length), running, begin)
                running = running + length
            row = lax.broadcasted_iota(jnp.int32, (half, rows), 1)
            position = ((frame - begin) * per_frame + first_row + row).astype(jnp.float32)
            angles = position * freq_ref[...]
            table[0, stream] = jnp.cos(angles)
            table[1, stream] = jnp.sin(angles)
        values = x_ref[...].astype(jnp.float32).reshape(streams * rows, width)
        normed = (normalize(values)[0] * gain_ref[...][None, :]).astype(low)
        normed_out[...] = normed.reshape(streams, rows, width)
        for kind, weight in enumerate((wq, wk, wv)):
            product = dot(normed, weight[...], 1, 0).T
            for stream in range(streams):
                columns = slice(stream * rows, (stream + 1) * rows)
                for head in range(HEADS):
                    piece = product[head * HEAD_DIM : (head + 1) * HEAD_DIM, columns]
                    if kind < 2:
                        piece = turned(piece, table[0, stream], table[1, stream], 1.0)
                    if kind == 0:
                        piece = piece * scale
                    out[
                        owners[stream][head], kind * HEAD_DIM : (kind + 1) * HEAD_DIM, :
                    ] = piece.astype(low)
        for spare in range(devices):
            if spare not in owned:
                out[spare] = jnp.zeros((3 * HEAD_DIM, rows), low)

    return pl.pallas_call(
        body,
        out_shape=(
            jax.ShapeDtypeStruct((devices, 3 * HEAD_DIM, rows), low),
            jax.ShapeDtypeStruct((streams, rows, width), low),
        ),
        in_specs=[SMEM, SMEM] + [VMEM] * 6,
        out_specs=(VMEM, VMEM),
        scratch_shapes=[pltpu.VMEM((2, streams, half, rows), jnp.float32)],
        compiler_params=LIMIT,
        cost_estimate=busy(5),
        name="project",
    )(place, clips, frequencies(rows), block_input, gain, w_query, w_key, w_value)


def rope_tables(lo, frames, per_frame):
    half = HEAD_DIM // 2

    def body(lo_ref, freq_ref, out):
        def one(frame, _):
            row = lax.broadcasted_iota(jnp.int32, (half, per_frame), 1)
            position = ((frame - lo_ref[frame]) * per_frame + row).astype(jnp.float32)
            angles = position * freq_ref[...]
            out[frame, 0] = jnp.cos(angles)
            out[frame, 1] = jnp.sin(angles)
            return 0

        lax.fori_loop(0, frames, one, 0)

    return pl.pallas_call(
        body,
        out_shape=jax.ShapeDtypeStruct((frames, 2, half, per_frame), jnp.float32),
        in_specs=[SMEM, VMEM],
        out_specs=VMEM,
        compiler_params=LIMIT,
        cost_estimate=busy(4),
        name="rope_tables",
    )(lo, frequencies(per_frame))


GELU = math.sqrt(2.0 / math.pi)


def gelu_pair(value):
    square = value * value
    bent = jnp.tanh(GELU * value * (1.0 + 0.044715 * square))
    side = 0.5 * (1.0 + bent)
    slope = side + 0.5 * value * (1.0 - bent * bent) * (GELU * (1.0 + 3 * 0.044715 * square))
    return value * side, slope


def attention_out(attended, block_input, w_out, gain, owners):
    streams, rows, width = block_input.shape
    low = jnp.bfloat16

    def body(att, x_ref, wo, gain_ref, middle, two_ref):
        for stream in range(streams):
            rows_of = slice(stream * rows, (stream + 1) * rows)
            flat = jnp.concatenate([att[owner] for owner in owners[stream]], axis=0)
            values = x_ref[stream].astype(jnp.float32) + dot(flat.T, wo[...], 1, 0)
            middle[rows_of] = values
            two_ref[rows_of] = (normalize(values)[0] * gain_ref[...]).astype(low)

    return pl.pallas_call(
        body,
        out_shape=(
            jax.ShapeDtypeStruct((streams * rows, width), jnp.float32),
            jax.ShapeDtypeStruct((streams * rows, width), low),
        ),
        in_specs=[VMEM] * 4,
        out_specs=(VMEM, VMEM),
        compiler_params=LIMIT,
        cost_estimate=busy(3),
        name="attention_out",
    )(attended, block_input, w_out, gain[None, :])


def as_row(column):
    return jnp.broadcast_to(column, (column.shape[0], 128)).T[:1]


def whole(shape):
    return pl.BlockSpec(shape, lambda *indices: (0,) * len(shape))


def feed_first(two, cotangent, w_up, w_down, chunk, steps):
    tokens, width = two.shape
    low = jnp.bfloat16

    def body(two_ref, cot, up, down, result, d_two):
        cot_flat = cot[...].reshape(tokens, width)
        active, slope = gelu_pair(dot(two_ref[...], up[...], 1, 0))
        d_hidden = (dot(cot_flat, down[...], 1, 1) * slope).astype(low)
        forward = dot(active.astype(low), down[...], 1, 0)
        backward = dot(d_hidden, up[...], 1, 1)

        @pl.when(pl.program_id(0) == 0)
        def _():
            result[...] = forward
            d_two[...] = backward

        @pl.when(pl.program_id(0) > 0)
        def _():
            result[...] += forward
            d_two[...] += backward

    return pl.pallas_call(
        body,
        grid=(steps,),
        out_shape=(jax.ShapeDtypeStruct((tokens, width), jnp.float32),) * 2,
        in_specs=[
            whole(two.shape), whole(cotangent.shape),
            pl.BlockSpec((width, chunk), lambda i: (0, i)),
            pl.BlockSpec((chunk, width), lambda i: (i, 0)),
        ],
        out_specs=(whole((tokens, width)),) * 2,
        compiler_params=LIMIT,
        cost_estimate=busy(7),
        name="feed_first",
    )(two, cotangent, w_up, w_down)


def feed_rest(core, so_far, attended, middle, two, cotangent, w_out, gain, w_up, w_down, chunk, skip, owners):
    devices, head_width, rows = attended.shape
    streams, _, width = cotangent.shape
    tokens = streams * rows
    half = width // 2
    steps = w_up.shape[1] // chunk - skip
    low = jnp.bfloat16
    f32 = jnp.float32
    owned = {device for row in owners for device in row}

    def body(
        core_ref, first_result, first_two, att, middle, two_ref, cot, wo, gain_ref, up, down,
        result_ref, d_middle_ref, d_own, keep, give,
        result, d_two,
    ):
        step = pl.program_id(0)
        cot_flat = cot[...].reshape(tokens, width)
        active, slope = gelu_pair(dot(two_ref[...], up[...], 1, 0))
        d_hidden = (dot(cot_flat, down[...], 1, 1) * slope).astype(low)
        forward = dot(active.astype(low), down[...], 1, 0)
        backward = dot(d_hidden, up[...], 1, 1)

        @pl.when(step == 0)
        def _():
            result[...] = first_result[...] + forward
            d_two[...] = first_two[...] + backward

        @pl.when(step > 0)
        def _():
            result[...] += forward
            d_two[...] += backward

        @pl.when(step == steps - 1)
        def _():
            result_ref[...] = (middle[...] + result[...]).astype(low).reshape(streams, rows, width)
            unit, root = normalize(middle[...])
            d_middle = cot_flat.astype(f32) + normalize_back(
                d_two[...], unit, root, gain_ref[...]
            )
            d_middle_ref[...] = d_middle
            branch = d_middle.astype(low)
            d_att = dot(branch, wo[...], 1, 1).T.astype(low)
            total = jnp.zeros((width, width), f32)
            for stream in range(streams):
                rows_of = slice(stream * rows, (stream + 1) * rows)
                for head, owner in enumerate(owners[stream]):
                    d_own[owner] = d_att[head * HEAD_DIM : (head + 1) * HEAD_DIM, rows_of]
                flat = jnp.concatenate([att[owner] for owner in owners[stream]], axis=0)
                total += dot(flat, branch[rows_of], 1, 0)
            for spare in range(devices):
                if spare not in owned:
                    d_own[spare] = jnp.zeros((head_width, rows), low)
            first = core_ref[0] == 0
            keep[...] = jnp.where(first, total[:, :half], total[:, half:])
            give[...] = jnp.where(first, total[:, half:], total[:, :half]).astype(low)

    shapes = (
        ((streams, rows, width), low),
        ((tokens, width), f32),
        ((devices, head_width, rows), low),
        ((width, half), f32),
        ((width, half), low),
    )
    return pl.pallas_call(
        body,
        grid=(steps,),
        out_shape=tuple(jax.ShapeDtypeStruct(*entry) for entry in shapes),
        in_specs=[
            SMEM, whole((tokens, width)), whole((tokens, width)),
            whole(attended.shape), whole(middle.shape), whole(two.shape),
            whole(cotangent.shape), whole(w_out.shape), whole((1, width)),
            pl.BlockSpec((width, chunk), lambda i: (0, i + skip)),
            pl.BlockSpec((chunk, width), lambda i: (i + skip, 0)),
        ],
        out_specs=tuple(whole(shape) for shape, _ in shapes),
        scratch_shapes=[pltpu.VMEM((tokens, width), f32), pltpu.VMEM((tokens, width), f32)],
        compiler_params=LIMIT,
        cost_estimate=busy(10),
        name="feed_rest",
    )(core, *so_far, attended, middle, two, cotangent, w_out, gain[None, :], w_up, w_down)


def hidden_gradients(where, two, cot, w_up, w_down, slots, planes):
    _, tokens, width = two[0].shape
    count = len(two)
    hidden = w_up.shape[1] // slots
    rows = width // planes
    height = 2 * rows
    low = jnp.bfloat16

    def body(where_ref, *rest):
        two_refs, cot_refs, (up, down) = rest[:count], rest[count : 2 * count], rest[2 * count :][:2]
        rest = rest[2 * count + 2 :]
        outs, (up_sum, down_sum) = rest[:planes], rest[planes:]
        step = pl.program_id(0)

        def run(two_ref, cot_ref):
            two = two_ref[...].reshape(2 * tokens, width)
            cot = cot_ref[...].reshape(2 * tokens, width)
            active, slope = gelu_pair(dot(two, up[...], 1, 0))
            d_hidden = (dot(cot, down[...], 1, 1) * slope).astype(low)
            up_term = dot(two, d_hidden, 0, 0)
            down_term = dot(active.astype(low), cot, 0, 0)

            @pl.when(step == 0)
            def _():
                up_sum[...] = up_term
                down_sum[:hidden] = down_term[:, :hidden]
                down_sum[hidden:] = down_term[:, hidden:]

            @pl.when(step > 0)
            def _():
                up_sum[...] += up_term
                down_sum[:hidden] += down_term[:, :hidden]
                down_sum[hidden:] += down_term[:, hidden:]

        for index, refs in enumerate(zip(two_refs, cot_refs)):
            pl.when(step == index)(functools.partial(run, *refs))

        @pl.when(step == count - 1)
        def _():
            for index, out in enumerate(outs):
                plane = lax.rem(where_ref[1] + index, planes)
                rows_of = pl.ds(pl.multiple_of(plane * rows, rows), rows)
                out[:rows] = up_sum[rows_of, :].astype(low)
                out[rows:] = down_sum[rows_of, :].astype(low)

    return pl.pallas_call(
        body,
        grid_spec=pltpu.PrefetchScalarGridSpec(
            num_scalar_prefetch=1,
            grid=(count,),
            in_specs=[
                *[whole(two[0].shape)] * (2 * count),
                pl.BlockSpec((width, hidden), lambda i, where: (0, where[0])),
                pl.BlockSpec((hidden, width), lambda i, where: (where[0], 0)),
            ],
            out_specs=[whole((height, hidden))] * planes,
            scratch_shapes=[
                pltpu.VMEM((width, hidden), jnp.float32),
                pltpu.VMEM((width, hidden), jnp.float32),
            ],
        ),
        out_shape=[jax.ShapeDtypeStruct((height, hidden), low)] * planes,
        compiler_params=LIMIT,
        cost_estimate=busy(12),
        name="hidden_gradients",
    )(where, *two, *cot, w_up, w_down)


def place_hidden(where, pieces, placed, w_up, gain, planes, last):
    count = len(pieces)
    height, hidden = pieces[0].shape
    width = w_up.shape[0]
    rows = width // planes
    f32 = jnp.float32
    second = placed is not None

    def body(where_ref, *rest):
        refs, (up_ref, gain_ref), rest = rest[:count], rest[count : count + 2], rest[count + 2 :]
        gain_before = rest[2] if second else None
        up_out, down_out, gain_out, low, sums = rest[3:] if second else rest
        step = pl.program_id(0)

        def put(ref):
            for index in range(planes):
                plane = lax.rem(where_ref[1, 0] + planes - index, planes)
                rows_of = pl.ds(pl.multiple_of(plane * rows, rows), rows)
                first = 2 * rows * index
                up_out[rows_of, :] = ref[first : first + rows].astype(f32)
                low[rows_of, :] = ref[first + rows : first + 2 * rows].astype(f32)

        for index, ref in enumerate(refs):
            pl.when(step == index)(functools.partial(put, ref))
        down_out[:, :hidden] = low[:hidden]
        down_out[:, hidden:] = low[hidden:]
        terms = jnp.sum(up_out[...] * up_ref[...].astype(f32), axis=1, keepdims=True)

        @pl.when(step == 0)
        def _():
            sums[...] = terms

        @pl.when(step > 0)
        def _():
            sums[...] += terms

        @pl.when(step == count - 1)
        def _():
            row = as_row(sums[...])
            row = row + gain_before[...][None, :] if second else row
            gain_out[...] = (row / gain_ref[...])[0] if last else row[0]

    unused = [pl.BlockSpec(memory_space=pl.ANY)] * 2 + [whole((width,))]
    return pl.pallas_call(
        body,
        grid_spec=pltpu.PrefetchScalarGridSpec(
            num_scalar_prefetch=1,
            grid=(count,),
            in_specs=[whole((height, hidden))] * count
            + [
                pl.BlockSpec((width, hidden), lambda i, where: (0, where[0, i])),
                whole((1, width)),
            ]
            + (unused if second else []),
            out_specs=[
                pl.BlockSpec((width, hidden), lambda i, where: (0, where[0, i])),
                pl.BlockSpec((hidden, width), lambda i, where: (where[0, i], 0)),
                whole((width,)),
            ],
            scratch_shapes=[pltpu.VMEM((width, hidden), f32), pltpu.VMEM((width, 1), f32)],
        ),
        out_shape=[
            jax.ShapeDtypeStruct(w_up.shape, f32),
            jax.ShapeDtypeStruct(w_up.shape[::-1], f32),
            jax.ShapeDtypeStruct((width,), f32),
        ],
        input_output_aliases={count + 3: 0, count + 4: 1} if second else {},
        compiler_params=LIMIT,
        cost_estimate=busy(2 * count),
        name="place_hidden",
    )(where, *pieces, w_up, gain[None, :], *(placed or []))


def place_heads(core, mine, other, weights, gain, owners):
    _, height, half = mine.shape
    width = 2 * half
    quarter = width // 4
    size = height - 3 * HEAD_DIM
    f32 = jnp.float32

    def body(core_ref, mine_ref, other_ref, wq, wk, wv, gain_ref, dq, dk, dv, out, gain_out):
        def rows_of_device(device, rows):
            own = core_ref[0] == device % 2
            return jnp.where(own, mine_ref[device // 2, rows], other_ref[device // 2, rows])

        for spot in range(4):
            for core in range(2):
                first = (spot if core else spot % 2 * 2 + spot // 2) * quarter
                columns = slice(core * half, (core + 1) * half)
                for plane in range(quarter // size):
                    piece = rows_of_device((plane * 4 + spot) * 2 + core, slice(3 * HEAD_DIM, height))
                    out[first + plane * size : first + (plane + 1) * size, columns] = piece.astype(f32)
        for side in range(2):
            rows_of = slice(side * half, (side + 1) * half)
            terms = jnp.zeros((half, 1), f32)
            for kind, (weight, out) in enumerate(((wq, dq), (wk, dk), (wv, dv))):
                rows = slice(kind * HEAD_DIM, (kind + 1) * HEAD_DIM)
                flat = jnp.concatenate([rows_of_device(owner, rows) for owner in owners[side]], axis=0)
                grad = flat.T.astype(f32)
                out[rows_of] = grad
                terms += jnp.sum(grad * weight[rows_of].astype(f32), axis=1, keepdims=True)
            gain_out[rows_of] = (as_row(terms) / gain_ref[:, rows_of])[0]

    return pl.pallas_call(
        body,
        out_shape=[jax.ShapeDtypeStruct((width, width), f32)] * 4
        + [jax.ShapeDtypeStruct((width,), f32)],
        in_specs=[SMEM] + [VMEM] * 6,
        out_specs=[VMEM] * 5,
        compiler_params=LIMIT,
        cost_estimate=busy(7),
        name="place_heads",
    )(core, mine, other, *weights, gain[None, :])


def input_gradient(grads, weights, block_input, gain, d_middle, owners):
    streams, rows, width = block_input.shape

    def body(d_ref, wq, wk, wv, x_ref, gain_ref, d_middle_ref, out):
        for stream in range(streams):
            d_normed = jnp.zeros((rows, width), jnp.float32)
            for kind, weight in enumerate((wq, wk, wv)):
                rows_of = slice(kind * HEAD_DIM, (kind + 1) * HEAD_DIM)
                flat = jnp.concatenate([d_ref[owner, rows_of] for owner in owners[stream]], axis=0)
                d_normed += dot(flat.T, weight[...], 1, 1)
            unit, root = normalize(x_ref[stream].astype(jnp.float32))
            d_values = normalize_back(d_normed, unit, root, gain_ref[...])
            out[stream] = d_middle_ref[stream * rows : (stream + 1) * rows] + d_values

    return pl.pallas_call(
        body,
        out_shape=jax.ShapeDtypeStruct(block_input.shape, jnp.float32),
        in_specs=[VMEM] * 7,
        out_specs=VMEM,
        compiler_params=LIMIT,
        cost_estimate=busy(6),
        name="input_gradient",
    )(grads, *weights, block_input, gain[None, :], d_middle)


def wide(ref, frame, spaces, first, last, count=1):
    return jnp.concatenate(
        [ref[frame * spaces + j, first:last, :] for j in range(spaces * count)], axis=1
    )


def attend(lo, packed, frames):
    devices, _, rows = packed.shape
    spaces = devices // frames
    per_frame = rows * spaces
    dim = HEAD_DIM

    def body(lo_ref, r_ref, o_ref, low_ref, lse_ref, kv, top, total, summed):
        def turn_keys(device, _):
            kv[pl.ds(pl.multiple_of(device * rows, rows), rows), :] = r_ref[device, dim:, :].T
            return 0

        lax.fori_loop(0, devices, turn_keys, 0, unroll=4)

        def group(queries, _):
            first = queries * CLIP
            query = [wide(r_ref, first + i, spaces, 0, dim) for i in range(CLIP)]

            def update(i, keys, scores, fresh):
                fold = lambda op, value: op(value.reshape(-1, 8, per_frame), axis=0)
                new_top = fold(jnp.max, scores[0])
                for part in scores[1:]:
                    new_top = jnp.maximum(new_top, fold(jnp.max, part))
                new_top = jnp.max(new_top, axis=0, keepdims=True)
                if not fresh:
                    old_top = top[i]
                    new_top = jnp.maximum(old_top, new_top)
                new_total, new_sum = 0.0, 0.0
                for j, part in enumerate(scores):
                    weights = jnp.exp(part - new_top)
                    new_total += fold(jnp.sum, weights)
                    values = wide(r_ref, keys * CLIP + j, spaces, 2 * dim, 3 * dim)
                    new_sum += dot(values, weights.astype(jnp.bfloat16), 1, 0)
                new_total = jnp.sum(new_total, axis=0, keepdims=True)
                if not fresh:
                    factor = jnp.exp(old_top - new_top)
                    new_total += total[i] * factor
                    new_sum += summed[i] * factor
                top[i] = new_top
                total[i] = new_total
                summed[i] = new_sum

            def against(keys, counts, fresh):
                scores = []
                for i, count in enumerate(counts):
                    rows_of = [
                        pl.ds(pl.multiple_of((keys * CLIP + j) * per_frame, per_frame), per_frame)
                        for j in range(count)
                    ]
                    scores.append([dot(kv[part, :dim], query[i], 1, 0) for part in rows_of])
                for i in range(CLIP):
                    update(i, keys, scores[i], fresh)

            against(queries, range(1, CLIP + 1), True)

            def earlier(keys, _):
                against(keys, [CLIP] * CLIP, False)
                return 0

            lax.fori_loop(lo_ref[first] // CLIP, queries, earlier, 0)
            for i in range(CLIP):
                out = summed[i] / total[i]
                for j in range(spaces):
                    piece = out[:, j * rows : (j + 1) * rows]
                    o_ref[(first + i) * spaces + j] = piece
                    low_ref[(first + i) * spaces + j] = piece.astype(jnp.bfloat16)
                lse_ref[first + i] = top[i] + jnp.log(total[i])
            return 0

        lax.fori_loop(0, frames // CLIP, group, 0)

    f32 = jnp.float32
    return pl.pallas_call(
        body,
        out_shape=(
            jax.ShapeDtypeStruct((devices, dim, rows), f32),
            jax.ShapeDtypeStruct((devices, dim, rows), jnp.bfloat16),
            jax.ShapeDtypeStruct((frames, 1, per_frame), f32),
            jax.ShapeDtypeStruct((devices * rows, 2 * dim), jnp.bfloat16),
        ),
        in_specs=[SMEM, VMEM],
        out_specs=(VMEM,) * 4,
        scratch_shapes=[
            pltpu.VMEM((CLIP, 1, per_frame), f32),
            pltpu.VMEM((CLIP, 1, per_frame), f32),
            pltpu.VMEM((CLIP, dim, per_frame), f32),
        ],
        compiler_params=LIMIT,
        cost_estimate=busy(28),
        name="attend",
    )(lo, packed)


def attend_back(hi, packed, d_own, lse, kv, tables, rest, frames, start, stop):
    devices, _, rows = packed.shape
    spaces = devices // frames
    per_frame = rows * spaces
    dim = HEAD_DIM
    last = stop * CLIP == frames
    f32 = jnp.float32
    shift = dim if last else 0
    base = 0 if last else start * CLIP * spaces

    def body(hi_ref, r_ref, d_ref, lse_ref, kv_ref, table_ref, *rest):
        if last:
            delta_ref, qd_ref, before, piece, where_ref, near_ref, far_ref, *rest = rest
            out, keep, give, acc, left, d_query_ref, product, near, far, sems = rest
        else:
            o_ref, out, d_query_ref, qd_ref, delta_ref, acc, left = rest

        def begin(frame, _):
            d_query_ref[frame] = jnp.zeros((dim, per_frame), f32)
            for j in range(spaces):
                device = frame * spaces + j
                both = jnp.concatenate([r_ref[device, :dim, :], d_ref[device]], axis=0)
                qd_ref[pl.ds(pl.multiple_of(device * rows, rows), rows), :] = both.T
                delta_ref[frame, :, j * rows : (j + 1) * rows] = jnp.sum(
                    d_ref[device].astype(f32) * o_ref[device], axis=0, keepdims=True
                )
            return 0

        def fetch(pair, slot):
            return [
                pltpu.make_async_copy(source.at[pl.ds(2 * pair, 2)], target.at[slot], sems.at[slot, i])
                for i, (source, target) in enumerate(((near_ref, near), (far_ref, far)))
            ]

        if last:
            for copy in fetch(0, 0):
                copy.start()
            pltpu.sync_copy(before, d_query_ref)
        else:
            lax.fori_loop(0, frames, begin, 0, unroll=2)
        if last:
            out[: piece.shape[0], dim:, :] = piece[...]
        first_half = lax.broadcasted_iota(jnp.int32, (per_frame, 2 * dim), 1) < dim

        def group(keys, _):
            first = keys * CLIP
            for i in range(CLIP):
                rows_of = pl.ds(pl.multiple_of((first + i) * per_frame, per_frame), per_frame)
                both = kv_ref[rows_of, :]
                zero = jnp.zeros_like(both)
                left[i, :per_frame] = jnp.where(first_half, both, zero)
                left[i, per_frame:] = jnp.where(first_half, zero, both)

            def against(queries, lead, fresh):
                own = queries * CLIP
                d_scores = [[] for _ in range(CLIP)]
                right = []
                for n in range(CLIP):
                    d_rows = [d_ref[(own + n) * spaces + j] for j in range(spaces)]
                    both = [wide(r_ref, own + n, spaces, 0, dim), jnp.concatenate(d_rows, axis=1)]
                    right.append(jnp.concatenate(both, axis=0))
                for i in range(CLIP):
                    term = 0.0
                    taken = range(i if lead else 0, CLIP)
                    products = [dot(left[i], right[n], 1, 0) for n in taken]
                    pairs = []
                    for n, both in zip(taken, products):
                        weights = jnp.exp(both[:per_frame] - lse_ref[own + n])
                        change = weights * (both[per_frame:] - delta_ref[own + n])
                        d_scores[n].append(change.astype(jnp.bfloat16))
                        pairs.append(
                            jnp.concatenate([weights.astype(jnp.bfloat16), d_scores[n][-1]], axis=0)
                        )
                    for n, pair in zip(taken, pairs):
                        rows_of = pl.ds(pl.multiple_of((own + n) * per_frame, per_frame), per_frame)
                        term += dot(pair, qd_ref[rows_of, :], 1, 0)
                    if fresh:
                        acc[i] = term
                    else:
                        acc[i] += term
                for n in range(CLIP):
                    keys_of = [
                        wide(r_ref, first + i, spaces, dim, 2 * dim) for i in range(len(d_scores[n]))
                    ]
                    d_query_ref[own + n] += dot(
                        jnp.concatenate(keys_of, axis=1), jnp.concatenate(d_scores[n], axis=0), 1, 0
                    )

            against(keys, True, True)

            def later(queries, _):
                against(queries, False, False)
                return 0

            lax.fori_loop(keys + 1, hi_ref[first] // CLIP, later, 0)
            for i in range(CLIP):
                total = acc[i]
                d_key = total[per_frame:].T[:dim]
                d_key = turned(d_key, table_ref[first + i, 0], table_ref[first + i, 1], -1.0)
                d_key = d_key.astype(jnp.bfloat16)
                d_value = total[:per_frame].T[dim:].astype(jnp.bfloat16)
                for j in range(spaces):
                    device = (first + i) * spaces + j - base
                    columns = slice(j * rows, (j + 1) * rows)
                    out[device, shift : shift + dim, :] = d_key[:, columns]
                    out[device, shift + dim : shift + 2 * dim, :] = d_value[:, columns]
            return 0

        lax.fori_loop(start, stop, group, 0)
        if last:

            def finish(frame, _):
                whole_query = d_query_ref[frame] * (1.0 / math.sqrt(dim))
                whole_query = turned(whole_query, table_ref[frame, 0], table_ref[frame, 1], -1.0)
                whole_query = whole_query.astype(jnp.bfloat16)
                for j in range(spaces):
                    out[frame * spaces + j, :dim, :] = whole_query[:, j * rows : (j + 1) * rows]
                return 0

            lax.fori_loop(0, frames, finish, 0)

            core = where_ref[0]
            product[...] = jnp.zeros_like(product)

            def multiply(pair, _):
                slot = lax.rem(pair, 2)

                @pl.when(pair + 1 < frames // 2)
                def _():
                    for copy in fetch(pair + 1, 1 - slot):
                        copy.start()

                for copy in fetch(pair, slot):
                    copy.wait()
                lefts, rights = [], []
                for index in range(2):
                    frame = 2 * pair + index
                    lefts += [out[spaces * frame + core], out[spaces * frame + 1 - core]]
                    rights += [near[slot, index], far[slot, index]]
                product[...] += dot(
                    jnp.concatenate(lefts, axis=1), jnp.concatenate(rights, axis=0), 1, 0
                )
                return 0

            lax.fori_loop(0, frames // 2, multiply, 0)
            half = product.shape[1] // 2
            first = where_ref[1] == 0
            keep[...] = jnp.where(first, product[:, :half], product[:, half:])
            give[...] = jnp.where(first, product[:, half:], product[:, :half]).astype(jnp.bfloat16)

    inputs = [hi, packed, d_own, lse, kv, tables, *rest]
    in_specs = [SMEM] + [VMEM] * 5
    query_sum = jax.ShapeDtypeStruct((frames, dim, per_frame), f32)
    scratch = [
        pltpu.VMEM((CLIP, 2 * per_frame, 2 * dim), f32),
        pltpu.VMEM((CLIP, 2 * per_frame, 2 * dim), jnp.bfloat16),
    ]
    if last:
        width = rest[-1].shape[2]
        in_specs += [VMEM, VMEM, ANY, VMEM, SMEM, ANY, ANY]
        out_shape = (
            jax.ShapeDtypeStruct((devices, 3 * dim, rows), jnp.bfloat16),
            jax.ShapeDtypeStruct((3 * dim, width // 2), f32),
            jax.ShapeDtypeStruct((3 * dim, width // 2), jnp.bfloat16),
        )
        scratch += [
            pltpu.VMEM((frames, dim, per_frame), f32),
            pltpu.VMEM((3 * dim, width), f32),
            pltpu.VMEM((2, 2, rows, width), jnp.bfloat16),
            pltpu.VMEM((2, 2, rows, width), jnp.bfloat16),
            pltpu.SemaphoreType.DMA((2, 2)),
        ]
    else:
        shape = ((stop - start) * CLIP * spaces, 2 * dim, rows)
        in_specs += [VMEM]
        out_shape = (
            jax.ShapeDtypeStruct(shape, jnp.bfloat16),
            query_sum,
            jax.ShapeDtypeStruct((devices * rows, 2 * dim), jnp.bfloat16),
            jax.ShapeDtypeStruct((frames, 1, per_frame), f32),
        )
    return pl.pallas_call(
        body,
        out_shape=out_shape,
        in_specs=in_specs,
        out_specs=(VMEM,) * len(out_shape),
        scratch_shapes=scratch,
        compiler_params=LIMIT,
        cost_estimate=busy(20),
        name="attend_back",
    )(*inputs)


def after(value, *others):
    return lax.optimization_barrier((value, *others))[0]


class Ring:
    def __init__(self):
        self.frames = lax.axis_size("frame")
        self.spaces = lax.axis_size("space")
        self.planes = self.frames // 4
        self.frame = lax.axis_index("frame")
        self.core = lax.axis_index("space")
        self.plane = self.frame // 4
        self.spot = self.frame % 4
        bits = (self.frame % 2, (self.frame // 2) % 2)
        self.first_bit = jnp.where(self.core == 0, bits[0], bits[1])
        self.second_bit = jnp.where(self.core == 0, bits[1], bits[0])

    def send(self, value, target):
        moves = []
        for frame in range(self.frames):
            for core in range(self.spaces):
                to_frame, to_core = target(frame, core)
                moves.append((frame * self.spaces + core, to_frame * self.spaces + to_core))
        return lax.ppermute(value, ("frame", "space"), moves)

    def first(self, value):
        return self.send(value, lambda frame, core: (frame ^ (1 if core == 0 else 2), core))

    def second(self, value):
        return self.send(value, lambda frame, core: (frame ^ (2 if core == 0 else 1), core))

    def across(self, value):
        return self.send(value, lambda frame, core: (frame, 1 - core))

    def up(self, value, step):
        size = self.frames
        return self.send(value, lambda frame, core: ((frame + 4 * step) % size, core))

    def send_planes(self, pieces):
        return [self.up(piece, step) for step, piece in enumerate(pieces[1:], 1)]

    def plane_part(self, value):
        groups = [list(range(spot, self.frames, 4)) for spot in range(4)]
        if value.shape[0] % (16 * self.planes):
            return lax.psum(value, "frame", axis_index_groups=groups)
        return lax.psum_scatter(
            value, "frame", scatter_dimension=0, axis_index_groups=groups, tiled=True
        )

    def add_planes(self, own, arrived):
        total = own.astype(jnp.float32)
        for piece in arrived:
            total = total + piece.astype(jnp.float32)
        return total.astype(jnp.bfloat16)

    def spread_planes(self, value, count):
        return [self.up(value, step) for step in range(1, count)]

    def gather_spots(self):
        near = jnp.where(self.core == 0, 2, 1)
        own = jnp.stack([self.spot, self.spot ^ near, self.spot ^ (3 - near), self.spot ^ 3])
        other = jnp.stack([self.spot, self.spot ^ (3 - near), self.spot ^ near, self.spot ^ 3])
        cores = jnp.repeat(jnp.stack([self.core, 1 - self.core]), 4)
        return jnp.concatenate([own, other]), cores

    def halves(self, value, bit):
        rows, columns = value.shape
        cut = value.reshape(2, rows // 2, columns)
        pick = lambda index: lax.dynamic_index_in_dim(cut, index, 0, keepdims=False)
        return pick(bit), pick(1 - bit).astype(jnp.bfloat16)


def frame_limits(clip_frames, frames):
    ends = jnp.cumsum(clip_frames, axis=1, dtype=jnp.int32)
    begins = ends - clip_frames
    index = jnp.arange(frames, dtype=jnp.int32)[None, :, None]
    inside = (index >= begins[:, None, :]) & (index < ends[:, None, :])
    pick = lambda table: jnp.sum(jnp.where(inside, table[:, None, :], 0), axis=2, dtype=jnp.int32)
    return pick(begins), pick(ends)


def local(
    block_input,
    norm1_gain,
    w_query,
    w_key,
    w_value,
    w_out,
    norm2_gain,
    w_up,
    w_down,
    clip_frames,
    cotangent,
):
    streams, rows, width = block_input.shape
    ring = Ring()
    frames, spaces, planes = ring.frames, ring.spaces, ring.planes
    devices = frames * spaces
    per_frame = rows * spaces
    tokens = streams * rows
    axes = ("frame", "space")
    low = jnp.bfloat16
    core = jnp.reshape(ring.core, (1,))
    spots, cores = ring.gather_spots()
    slots = 4 * spaces

    owners = head_owners(frames, spaces)
    w_projections = (w_query, w_key, w_value)
    side = ring.frame % 2

    def swap(value):
        return lax.all_to_all(value, axes, 0, 0, tiled=True)

    spot_of = jnp.stack([ring.frame, ring.core * rows])
    sent, normed = project(
        spot_of, clip_frames, block_input, norm1_gain, *w_projections, owners, devices, per_frame
    )
    packed = swap(sent)

    begin, end = frame_limits(after(clip_frames, sent), frames)
    frame_ids = jnp.arange(frames, dtype=jnp.int32)
    mine = ring.frame * spaces + ring.core
    idle = ~jnp.any(mine == jnp.asarray(owners))
    lo = jnp.where(idle, frame_ids, jnp.where(side == 0, begin[0], begin[1]))
    hi = jnp.where(idle, frame_ids, jnp.where(side == 0, end[0], end[1]))

    neighbour = lambda value: ring.send(value, lambda frame, core: (frame ^ 1, core))
    stream_near = neighbour(lax.dynamic_index_in_dim(normed, 1 - side, 0))
    stream_own = lax.dynamic_index_in_dim(normed, side, 0)
    stream_pair = jnp.where(
        side == 0,
        jnp.concatenate([stream_own, stream_near]),
        jnp.concatenate([stream_near, stream_own]),
    )
    same_side = [list(range(start, frames, 2)) for start in range(2)]
    stream_mine = lax.all_gather(
        stream_pair, "frame", axis=0, tiled=True, axis_index_groups=same_side
    )
    cot_flat = cotangent.reshape(tokens, width)
    cot_one = ring.second(cot_flat)
    out, out_low, lse, kv = attend(lo, after(packed, stream_pair), frames)
    cot_pair = jnp.stack([cot_flat, after(cot_one, out_low)])
    attended = swap(after(out_low, cot_pair))
    tables = rope_tables(after(lo, out_low), frames, per_frame)
    attended = after(attended, tables)
    cot_far = ring.first(cot_pair)

    middle, two = attention_out(attended, block_input, w_out, norm2_gain, owners)
    chunk, skip = 512, 3
    cot_far = after(cot_far, middle)
    cot_plane = [cot_pair, cot_far, ring.across(cot_pair), ring.across(cot_far)]
    so_far = feed_first(two, cotangent, w_up, w_down, chunk, skip)
    two_pair = jnp.stack([two, ring.second(two)])
    so_far = after(so_far, two_pair, stream_mine)
    two_far = ring.first(two_pair)
    two_pair_other = ring.across(two_pair)
    block_output, d_middle, d_sent, out_keep, out_give = feed_rest(
        core, so_far, attended, middle, two, cotangent, w_out, norm2_gain, w_up, w_down,
        chunk, skip, owners,
    )
    d_own = swap(d_sent)
    two_far, two_pair_other = after((two_far, two_pair_other), d_sent)
    two_plane = [two_pair, two_far, two_pair_other, ring.across(two_far)]
    out_sum = out_keep + ring.across(out_give).astype(jnp.float32)
    out_keep, out_give = ring.halves(out_sum, ring.first_bit)
    out_other = ring.first(out_give)
    pieces = hidden_gradients(
        jnp.stack([ring.spot * spaces + ring.core, ring.plane]),
        after(two_plane, out_give), cot_plane, w_up, w_down, slots, planes,
    )

    arrived = ring.send_planes(pieces)
    out_sum = out_keep + after(out_other, pieces[0]).astype(jnp.float32)
    out_keep, out_give = ring.halves(out_sum, ring.second_bit)
    out_sum = (out_keep + ring.second(out_give).astype(jnp.float32)).astype(low)
    d_own = after(d_own, out_sum)
    out_sum = ring.plane_part(out_sum)
    groups = frames // CLIP
    first_part, d_query, qd, delta = attend_back(
        hi, packed, d_own, lse, kv, tables, (out,), frames, 0, groups // 2
    )
    total = ring.add_planes(pieces[0], after(arrived, first_part))
    stream_other = ring.across(stream_mine)
    grads, keep, give = attend_back(
        hi, packed, d_own, lse, kv, tables,
        (after(delta, total, out_sum), qd, d_query, first_part, jnp.stack([ring.core, side]),
         stream_mine, stream_other),
        frames, groups // 2, groups,
    )
    spread, grads, keep, give = lax.optimization_barrier(
        (ring.spread_planes(total, planes), grads, keep, give)
    )
    back = swap(grads)
    heads_sum = (keep + neighbour(give).astype(jnp.float32)).astype(low)
    heads_mine = lax.all_gather(jnp.concatenate([heads_sum, out_sum]), "frame")
    hidden = after(jnp.concatenate([total, *spread]), heads_sum)
    one, two = ring.second(hidden), ring.first(hidden)
    three = ring.first(after(one, back))
    near = [hidden, one, two]
    far = [ring.across(value) for value in near]
    grad_input = input_gradient(back, w_projections, block_input, norm1_gain, d_middle, owners)
    unit_slots = spots * spaces + cores
    where = jnp.stack([unit_slots, jnp.broadcast_to(ring.plane, cores.shape)])
    places = lambda *entries: jnp.stack([where[:, entry] for entry in entries], axis=1)
    placed = place_hidden(
        places(0, 1, 2, 4, 5, 6), after(near + far, grad_input), None, w_up, norm2_gain, planes, False
    )
    three = after(three, placed[0])
    three_other = ring.across(three)
    heads_other = ring.across(after(heads_mine, three))
    grad_query, grad_key, grad_value, grad_out, gain_one = place_heads(
        jnp.reshape(ring.core, (1,)), heads_mine, heads_other,
        w_projections, norm1_gain, owners,
    )
    grad_up, grad_down, gain_two = place_hidden(
        places(3, 7), [three, after(three_other, grad_query)], placed, w_up, norm2_gain, planes, True
    )
    return (
        block_output,
        grad_input,
        gain_one,
        grad_query,
        grad_key,
        grad_value,
        grad_out,
        gain_two,
        grad_up,
        grad_down,
    )


def solution(mesh):
    spread = P(None, ("frame", "space"), None)
    in_specs = (spread,) + (P(),) * 9 + (spread,)
    out_specs = (spread, spread) + (P(),) * 8
    return jax.shard_map(local, mesh=mesh, in_specs=in_specs, out_specs=out_specs, check_vma=False)
```

```python
import functools
import math

import jax
import jax.numpy as jnp
import numpy as np
from jax import lax
from jax.experimental import pallas as pl
from jax.experimental.pallas import tpu as pltpu
from jax.sharding import PartitionSpec as P

HEADS = 12
HEAD_DIM = 64
VMEM = pl.BlockSpec(memory_space=pltpu.VMEM)
ANY = pl.BlockSpec(memory_space=pl.ANY)
SMEM = pl.BlockSpec(memory_space=pltpu.SMEM)
LIMIT = pltpu.CompilerParams(vmem_limit_bytes=56 * 2**20)
FLOPS = 1.15e9


def busy(microseconds):
    return pl.CostEstimate(flops=int(microseconds * FLOPS), transcendentals=0, bytes_accessed=0)


CLIP = 4


def dot(left, right, left_dim, right_dim):
    return lax.dot_general(
        left,
        right,
        (((left_dim,), (right_dim,)), ((), ())),
        preferred_element_type=jnp.float32,
    )


def head_owners(frames, spaces):
    planes = frames // 4
    share = -(-HEADS // planes)
    return [
        [
            ((head // share) * 4 + (head % share) // spaces * 2 + stream) * spaces
            + (head % share) % spaces
            for head in range(HEADS)
        ]
        for stream in range(2)
    ]


def normalize(values):
    average = jnp.mean(values, axis=-1, keepdims=True)
    centred = values - average
    root = lax.rsqrt(jnp.mean(centred * centred, axis=-1, keepdims=True) + 1e-05)
    return centred * root, root


def normalize_back(d_scaled, unit, root, gain):
    d_unit = d_scaled * gain
    mean_one = jnp.mean(d_unit, axis=-1, keepdims=True)
    mean_two = jnp.mean(d_unit * unit, axis=-1, keepdims=True)
    return root * (d_unit - mean_one - unit * mean_two)


def frequencies(columns):
    half = HEAD_DIM // 2
    values = np.exp(np.arange(half) * (-2.0 * math.log(10000.0) / HEAD_DIM))
    return jnp.asarray(np.broadcast_to(values[:, None], (half, columns)), jnp.float32)


def turned(value, cosine, sine, sign):
    half = HEAD_DIM // 2
    first, second = value[:half], value[half:]
    return jnp.concatenate(
        [first * cosine - sign * second * sine, second * cosine + sign * first * sine], axis=0
    )


def project(place, clips, block_input, gain, w_query, w_key, w_value, owners, devices, per_frame):
    streams, rows, width = block_input.shape
    half = HEAD_DIM // 2
    low = jnp.bfloat16
    scale = 1.0 / math.sqrt(HEAD_DIM)
    owned = {device for row in owners for device in row}

    def body(place_ref, clips_ref, freq_ref, x_ref, gain_ref, wq, wk, wv, out, normed_out, table):
        frame, first_row = place_ref[0], place_ref[1]
        for stream in range(streams):
            begin = jnp.int32(0)
            running = jnp.int32(0)
            for clip in range(clips_ref.shape[1]):
                length = clips_ref[stream, clip]
                begin = jnp.where((frame >= running) & (frame < running + length), running, begin)
                running = running + length
            row = lax.broadcasted_iota(jnp.int32, (half, rows), 1)
            position = ((frame - begin) * per_frame + first_row + row).astype(jnp.float32)
            angles = position * freq_ref[...]
            table[0, stream] = jnp.cos(angles)
            table[1, stream] = jnp.sin(angles)
        values = x_ref[...].astype(jnp.float32).reshape(streams * rows, width)
        normed = (normalize(values)[0] * gain_ref[...][None, :]).astype(low)
        normed_out[...] = normed.reshape(streams, rows, width)
        for kind, weight in enumerate((wq, wk, wv)):
            product = dot(normed, weight[...], 1, 0).T
            for stream in range(streams):
                columns = slice(stream * rows, (stream + 1) * rows)
                for head in range(HEADS):
                    piece = product[head * HEAD_DIM : (head + 1) * HEAD_DIM, columns]
                    if kind < 2:
                        piece = turned(piece, table[0, stream], table[1, stream], 1.0)
                    if kind == 0:
                        piece = piece * scale
                    out[
                        owners[stream][head], kind * HEAD_DIM : (kind + 1) * HEAD_DIM, :
                    ] = piece.astype(low)
        for spare in range(devices):
            if spare not in owned:
                out[spare] = jnp.zeros((3 * HEAD_DIM, rows), low)

    return pl.pallas_call(
        body,
        out_shape=(
            jax.ShapeDtypeStruct((devices, 3 * HEAD_DIM, rows), low),
            jax.ShapeDtypeStruct((streams, rows, width), low),
        ),
        in_specs=[SMEM, SMEM] + [VMEM] * 6,
        out_specs=(VMEM, VMEM),
        scratch_shapes=[pltpu.VMEM((2, streams, half, rows), jnp.float32)],
        compiler_params=LIMIT,
        cost_estimate=busy(5),
        name="project",
    )(place, clips, frequencies(rows), block_input, gain, w_query, w_key, w_value)


def rope_tables(lo, frames, per_frame):
    half = HEAD_DIM // 2

    def body(lo_ref, freq_ref, out):
        def one(frame, _):
            row = lax.broadcasted_iota(jnp.int32, (half, per_frame), 1)
            position = ((frame - lo_ref[frame]) * per_frame + row).astype(jnp.float32)
            angles = position * freq_ref[...]
            out[frame, 0] = jnp.cos(angles)
            out[frame, 1] = jnp.sin(angles)
            return 0

        lax.fori_loop(0, frames, one, 0)

    return pl.pallas_call(
        body,
        out_shape=jax.ShapeDtypeStruct((frames, 2, half, per_frame), jnp.float32),
        in_specs=[SMEM, VMEM],
        out_specs=VMEM,
        compiler_params=LIMIT,
        cost_estimate=busy(4),
        name="rope_tables",
    )(lo, frequencies(per_frame))


GELU = math.sqrt(2.0 / math.pi)


def gelu_pair(value):
    square = value * value
    bent = jnp.tanh(GELU * value * (1.0 + 0.044715 * square))
    side = 0.5 * (1.0 + bent)
    slope = side + 0.5 * value * (1.0 - bent * bent) * (GELU * (1.0 + 3 * 0.044715 * square))
    return value * side, slope


def attention_out(attended, block_input, w_out, gain, owners):
    streams, rows, width = block_input.shape
    low = jnp.bfloat16

    def body(att, x_ref, wo, gain_ref, middle, two_ref):
        for stream in range(streams):
            rows_of = slice(stream * rows, (stream + 1) * rows)
            flat = jnp.concatenate([att[owner] for owner in owners[stream]], axis=0)
            values = x_ref[stream].astype(jnp.float32) + dot(flat.T, wo[...], 1, 0)
            middle[rows_of] = values
            two_ref[rows_of] = (normalize(values)[0] * gain_ref[...]).astype(low)

    return pl.pallas_call(
        body,
        out_shape=(
            jax.ShapeDtypeStruct((streams * rows, width), jnp.float32),
            jax.ShapeDtypeStruct((streams * rows, width), low),
        ),
        in_specs=[VMEM] * 4,
        out_specs=(VMEM, VMEM),
        compiler_params=LIMIT,
        cost_estimate=busy(3),
        name="attention_out",
    )(attended, block_input, w_out, gain[None, :])


def as_row(column):
    return jnp.broadcast_to(column, (column.shape[0], 128)).T[:1]


def whole(shape):
    return pl.BlockSpec(shape, lambda *indices: (0,) * len(shape))


def feed_first(two, cotangent, w_up, w_down, chunk, steps):
    tokens, width = two.shape
    low = jnp.bfloat16

    def body(two_ref, cot, up, down, result, d_two):
        cot_flat = cot[...].reshape(tokens, width)
        active, slope = gelu_pair(dot(two_ref[...], up[...], 1, 0))
        d_hidden = (dot(cot_flat, down[...], 1, 1) * slope).astype(low)
        forward = dot(active.astype(low), down[...], 1, 0)
        backward = dot(d_hidden, up[...], 1, 1)

        @pl.when(pl.program_id(0) == 0)
        def _():
            result[...] = forward
            d_two[...] = backward

        @pl.when(pl.program_id(0) > 0)
        def _():
            result[...] += forward
            d_two[...] += backward

    return pl.pallas_call(
        body,
        grid=(steps,),
        out_shape=(jax.ShapeDtypeStruct((tokens, width), jnp.float32),) * 2,
        in_specs=[
            whole(two.shape), whole(cotangent.shape),
            pl.BlockSpec((width, chunk), lambda i: (0, i)),
            pl.BlockSpec((chunk, width), lambda i: (i, 0)),
        ],
        out_specs=(whole((tokens, width)),) * 2,
        compiler_params=LIMIT,
        cost_estimate=busy(7),
        name="feed_first",
    )(two, cotangent, w_up, w_down)


def feed_rest(core, so_far, attended, middle, two, cotangent, w_out, gain, w_up, w_down, chunk, skip, owners):
    devices, head_width, rows = attended.shape
    streams, _, width = cotangent.shape
    tokens = streams * rows
    half = width // 2
    steps = w_up.shape[1] // chunk - skip
    low = jnp.bfloat16
    f32 = jnp.float32
    owned = {device for row in owners for device in row}

    def body(
        core_ref, first_result, first_two, att, middle, two_ref, cot, wo, gain_ref, up, down,
        result_ref, d_middle_ref, d_own, keep, give,
        result, d_two,
    ):
        step = pl.program_id(0)
        cot_flat = cot[...].reshape(tokens, width)
        active, slope = gelu_pair(dot(two_ref[...], up[...], 1, 0))
        d_hidden = (dot(cot_flat, down[...], 1, 1) * slope).astype(low)
        forward = dot(active.astype(low), down[...], 1, 0)
        backward = dot(d_hidden, up[...], 1, 1)

        @pl.when(step == 0)
        def _():
            result[...] = first_result[...] + forward
            d_two[...] = first_two[...] + backward

        @pl.when(step > 0)
        def _():
            result[...] += forward
            d_two[...] += backward

        @pl.when(step == steps - 1)
        def _():
            result_ref[...] = (middle[...] + result[...]).astype(low).reshape(streams, rows, width)
            unit, root = normalize(middle[...])
            d_middle = cot_flat.astype(f32) + normalize_back(
                d_two[...], unit, root, gain_ref[...]
            )
            d_middle_ref[...] = d_middle
            branch = d_middle.astype(low)
            d_att = dot(branch, wo[...], 1, 1).T.astype(low)
            total = jnp.zeros((width, width), f32)
            for stream in range(streams):
                rows_of = slice(stream * rows, (stream + 1) * rows)
                for head, owner in enumerate(owners[stream]):
                    d_own[owner] = d_att[head * HEAD_DIM : (head + 1) * HEAD_DIM, rows_of]
                flat = jnp.concatenate([att[owner] for owner in owners[stream]], axis=0)
                total += dot(flat, branch[rows_of], 1, 0)
            for spare in range(devices):
                if spare not in owned:
                    d_own[spare] = jnp.zeros((head_width, rows), low)
            first = core_ref[0] == 0
            keep[...] = jnp.where(first, total[:, :half], total[:, half:])
            give[...] = jnp.where(first, total[:, half:], total[:, :half]).astype(low)

    shapes = (
        ((streams, rows, width), low),
        ((tokens, width), f32),
        ((devices, head_width, rows), low),
        ((width, half), f32),
        ((width, half), low),
    )
    return pl.pallas_call(
        body,
        grid=(steps,),
        out_shape=tuple(jax.ShapeDtypeStruct(*entry) for entry in shapes),
        in_specs=[
            SMEM, whole((tokens, width)), whole((tokens, width)),
            whole(attended.shape), whole(middle.shape), whole(two.shape),
            whole(cotangent.shape), whole(w_out.shape), whole((1, width)),
            pl.BlockSpec((width, chunk), lambda i: (0, i + skip)),
            pl.BlockSpec((chunk, width), lambda i: (i + skip, 0)),
        ],
        out_specs=tuple(whole(shape) for shape, _ in shapes),
        scratch_shapes=[pltpu.VMEM((tokens, width), f32), pltpu.VMEM((tokens, width), f32)],
        compiler_params=LIMIT,
        cost_estimate=busy(10),
        name="feed_rest",
    )(core, *so_far, attended, middle, two, cotangent, w_out, gain[None, :], w_up, w_down)


def hidden_gradients(where, two, cot, w_up, w_down, slots, planes):
    _, tokens, width = two[0].shape
    count = len(two)
    hidden = w_up.shape[1] // slots
    rows = width // planes
    height = 2 * rows
    low = jnp.bfloat16

    def body(where_ref, *rest):
        two_refs, cot_refs, (up, down) = rest[:count], rest[count : 2 * count], rest[2 * count :][:2]
        rest = rest[2 * count + 2 :]
        outs, (up_sum, down_sum) = rest[:planes], rest[planes:]
        step = pl.program_id(0)

        def run(two_ref, cot_ref):
            two = two_ref[...].reshape(2 * tokens, width)
            cot = cot_ref[...].reshape(2 * tokens, width)
            active, slope = gelu_pair(dot(two, up[...], 1, 0))
            d_hidden = (dot(cot, down[...], 1, 1) * slope).astype(low)
            up_term = dot(two, d_hidden, 0, 0)
            down_term = dot(active.astype(low), cot, 0, 0)

            @pl.when(step == 0)
            def _():
                up_sum[...] = up_term
                down_sum[:hidden] = down_term[:, :hidden]
                down_sum[hidden:] = down_term[:, hidden:]

            @pl.when(step > 0)
            def _():
                up_sum[...] += up_term
                down_sum[:hidden] += down_term[:, :hidden]
                down_sum[hidden:] += down_term[:, hidden:]

        for index, refs in enumerate(zip(two_refs, cot_refs)):
            pl.when(step == index)(functools.partial(run, *refs))

        @pl.when(step == count - 1)
        def _():
            for index, out in enumerate(outs):
                plane = lax.rem(where_ref[1] + index, planes)
                rows_of = pl.ds(pl.multiple_of(plane * rows, rows), rows)
                out[:rows] = up_sum[rows_of, :].astype(low)
                out[rows:] = down_sum[rows_of, :].astype(low)

    return pl.pallas_call(
        body,
        grid_spec=pltpu.PrefetchScalarGridSpec(
            num_scalar_prefetch=1,
            grid=(count,),
            in_specs=[
                *[whole(two[0].shape)] * (2 * count),
                pl.BlockSpec((width, hidden), lambda i, where: (0, where[0])),
                pl.BlockSpec((hidden, width), lambda i, where: (where[0], 0)),
            ],
            out_specs=[whole((height, hidden))] * planes,
            scratch_shapes=[
                pltpu.VMEM((width, hidden), jnp.float32),
                pltpu.VMEM((width, hidden), jnp.float32),
            ],
        ),
        out_shape=[jax.ShapeDtypeStruct((height, hidden), low)] * planes,
        compiler_params=LIMIT,
        cost_estimate=busy(12),
        name="hidden_gradients",
    )(where, *two, *cot, w_up, w_down)


def place_hidden(where, pieces, placed, w_up, gain, planes, last):
    count = len(pieces)
    height, hidden = pieces[0].shape
    width = w_up.shape[0]
    rows = width // planes
    f32 = jnp.float32
    second = placed is not None

    def body(where_ref, *rest):
        refs, (up_ref, gain_ref), rest = rest[:count], rest[count : count + 2], rest[count + 2 :]
        gain_before = rest[2] if second else None
        up_out, down_out, gain_out, low, sums = rest[3:] if second else rest
        step = pl.program_id(0)

        def put(ref):
            for index in range(planes):
                plane = lax.rem(where_ref[1, 0] + planes - index, planes)
                rows_of = pl.ds(pl.multiple_of(plane * rows, rows), rows)
                first = 2 * rows * index
                up_out[rows_of, :] = ref[first : first + rows].astype(f32)
                low[rows_of, :] = ref[first + rows : first + 2 * rows].astype(f32)

        for index, ref in enumerate(refs):
            pl.when(step == index)(functools.partial(put, ref))
        down_out[:, :hidden] = low[:hidden]
        down_out[:, hidden:] = low[hidden:]
        terms = jnp.sum(up_out[...] * up_ref[...].astype(f32), axis=1, keepdims=True)

        @pl.when(step == 0)
        def _():
            sums[...] = terms

        @pl.when(step > 0)
        def _():
            sums[...] += terms

        @pl.when(step == count - 1)
        def _():
            row = as_row(sums[...])
            row = row + gain_before[...][None, :] if second else row
            gain_out[...] = (row / gain_ref[...])[0] if last else row[0]

    unused = [pl.BlockSpec(memory_space=pl.ANY)] * 2 + [whole((width,))]
    return pl.pallas_call(
        body,
        grid_spec=pltpu.PrefetchScalarGridSpec(
            num_scalar_prefetch=1,
            grid=(count,),
            in_specs=[whole((height, hidden))] * count
            + [
                pl.BlockSpec((width, hidden), lambda i, where: (0, where[0, i])),
                whole((1, width)),
            ]
            + (unused if second else []),
            out_specs=[
                pl.BlockSpec((width, hidden), lambda i, where: (0, where[0, i])),
                pl.BlockSpec((hidden, width), lambda i, where: (where[0, i], 0)),
                whole((width,)),
            ],
            scratch_shapes=[pltpu.VMEM((width, hidden), f32), pltpu.VMEM((width, 1), f32)],
        ),
        out_shape=[
            jax.ShapeDtypeStruct(w_up.shape, f32),
            jax.ShapeDtypeStruct(w_up.shape[::-1], f32),
            jax.ShapeDtypeStruct((width,), f32),
        ],
        input_output_aliases={count + 3: 0, count + 4: 1} if second else {},
        compiler_params=LIMIT,
        cost_estimate=busy(2 * count),
        name="place_hidden",
    )(where, *pieces, w_up, gain[None, :], *(placed or []))


def place_heads(core, mine, other, weights, gain, owners):
    _, height, half = mine.shape
    width = 2 * half
    quarter = width // 4
    size = height - 3 * HEAD_DIM
    f32 = jnp.float32

    def body(core_ref, mine_ref, other_ref, wq, wk, wv, gain_ref, dq, dk, dv, out, gain_out):
        def rows_of_device(device, rows):
            own = core_ref[0] == device % 2
            return jnp.where(own, mine_ref[device // 2, rows], other_ref[device // 2, rows])

        for spot in range(4):
            for core in range(2):
                first = (spot if core else spot % 2 * 2 + spot // 2) * quarter
                columns = slice(core * half, (core + 1) * half)
                for plane in range(quarter // size):
                    piece = rows_of_device((plane * 4 + spot) * 2 + core, slice(3 * HEAD_DIM, height))
                    out[first + plane * size : first + (plane + 1) * size, columns] = piece.astype(f32)
        for side in range(2):
            rows_of = slice(side * half, (side + 1) * half)
            terms = jnp.zeros((half, 1), f32)
            for kind, (weight, out) in enumerate(((wq, dq), (wk, dk), (wv, dv))):
                rows = slice(kind * HEAD_DIM, (kind + 1) * HEAD_DIM)
                flat = jnp.concatenate([rows_of_device(owner, rows) for owner in owners[side]], axis=0)
                grad = flat.T.astype(f32)
                out[rows_of] = grad
                terms += jnp.sum(grad * weight[rows_of].astype(f32), axis=1, keepdims=True)
            gain_out[rows_of] = (as_row(terms) / gain_ref[:, rows_of])[0]

    return pl.pallas_call(
        body,
        out_shape=[jax.ShapeDtypeStruct((width, width), f32)] * 4
        + [jax.ShapeDtypeStruct((width,), f32)],
        in_specs=[SMEM] + [VMEM] * 6,
        out_specs=[VMEM] * 5,
        compiler_params=LIMIT,
        cost_estimate=busy(7),
        name="place_heads",
    )(core, mine, other, *weights, gain[None, :])


def input_gradient(grads, weights, block_input, gain, d_middle, owners):
    streams, rows, width = block_input.shape

    def body(d_ref, wq, wk, wv, x_ref, gain_ref, d_middle_ref, out):
        for stream in range(streams):
            d_normed = jnp.zeros((rows, width), jnp.float32)
            for kind, weight in enumerate((wq, wk, wv)):
                rows_of = slice(kind * HEAD_DIM, (kind + 1) * HEAD_DIM)
                flat = jnp.concatenate([d_ref[owner, rows_of] for owner in owners[stream]], axis=0)
                d_normed += dot(flat.T, weight[...], 1, 1)
            unit, root = normalize(x_ref[stream].astype(jnp.float32))
            d_values = normalize_back(d_normed, unit, root, gain_ref[...])
            out[stream] = d_middle_ref[stream * rows : (stream + 1) * rows] + d_values

    return pl.pallas_call(
        body,
        out_shape=jax.ShapeDtypeStruct(block_input.shape, jnp.float32),
        in_specs=[VMEM] * 7,
        out_specs=VMEM,
        compiler_params=LIMIT,
        cost_estimate=busy(6),
        name="input_gradient",
    )(grads, *weights, block_input, gain[None, :], d_middle)


def wide(ref, frame, spaces, first, last, count=1):
    return jnp.concatenate(
        [ref[frame * spaces + j, first:last, :] for j in range(spaces * count)], axis=1
    )


def attend(lo, packed, frames):
    devices, _, rows = packed.shape
    spaces = devices // frames
    per_frame = rows * spaces
    dim = HEAD_DIM

    def body(lo_ref, r_ref, o_ref, low_ref, lse_ref, kv, top, total, summed):
        def turn_keys(device, _):
            kv[pl.ds(pl.multiple_of(device * rows, rows), rows), :] = r_ref[device, dim:, :].T
            return 0

        lax.fori_loop(0, devices, turn_keys, 0, unroll=4)

        def group(queries, _):
            first = queries * CLIP
            query = [wide(r_ref, first + i, spaces, 0, dim) for i in range(CLIP)]

            def update(i, keys, scores, fresh):
                fold = lambda op, value: op(value.reshape(-1, 8, per_frame), axis=0)
                new_top = fold(jnp.max, scores[0])
                for part in scores[1:]:
                    new_top = jnp.maximum(new_top, fold(jnp.max, part))
                new_top = jnp.max(new_top, axis=0, keepdims=True)
                if not fresh:
                    old_top = top[i]
                    new_top = jnp.maximum(old_top, new_top)
                new_total, new_sum = 0.0, 0.0
                for j, part in enumerate(scores):
                    weights = jnp.exp(part - new_top)
                    new_total += fold(jnp.sum, weights)
                    values = wide(r_ref, keys * CLIP + j, spaces, 2 * dim, 3 * dim)
                    new_sum += dot(values, weights.astype(jnp.bfloat16), 1, 0)
                new_total = jnp.sum(new_total, axis=0, keepdims=True)
                if not fresh:
                    factor = jnp.exp(old_top - new_top)
                    new_total += total[i] * factor
                    new_sum += summed[i] * factor
                top[i] = new_top
                total[i] = new_total
                summed[i] = new_sum

            def against(keys, counts, fresh):
                scores = []
                for i, count in enumerate(counts):
                    rows_of = [
                        pl.ds(pl.multiple_of((keys * CLIP + j) * per_frame, per_frame), per_frame)
                        for j in range(count)
                    ]
                    scores.append([dot(kv[part, :dim], query[i], 1, 0) for part in rows_of])
                for i in range(CLIP):
                    update(i, keys, scores[i], fresh)

            against(queries, range(1, CLIP + 1), True)

            def earlier(keys, _):
                against(keys, [CLIP] * CLIP, False)
                return 0

            lax.fori_loop(lo_ref[first] // CLIP, queries, earlier, 0)
            for i in range(CLIP):
                out = summed[i] / total[i]
                for j in range(spaces):
                    piece = out[:, j * rows : (j + 1) * rows]
                    o_ref[(first + i) * spaces + j] = piece
                    low_ref[(first + i) * spaces + j] = piece.astype(jnp.bfloat16)
                lse_ref[first + i] = top[i] + jnp.log(total[i])
            return 0

        lax.fori_loop(0, frames // CLIP, group, 0)

    f32 = jnp.float32
    return pl.pallas_call(
        body,
        out_shape=(
            jax.ShapeDtypeStruct((devices, dim, rows), f32),
            jax.ShapeDtypeStruct((devices, dim, rows), jnp.bfloat16),
            jax.ShapeDtypeStruct((frames, 1, per_frame), f32),
            jax.ShapeDtypeStruct((devices * rows, 2 * dim), jnp.bfloat16),
        ),
        in_specs=[SMEM, VMEM],
        out_specs=(VMEM,) * 4,
        scratch_shapes=[
            pltpu.VMEM((CLIP, 1, per_frame), f32),
            pltpu.VMEM((CLIP, 1, per_frame), f32),
            pltpu.VMEM((CLIP, dim, per_frame), f32),
        ],
        compiler_params=LIMIT,
        cost_estimate=busy(28),
        name="attend",
    )(lo, packed)


def attend_back(hi, packed, d_own, lse, kv, tables, rest, frames, start, stop):
    devices, _, rows = packed.shape
    spaces = devices // frames
    per_frame = rows * spaces
    dim = HEAD_DIM
    last = stop * CLIP == frames
    f32 = jnp.float32
    shift = dim if last else 0
    base = 0 if last else start * CLIP * spaces

    def body(hi_ref, r_ref, d_ref, lse_ref, kv_ref, table_ref, *rest):
        if last:
            delta_ref, qd_ref, before, piece, where_ref, near_ref, far_ref, *rest = rest
            out, keep, give, acc, left, d_query_ref, product, near, far, sems = rest
        else:
            o_ref, out, d_query_ref, qd_ref, delta_ref, acc, left = rest

        def begin(frame, _):
            d_query_ref[frame] = jnp.zeros((dim, per_frame), f32)
            for j in range(spaces):
                device = frame * spaces + j
                both = jnp.concatenate([r_ref[device, :dim, :], d_ref[device]], axis=0)
                qd_ref[pl.ds(pl.multiple_of(device * rows, rows), rows), :] = both.T
                delta_ref[frame, :, j * rows : (j + 1) * rows] = jnp.sum(
                    d_ref[device].astype(f32) * o_ref[device], axis=0, keepdims=True
                )
            return 0

        def fetch(pair, slot):
            plane = pair // 2
            entry = jnp.where(pair % 2 == 0, plane, frames // 2 - 1 - plane)
            return [
                pltpu.make_async_copy(source.at[pl.ds(2 * entry, 2)], target.at[slot], sems.at[slot, i])
                for i, (source, target) in enumerate(((near_ref, near), (far_ref, far)))
            ]

        if last:
            for copy in fetch(0, 0):
                copy.start()
            pltpu.sync_copy(before, d_query_ref)
        else:
            lax.fori_loop(0, frames, begin, 0, unroll=2)
        if last:
            out[: piece.shape[0], dim:, :] = piece[...]
        first_half = lax.broadcasted_iota(jnp.int32, (per_frame, 2 * dim), 1) < dim

        def group(keys, _):
            first = keys * CLIP
            for i in range(CLIP):
                rows_of = pl.ds(pl.multiple_of((first + i) * per_frame, per_frame), per_frame)
                both = kv_ref[rows_of, :]
                zero = jnp.zeros_like(both)
                left[i, :per_frame] = jnp.where(first_half, both, zero)
                left[i, per_frame:] = jnp.where(first_half, zero, both)

            def against(queries, lead, fresh):
                own = queries * CLIP
                d_scores = [[] for _ in range(CLIP)]
                right = []
                for n in range(CLIP):
                    d_rows = [d_ref[(own + n) * spaces + j] for j in range(spaces)]
                    both = [wide(r_ref, own + n, spaces, 0, dim), jnp.concatenate(d_rows, axis=1)]
                    right.append(jnp.concatenate(both, axis=0))
                for i in range(CLIP):
                    term = 0.0
                    taken = range(i if lead else 0, CLIP)
                    products = [dot(left[i], right[n], 1, 0) for n in taken]
                    pairs = []
                    for n, both in zip(taken, products):
                        weights = jnp.exp(both[:per_frame] - lse_ref[own + n])
                        change = weights * (both[per_frame:] - delta_ref[own + n])
                        d_scores[n].append(change.astype(jnp.bfloat16))
                        pairs.append(
                            jnp.concatenate([weights.astype(jnp.bfloat16), d_scores[n][-1]], axis=0)
                        )
                    for n, pair in zip(taken, pairs):
                        rows_of = pl.ds(pl.multiple_of((own + n) * per_frame, per_frame), per_frame)
                        term += dot(pair, qd_ref[rows_of, :], 1, 0)
                    if fresh:
                        acc[i] = term
                    else:
                        acc[i] += term
                for n in range(CLIP):
                    keys_of = [
                        wide(r_ref, first + i, spaces, dim, 2 * dim) for i in range(len(d_scores[n]))
                    ]
                    d_query_ref[own + n] += dot(
                        jnp.concatenate(keys_of, axis=1), jnp.concatenate(d_scores[n], axis=0), 1, 0
                    )

            against(keys, True, True)

            def later(queries, _):
                against(queries, False, False)
                return 0

            lax.fori_loop(keys + 1, hi_ref[first] // CLIP, later, 0)
            for i in range(CLIP):
                total = acc[i]
                d_key = total[per_frame:].T[:dim]
                d_key = turned(d_key, table_ref[first + i, 0], table_ref[first + i, 1], -1.0)
                d_key = d_key.astype(jnp.bfloat16)
                d_value = total[:per_frame].T[dim:].astype(jnp.bfloat16)
                for j in range(spaces):
                    device = (first + i) * spaces + j - base
                    columns = slice(j * rows, (j + 1) * rows)
                    out[device, shift : shift + dim, :] = d_key[:, columns]
                    out[device, shift + dim : shift + 2 * dim, :] = d_value[:, columns]
            return 0

        lax.fori_loop(start, stop, group, 0)
        if last:

            def finish(frame, _):
                whole_query = d_query_ref[frame] * (1.0 / math.sqrt(dim))
                whole_query = turned(whole_query, table_ref[frame, 0], table_ref[frame, 1], -1.0)
                whole_query = whole_query.astype(jnp.bfloat16)
                for j in range(spaces):
                    out[frame * spaces + j, :dim, :] = whole_query[:, j * rows : (j + 1) * rows]
                return 0

            lax.fori_loop(0, frames, finish, 0)

            core = where_ref[0]
            product[...] = jnp.zeros_like(product)

            def multiply(pair, _):
                slot = lax.rem(pair, 2)

                @pl.when(pair + 1 < frames // 2)
                def _():
                    for copy in fetch(pair + 1, 1 - slot):
                        copy.start()

                for copy in fetch(pair, slot):
                    copy.wait()
                lefts, rights = [], []
                for index in range(2):
                    frame = 2 * pair + index
                    lefts += [out[spaces * frame + core], out[spaces * frame + 1 - core]]
                    rights += [near[slot, index], far[slot, index]]
                product[...] += dot(
                    jnp.concatenate(lefts, axis=1), jnp.concatenate(rights, axis=0), 1, 0
                )
                return 0

            lax.fori_loop(0, frames // 2, multiply, 0)
            half = product.shape[1] // 2
            first = where_ref[1] == 0
            keep[...] = jnp.where(first, product[:, :half], product[:, half:])
            give[...] = jnp.where(first, product[:, half:], product[:, :half]).astype(jnp.bfloat16)

    inputs = [hi, packed, d_own, lse, kv, tables, *rest]
    in_specs = [SMEM] + [VMEM] * 5
    query_sum = jax.ShapeDtypeStruct((frames, dim, per_frame), f32)
    scratch = [
        pltpu.VMEM((CLIP, 2 * per_frame, 2 * dim), f32),
        pltpu.VMEM((CLIP, 2 * per_frame, 2 * dim), jnp.bfloat16),
    ]
    if last:
        width = rest[-1].shape[2]
        in_specs += [VMEM, VMEM, ANY, VMEM, SMEM, ANY, ANY]
        out_shape = (
            jax.ShapeDtypeStruct((devices, 3 * dim, rows), jnp.bfloat16),
            jax.ShapeDtypeStruct((3 * dim, width // 2), f32),
            jax.ShapeDtypeStruct((3 * dim, width // 2), jnp.bfloat16),
        )
        scratch += [
            pltpu.VMEM((frames, dim, per_frame), f32),
            pltpu.VMEM((3 * dim, width), f32),
            pltpu.VMEM((2, 2, rows, width), jnp.bfloat16),
            pltpu.VMEM((2, 2, rows, width), jnp.bfloat16),
            pltpu.SemaphoreType.DMA((2, 2)),
        ]
    else:
        shape = ((stop - start) * CLIP * spaces, 2 * dim, rows)
        in_specs += [VMEM]
        out_shape = (
            jax.ShapeDtypeStruct(shape, jnp.bfloat16),
            query_sum,
            jax.ShapeDtypeStruct((devices * rows, 2 * dim), jnp.bfloat16),
            jax.ShapeDtypeStruct((frames, 1, per_frame), f32),
        )
    return pl.pallas_call(
        body,
        out_shape=out_shape,
        in_specs=in_specs,
        out_specs=(VMEM,) * len(out_shape),
        scratch_shapes=scratch,
        compiler_params=LIMIT,
        cost_estimate=busy(20),
        name="attend_back",
    )(*inputs)


def after(value, *others):
    return lax.optimization_barrier((value, *others))[0]


class Ring:
    def __init__(self):
        self.frames = lax.axis_size("frame")
        self.spaces = lax.axis_size("space")
        self.planes = self.frames // 4
        self.frame = lax.axis_index("frame")
        self.core = lax.axis_index("space")
        self.plane = self.frame // 4
        self.spot = self.frame % 4
        bits = (self.frame % 2, (self.frame // 2) % 2)
        self.first_bit = jnp.where(self.core == 0, bits[0], bits[1])
        self.second_bit = jnp.where(self.core == 0, bits[1], bits[0])

    def send(self, value, target):
        moves = []
        for frame in range(self.frames):
            for core in range(self.spaces):
                to_frame, to_core = target(frame, core)
                moves.append((frame * self.spaces + core, to_frame * self.spaces + to_core))
        return lax.ppermute(value, ("frame", "space"), moves)

    def first(self, value):
        return self.send(value, lambda frame, core: (frame ^ (1 if core == 0 else 2), core))

    def second(self, value):
        return self.send(value, lambda frame, core: (frame ^ (2 if core == 0 else 1), core))

    def across(self, value):
        return self.send(value, lambda frame, core: (frame, 1 - core))

    def up(self, value, step):
        size = self.frames
        return self.send(value, lambda frame, core: ((frame + 4 * step) % size, core))

    def send_planes(self, pieces):
        return [self.up(piece, step) for step, piece in enumerate(pieces[1:], 1)]

    def plane_part(self, value):
        groups = [list(range(spot, self.frames, 4)) for spot in range(4)]
        if value.shape[0] % (16 * self.planes):
            return lax.psum(value, "frame", axis_index_groups=groups)
        return lax.psum_scatter(
            value, "frame", scatter_dimension=0, axis_index_groups=groups, tiled=True
        )

    def add_planes(self, own, arrived):
        total = own.astype(jnp.float32)
        for piece in arrived:
            total = total + piece.astype(jnp.float32)
        return total.astype(jnp.bfloat16)

    def spread_planes(self, value, count):
        return [self.up(value, step) for step in range(1, count)]

    def gather_spots(self):
        near = jnp.where(self.core == 0, 2, 1)
        own = jnp.stack([self.spot, self.spot ^ near, self.spot ^ (3 - near), self.spot ^ 3])
        other = jnp.stack([self.spot, self.spot ^ (3 - near), self.spot ^ near, self.spot ^ 3])
        cores = jnp.repeat(jnp.stack([self.core, 1 - self.core]), 4)
        return jnp.concatenate([own, other]), cores

    def halves(self, value, bit):
        rows, columns = value.shape
        cut = value.reshape(2, rows // 2, columns)
        pick = lambda index: lax.dynamic_index_in_dim(cut, index, 0, keepdims=False)
        return pick(bit), pick(1 - bit).astype(jnp.bfloat16)


def frame_limits(clip_frames, frames):
    ends = jnp.cumsum(clip_frames, axis=1, dtype=jnp.int32)
    begins = ends - clip_frames
    index = jnp.arange(frames, dtype=jnp.int32)[None, :, None]
    inside = (index >= begins[:, None, :]) & (index < ends[:, None, :])
    pick = lambda table: jnp.sum(jnp.where(inside, table[:, None, :], 0), axis=2, dtype=jnp.int32)
    return pick(begins), pick(ends)


def local(
    block_input,
    norm1_gain,
    w_query,
    w_key,
    w_value,
    w_out,
    norm2_gain,
    w_up,
    w_down,
    clip_frames,
    cotangent,
):
    streams, rows, width = block_input.shape
    ring = Ring()
    frames, spaces, planes = ring.frames, ring.spaces, ring.planes
    devices = frames * spaces
    per_frame = rows * spaces
    tokens = streams * rows
    axes = ("frame", "space")
    low = jnp.bfloat16
    core = jnp.reshape(ring.core, (1,))
    spots, cores = ring.gather_spots()
    slots = 4 * spaces

    owners = head_owners(frames, spaces)
    w_projections = (w_query, w_key, w_value)
    side = ring.frame % 2

    def swap(value):
        return lax.all_to_all(value, axes, 0, 0, tiled=True)

    spot_of = jnp.stack([ring.frame, ring.core * rows])
    sent, normed = project(
        spot_of, clip_frames, block_input, norm1_gain, *w_projections, owners, devices, per_frame
    )
    packed = swap(sent)

    begin, end = frame_limits(after(clip_frames, sent), frames)
    frame_ids = jnp.arange(frames, dtype=jnp.int32)
    mine = ring.frame * spaces + ring.core
    idle = ~jnp.any(mine == jnp.asarray(owners))
    lo = jnp.where(idle, frame_ids, jnp.where(side == 0, begin[0], begin[1]))
    hi = jnp.where(idle, frame_ids, jnp.where(side == 0, end[0], end[1]))

    neighbour = lambda value: ring.send(value, lambda frame, core: (frame ^ 1, core))
    stream_near = neighbour(lax.dynamic_index_in_dim(normed, 1 - side, 0))
    stream_own = lax.dynamic_index_in_dim(normed, side, 0)
    stream_pair = jnp.where(
        side == 0,
        jnp.concatenate([stream_own, stream_near]),
        jnp.concatenate([stream_near, stream_own]),
    )
    up, down = range(planes), range(planes)[::-1]
    same_side = [
        [4 * plane + bit for plane in up] + [4 * plane + 2 + bit for plane in down] for bit in range(2)
    ]
    stream_mine = lax.all_gather(
        stream_pair, "frame", axis=0, tiled=True, axis_index_groups=same_side
    )
    cot_flat = cotangent.reshape(tokens, width)
    cot_one = ring.second(cot_flat)
    out, out_low, lse, kv = attend(lo, after(packed, stream_pair), frames)
    cot_pair = jnp.stack([cot_flat, after(cot_one, out_low)])
    attended = swap(after(out_low, cot_pair))
    tables = rope_tables(after(lo, out_low), frames, per_frame)
    attended = after(attended, tables)
    cot_far = ring.first(cot_pair)

    middle, two = attention_out(attended, block_input, w_out, norm2_gain, owners)
    chunk, skip = 512, 3
    cot_far = after(cot_far, middle)
    cot_plane = [cot_pair, cot_far, ring.across(cot_pair), ring.across(cot_far)]
    so_far = feed_first(two, cotangent, w_up, w_down, chunk, skip)
    two_pair = jnp.stack([two, ring.second(two)])
    so_far = after(so_far, two_pair, stream_mine)
    two_far = ring.first(two_pair)
    two_pair_other = ring.across(two_pair)
    block_output, d_middle, d_sent, out_keep, out_give = feed_rest(
        core, so_far, attended, middle, two, cotangent, w_out, norm2_gain, w_up, w_down,
        chunk, skip, owners,
    )
    d_own = swap(d_sent)
    two_far, two_pair_other = after((two_far, two_pair_other), d_sent)
    two_plane = [two_pair, two_far, two_pair_other, ring.across(two_far)]
    out_sum = out_keep + ring.across(out_give).astype(jnp.float32)
    out_keep, out_give = ring.halves(out_sum, ring.first_bit)
    out_other = ring.first(out_give)
    pieces = hidden_gradients(
        jnp.stack([ring.spot * spaces + ring.core, ring.plane]),
        after(two_plane, out_give), cot_plane, w_up, w_down, slots, planes,
    )

    arrived = ring.send_planes(pieces)
    out_sum = out_keep + after(out_other, pieces[0]).astype(jnp.float32)
    out_keep, out_give = ring.halves(out_sum, ring.second_bit)
    out_sum = (out_keep + ring.second(out_give).astype(jnp.float32)).astype(low)
    d_own = after(d_own, out_sum)
    out_sum = ring.plane_part(out_sum)
    groups = frames // CLIP
    first_part, d_query, qd, delta = attend_back(
        hi, packed, d_own, lse, kv, tables, (out,), frames, 0, groups // 2
    )
    total = ring.add_planes(pieces[0], after(arrived, first_part))
    stream_other = ring.across(stream_mine)
    grads, keep, give = attend_back(
        hi, packed, d_own, lse, kv, tables,
        (after(delta, total, out_sum), qd, d_query, first_part, jnp.stack([ring.core, side]),
         stream_mine, stream_other),
        frames, groups // 2, groups,
    )
    spread, keep = lax.optimization_barrier((ring.spread_planes(total, planes), keep))
    back = swap(grads)
    heads_sum = (keep + neighbour(give).astype(jnp.float32)).astype(low)
    heads_mine = lax.all_gather(jnp.concatenate([heads_sum, out_sum]), "frame")
    hidden = after(jnp.concatenate([total, *spread]), heads_sum)
    one, two = ring.second(hidden), ring.first(hidden)
    three = ring.first(after(one, back))
    near = [hidden, one, two]
    far = [ring.across(value) for value in near]
    grad_input = input_gradient(back, w_projections, block_input, norm1_gain, d_middle, owners)
    unit_slots = spots * spaces + cores
    where = jnp.stack([unit_slots, jnp.broadcast_to(ring.plane, cores.shape)])
    places = lambda *entries: jnp.stack([where[:, entry] for entry in entries], axis=1)
    placed = place_hidden(
        places(0, 1, 2, 4, 5, 6), after(near + far, grad_input), None, w_up, norm2_gain, planes, False
    )
    three = after(three, placed[0])
    three_other = ring.across(three)
    heads_other = ring.across(after(heads_mine, three))
    grad_query, grad_key, grad_value, grad_out, gain_one = place_heads(
        jnp.reshape(ring.core, (1,)), heads_mine, heads_other,
        w_projections, norm1_gain, owners,
    )
    grad_up, grad_down, gain_two = place_hidden(
        places(3, 7), [three, after(three_other, grad_query)], placed, w_up, norm2_gain, planes, True
    )
    return (
        block_output,
        grad_input,
        gain_one,
        grad_query,
        grad_key,
        grad_value,
        grad_out,
        gain_two,
        grad_up,
        grad_down,
    )


def solution(mesh):
    spread = P(None, ("frame", "space"), None)
    in_specs = (spread,) + (P(),) * 9 + (spread,)
    out_specs = (spread, spread) + (P(),) * 8
    return jax.shard_map(local, mesh=mesh, in_specs=in_specs, out_specs=out_specs, check_vma=False)
```

```python
import functools
import math

import jax
import jax.numpy as jnp
import numpy as np
from jax import lax
from jax.experimental import pallas as pl
from jax.experimental.pallas import tpu as pltpu
from jax.sharding import PartitionSpec as P

HEADS = 12
HEAD_DIM = 64
VMEM = pl.BlockSpec(memory_space=pltpu.VMEM)
ANY = pl.BlockSpec(memory_space=pl.ANY)
SMEM = pl.BlockSpec(memory_space=pltpu.SMEM)
LIMIT = pltpu.CompilerParams(vmem_limit_bytes=56 * 2**20)
FLOPS = 1.15e9


def busy(microseconds):
    return pl.CostEstimate(flops=int(microseconds * FLOPS), transcendentals=0, bytes_accessed=0)


CLIP = 4


def dot(left, right, left_dim, right_dim):
    return lax.dot_general(
        left,
        right,
        (((left_dim,), (right_dim,)), ((), ())),
        preferred_element_type=jnp.float32,
    )


def head_owners(frames, spaces):
    planes = frames // 4
    share = -(-HEADS // planes)
    return [
        [
            ((head // share) * 4 + (head % share) // spaces * 2 + stream) * spaces
            + (head % share) % spaces
            for head in range(HEADS)
        ]
        for stream in range(2)
    ]


def normalize(values):
    average = jnp.mean(values, axis=-1, keepdims=True)
    centred = values - average
    root = lax.rsqrt(jnp.mean(centred * centred, axis=-1, keepdims=True) + 1e-05)
    return centred * root, root


def normalize_back(d_scaled, unit, root, gain):
    d_unit = d_scaled * gain
    mean_one = jnp.mean(d_unit, axis=-1, keepdims=True)
    mean_two = jnp.mean(d_unit * unit, axis=-1, keepdims=True)
    return root * (d_unit - mean_one - unit * mean_two)


def frequencies(columns):
    half = HEAD_DIM // 2
    values = np.exp(np.arange(half) * (-2.0 * math.log(10000.0) / HEAD_DIM))
    return jnp.asarray(np.broadcast_to(values[:, None], (half, columns)), jnp.float32)


def turned(value, cosine, sine, sign):
    half = HEAD_DIM // 2
    first, second = value[:half], value[half:]
    return jnp.concatenate(
        [first * cosine - sign * second * sine, second * cosine + sign * first * sine], axis=0
    )


def project(place, clips, block_input, gain, w_query, w_key, w_value, owners, devices, per_frame):
    streams, rows, width = block_input.shape
    half = HEAD_DIM // 2
    low = jnp.bfloat16
    scale = 1.0 / math.sqrt(HEAD_DIM)
    owned = {device for row in owners for device in row}

    def body(place_ref, clips_ref, freq_ref, x_ref, gain_ref, wq, wk, wv, out, normed_out, table):
        frame, first_row = place_ref[0], place_ref[1]
        for stream in range(streams):
            begin = jnp.int32(0)
            running = jnp.int32(0)
            for clip in range(clips_ref.shape[1]):
                length = clips_ref[stream, clip]
                begin = jnp.where((frame >= running) & (frame < running + length), running, begin)
                running = running + length
            row = lax.broadcasted_iota(jnp.int32, (half, rows), 1)
            position = ((frame - begin) * per_frame + first_row + row).astype(jnp.float32)
            angles = position * freq_ref[...]
            table[0, stream] = jnp.cos(angles)
            table[1, stream] = jnp.sin(angles)
        values = x_ref[...].astype(jnp.float32).reshape(streams * rows, width)
        normed = (normalize(values)[0] * gain_ref[...][None, :]).astype(low)
        normed_out[...] = normed.reshape(streams, rows, width)
        for kind, weight in enumerate((wq, wk, wv)):
            product = dot(normed, weight[...], 1, 0).T
            for stream in range(streams):
                columns = slice(stream * rows, (stream + 1) * rows)
                for head in range(HEADS):
                    piece = product[head * HEAD_DIM : (head + 1) * HEAD_DIM, columns]
                    if kind < 2:
                        piece = turned(piece, table[0, stream], table[1, stream], 1.0)
                    if kind == 0:
                        piece = piece * scale
                    out[
                        owners[stream][head], kind * HEAD_DIM : (kind + 1) * HEAD_DIM, :
                    ] = piece.astype(low)
        for spare in range(devices):
            if spare not in owned:
                out[spare] = jnp.zeros((3 * HEAD_DIM, rows), low)

    return pl.pallas_call(
        body,
        out_shape=(
            jax.ShapeDtypeStruct((devices, 3 * HEAD_DIM, rows), low),
            jax.ShapeDtypeStruct((streams, rows, width), low),
        ),
        in_specs=[SMEM, SMEM] + [VMEM] * 6,
        out_specs=(VMEM, VMEM),
        scratch_shapes=[pltpu.VMEM((2, streams, half, rows), jnp.float32)],
        compiler_params=LIMIT,
        cost_estimate=busy(5),
        name="project",
    )(place, clips, frequencies(rows), block_input, gain, w_query, w_key, w_value)


def rope_tables(lo, frames, per_frame):
    half = HEAD_DIM // 2

    def body(lo_ref, freq_ref, out):
        def one(frame, _):
            row = lax.broadcasted_iota(jnp.int32, (half, per_frame), 1)
            position = ((frame - lo_ref[frame]) * per_frame + row).astype(jnp.float32)
            angles = position * freq_ref[...]
            out[frame, 0] = jnp.cos(angles)
            out[frame, 1] = jnp.sin(angles)
            return 0

        lax.fori_loop(0, frames, one, 0)

    return pl.pallas_call(
        body,
        out_shape=jax.ShapeDtypeStruct((frames, 2, half, per_frame), jnp.float32),
        in_specs=[SMEM, VMEM],
        out_specs=VMEM,
        compiler_params=LIMIT,
        cost_estimate=busy(4),
        name="rope_tables",
    )(lo, frequencies(per_frame))


GELU = math.sqrt(2.0 / math.pi)


def gelu_pair(value):
    square = value * value
    bent = jnp.tanh(GELU * value * (1.0 + 0.044715 * square))
    side = 0.5 * (1.0 + bent)
    slope = side + 0.5 * value * (1.0 - bent * bent) * (GELU * (1.0 + 3 * 0.044715 * square))
    return value * side, slope


def attention_out(attended, block_input, w_out, gain, owners):
    streams, rows, width = block_input.shape
    low = jnp.bfloat16

    def body(att, x_ref, wo, gain_ref, middle, two_ref):
        for stream in range(streams):
            rows_of = slice(stream * rows, (stream + 1) * rows)
            flat = jnp.concatenate([att[owner] for owner in owners[stream]], axis=0)
            values = x_ref[stream].astype(jnp.float32) + dot(flat.T, wo[...], 1, 0)
            middle[rows_of] = values
            two_ref[rows_of] = (normalize(values)[0] * gain_ref[...]).astype(low)

    return pl.pallas_call(
        body,
        out_shape=(
            jax.ShapeDtypeStruct((streams * rows, width), jnp.float32),
            jax.ShapeDtypeStruct((streams * rows, width), low),
        ),
        in_specs=[VMEM] * 4,
        out_specs=(VMEM, VMEM),
        compiler_params=LIMIT,
        cost_estimate=busy(3),
        name="attention_out",
    )(attended, block_input, w_out, gain[None, :])


def as_row(column):
    return jnp.broadcast_to(column, (column.shape[0], 128)).T[:1]


def whole(shape):
    return pl.BlockSpec(shape, lambda *indices: (0,) * len(shape))


def feed_first(two, cotangent, w_up, w_down, chunk, steps):
    tokens, width = two.shape
    low = jnp.bfloat16

    def body(two_ref, cot, up, down, result, d_two):
        cot_flat = cot[...].reshape(tokens, width)
        active, slope = gelu_pair(dot(two_ref[...], up[...], 1, 0))
        d_hidden = (dot(cot_flat, down[...], 1, 1) * slope).astype(low)
        forward = dot(active.astype(low), down[...], 1, 0)
        backward = dot(d_hidden, up[...], 1, 1)

        @pl.when(pl.program_id(0) == 0)
        def _():
            result[...] = forward
            d_two[...] = backward

        @pl.when(pl.program_id(0) > 0)
        def _():
            result[...] += forward
            d_two[...] += backward

    return pl.pallas_call(
        body,
        grid=(steps,),
        out_shape=(jax.ShapeDtypeStruct((tokens, width), jnp.float32),) * 2,
        in_specs=[
            whole(two.shape), whole(cotangent.shape),
            pl.BlockSpec((width, chunk), lambda i: (0, i)),
            pl.BlockSpec((chunk, width), lambda i: (i, 0)),
        ],
        out_specs=(whole((tokens, width)),) * 2,
        compiler_params=LIMIT,
        cost_estimate=busy(7),
        name="feed_first",
    )(two, cotangent, w_up, w_down)


def feed_rest(core, so_far, attended, middle, two, cotangent, w_out, gain, w_up, w_down, chunk, skip, owners):
    devices, head_width, rows = attended.shape
    streams, _, width = cotangent.shape
    tokens = streams * rows
    half = width // 2
    steps = w_up.shape[1] // chunk - skip
    low = jnp.bfloat16
    f32 = jnp.float32
    owned = {device for row in owners for device in row}

    def body(
        core_ref, first_result, first_two, att, middle, two_ref, cot, wo, gain_ref, up, down,
        result_ref, d_middle_ref, d_own, keep, give,
        result, d_two,
    ):
        step = pl.program_id(0)
        cot_flat = cot[...].reshape(tokens, width)
        active, slope = gelu_pair(dot(two_ref[...], up[...], 1, 0))
        d_hidden = (dot(cot_flat, down[...], 1, 1) * slope).astype(low)
        forward = dot(active.astype(low), down[...], 1, 0)
        backward = dot(d_hidden, up[...], 1, 1)

        @pl.when(step == 0)
        def _():
            result[...] = first_result[...] + forward
            d_two[...] = first_two[...] + backward

        @pl.when(step > 0)
        def _():
            result[...] += forward
            d_two[...] += backward

        @pl.when(step == steps - 1)
        def _():
            result_ref[...] = (middle[...] + result[...]).astype(low).reshape(streams, rows, width)
            unit, root = normalize(middle[...])
            d_middle = cot_flat.astype(f32) + normalize_back(
                d_two[...], unit, root, gain_ref[...]
            )
            d_middle_ref[...] = d_middle
            branch = d_middle.astype(low)
            d_att = dot(branch, wo[...], 1, 1).T.astype(low)
            total = jnp.zeros((width, width), f32)
            for stream in range(streams):
                rows_of = slice(stream * rows, (stream + 1) * rows)
                for head, owner in enumerate(owners[stream]):
                    d_own[owner] = d_att[head * HEAD_DIM : (head + 1) * HEAD_DIM, rows_of]
                flat = jnp.concatenate([att[owner] for owner in owners[stream]], axis=0)
                total += dot(flat, branch[rows_of], 1, 0)
            for spare in range(devices):
                if spare not in owned:
                    d_own[spare] = jnp.zeros((head_width, rows), low)
            first = core_ref[0] == 0
            keep[...] = jnp.where(first, total[:, :half], total[:, half:])
            give[...] = jnp.where(first, total[:, half:], total[:, :half]).astype(low)

    shapes = (
        ((streams, rows, width), low),
        ((tokens, width), f32),
        ((devices, head_width, rows), low),
        ((width, half), f32),
        ((width, half), low),
    )
    return pl.pallas_call(
        body,
        grid=(steps,),
        out_shape=tuple(jax.ShapeDtypeStruct(*entry) for entry in shapes),
        in_specs=[
            SMEM, whole((tokens, width)), whole((tokens, width)),
            whole(attended.shape), whole(middle.shape), whole(two.shape),
            whole(cotangent.shape), whole(w_out.shape), whole((1, width)),
            pl.BlockSpec((width, chunk), lambda i: (0, i + skip)),
            pl.BlockSpec((chunk, width), lambda i: (i + skip, 0)),
        ],
        out_specs=tuple(whole(shape) for shape, _ in shapes),
        scratch_shapes=[pltpu.VMEM((tokens, width), f32), pltpu.VMEM((tokens, width), f32)],
        compiler_params=LIMIT,
        cost_estimate=busy(10),
        name="feed_rest",
    )(core, *so_far, attended, middle, two, cotangent, w_out, gain[None, :], w_up, w_down)


def hidden_gradients(where, two, cot, w_up, w_down, slots, planes):
    _, tokens, width = two[0].shape
    count = len(two)
    hidden = w_up.shape[1] // slots
    rows = width // planes
    height = 2 * rows
    low = jnp.bfloat16

    def body(where_ref, *rest):
        two_refs, cot_refs, (up, down) = rest[:count], rest[count : 2 * count], rest[2 * count :][:2]
        rest = rest[2 * count + 2 :]
        outs, (up_sum, down_sum) = rest[:planes], rest[planes:]
        step = pl.program_id(0)

        def run(two_ref, cot_ref):
            two = two_ref[...].reshape(2 * tokens, width)
            cot = cot_ref[...].reshape(2 * tokens, width)
            active, slope = gelu_pair(dot(two, up[...], 1, 0))
            d_hidden = (dot(cot, down[...], 1, 1) * slope).astype(low)
            up_term = dot(two, d_hidden, 0, 0)
            down_term = dot(active.astype(low), cot, 0, 0)

            @pl.when(step == 0)
            def _():
                up_sum[...] = up_term
                down_sum[:hidden] = down_term[:, :hidden]
                down_sum[hidden:] = down_term[:, hidden:]

            @pl.when(step > 0)
            def _():
                up_sum[...] += up_term
                down_sum[:hidden] += down_term[:, :hidden]
                down_sum[hidden:] += down_term[:, hidden:]

        for index, refs in enumerate(zip(two_refs, cot_refs)):
            pl.when(step == index)(functools.partial(run, *refs))

        @pl.when(step == count - 1)
        def _():
            for index, out in enumerate(outs):
                plane = lax.rem(where_ref[1] + index, planes)
                rows_of = pl.ds(pl.multiple_of(plane * rows, rows), rows)
                out[:rows] = up_sum[rows_of, :].astype(low)
                out[rows:] = down_sum[rows_of, :].astype(low)

    return pl.pallas_call(
        body,
        grid_spec=pltpu.PrefetchScalarGridSpec(
            num_scalar_prefetch=1,
            grid=(count,),
            in_specs=[
                *[whole(two[0].shape)] * (2 * count),
                pl.BlockSpec((width, hidden), lambda i, where: (0, where[0])),
                pl.BlockSpec((hidden, width), lambda i, where: (where[0], 0)),
            ],
            out_specs=[whole((height, hidden))] * planes,
            scratch_shapes=[
                pltpu.VMEM((width, hidden), jnp.float32),
                pltpu.VMEM((width, hidden), jnp.float32),
            ],
        ),
        out_shape=[jax.ShapeDtypeStruct((height, hidden), low)] * planes,
        compiler_params=LIMIT,
        cost_estimate=busy(12),
        name="hidden_gradients",
    )(where, *two, *cot, w_up, w_down)


def place_hidden(where, pieces, placed, w_up, gain, planes, last):
    count = len(pieces)
    hidden = pieces[0][0].shape[1]
    width = w_up.shape[0]
    rows = width // planes
    f32 = jnp.float32
    second = placed is not None

    def body(where_ref, *rest):
        refs, (up_ref, gain_ref), rest = rest[: 2 * count], rest[2 * count :][:2], rest[2 * count + 2 :]
        gain_before = rest[2] if second else None
        up_out, down_out, gain_out, low, sums = rest[3:] if second else rest
        step = pl.program_id(0)

        def put(first_ref, others_ref):
            for index in range(planes):
                plane = lax.rem(where_ref[1, 0] + planes - index, planes)
                rows_of = pl.ds(pl.multiple_of(plane * rows, rows), rows)
                ref, first = (others_ref, 2 * rows * (index - 1)) if index else (first_ref, 0)
                up_out[rows_of, :] = ref[first : first + rows].astype(f32)
                low[rows_of, :] = ref[first + rows : first + 2 * rows].astype(f32)

        for index in range(count):
            pl.when(step == index)(functools.partial(put, *refs[2 * index : 2 * index + 2]))
        down_out[:, :hidden] = low[:hidden]
        down_out[:, hidden:] = low[hidden:]
        terms = jnp.sum(up_out[...] * up_ref[...].astype(f32), axis=1, keepdims=True)

        @pl.when(step == 0)
        def _():
            sums[...] = terms

        @pl.when(step > 0)
        def _():
            sums[...] += terms

        @pl.when(step == count - 1)
        def _():
            row = as_row(sums[...])
            row = row + gain_before[...][None, :] if second else row
            gain_out[...] = (row / gain_ref[...])[0] if last else row[0]

    unused = [pl.BlockSpec(memory_space=pl.ANY)] * 2 + [whole((width,))]
    return pl.pallas_call(
        body,
        grid_spec=pltpu.PrefetchScalarGridSpec(
            num_scalar_prefetch=1,
            grid=(count,),
            in_specs=[whole(part.shape) for pair in pieces for part in pair]
            + [
                pl.BlockSpec((width, hidden), lambda i, where: (0, where[0, i])),
                whole((1, width)),
            ]
            + (unused if second else []),
            out_specs=[
                pl.BlockSpec((width, hidden), lambda i, where: (0, where[0, i])),
                pl.BlockSpec((hidden, width), lambda i, where: (where[0, i], 0)),
                whole((width,)),
            ],
            scratch_shapes=[pltpu.VMEM((width, hidden), f32), pltpu.VMEM((width, 1), f32)],
        ),
        out_shape=[
            jax.ShapeDtypeStruct(w_up.shape, f32),
            jax.ShapeDtypeStruct(w_up.shape[::-1], f32),
            jax.ShapeDtypeStruct((width,), f32),
        ],
        input_output_aliases={2 * count + 3: 0, 2 * count + 4: 1} if second else {},
        compiler_params=LIMIT,
        cost_estimate=busy(0.2),
        name="place_hidden",
    )(where, *[part for pair in pieces for part in pair], w_up, gain[None, :], *(placed or []))


def place_heads(core, mine, other, weights, gain, owners):
    chips, height, width = mine.shape
    half = width // 2
    quarter = width // 4
    size = height - 3 * HEAD_DIM
    f32 = jnp.float32

    def body(core_ref, mine_ref, other_ref, wq, wk, wv, gain_ref, dq, dk, dv, out, gain_out):
        def rows_of_device(plane, row, core, rows):
            entry = chips - 1 - plane if row else plane
            own = core_ref[0] == core
            return jnp.where(own, mine_ref[entry, rows], other_ref[entry, rows])

        for spot in range(4):
            for core in range(2):
                first = (spot if core else spot % 2 * 2 + spot // 2) * quarter
                columns = slice(core * half, (core + 1) * half)
                held = slice(spot % 2 * half, (spot % 2 + 1) * half)
                for plane in range(quarter // size):
                    piece = rows_of_device(plane, spot // 2, core, slice(3 * HEAD_DIM, height))
                    rows_of = slice(first + plane * size, first + (plane + 1) * size)
                    out[rows_of, columns] = piece[:, held].astype(f32)
        terms = jnp.zeros((width, 1), f32)
        for kind, (weight, target) in enumerate(((wq, dq), (wk, dk), (wv, dv))):
            rows = slice(kind * HEAD_DIM, (kind + 1) * HEAD_DIM)
            pieces = [
                rows_of_device(owner // 8, owner // 4 % 2, owner % 2, rows) for owner in owners[0]
            ]
            grad = jnp.concatenate(pieces, axis=0).T.astype(f32)
            target[...] = grad
            terms += jnp.sum(grad * weight[...].astype(f32), axis=1, keepdims=True)
        gain_out[...] = (as_row(terms) / gain_ref[...])[0]

    return pl.pallas_call(
        body,
        out_shape=[jax.ShapeDtypeStruct((width, width), f32)] * 4
        + [jax.ShapeDtypeStruct((width,), f32)],
        in_specs=[SMEM] + [VMEM] * 6,
        out_specs=[VMEM] * 5,
        compiler_params=LIMIT,
        cost_estimate=busy(0.2),
        name="place_heads",
    )(core, mine, other, *weights, gain[None, :])


def input_gradient(grads, weights, block_input, gain, d_middle, owners):
    streams, rows, width = block_input.shape

    def body(d_ref, wq, wk, wv, x_ref, gain_ref, d_middle_ref, out):
        for stream in range(streams):
            d_normed = jnp.zeros((rows, width), jnp.float32)
            for kind, weight in enumerate((wq, wk, wv)):
                rows_of = slice(kind * HEAD_DIM, (kind + 1) * HEAD_DIM)
                flat = jnp.concatenate([d_ref[owner, rows_of] for owner in owners[stream]], axis=0)
                d_normed += dot(flat.T, weight[...], 1, 1)
            unit, root = normalize(x_ref[stream].astype(jnp.float32))
            d_values = normalize_back(d_normed, unit, root, gain_ref[...])
            out[stream] = d_middle_ref[stream * rows : (stream + 1) * rows] + d_values

    return pl.pallas_call(
        body,
        out_shape=jax.ShapeDtypeStruct(block_input.shape, jnp.float32),
        in_specs=[VMEM] * 7,
        out_specs=VMEM,
        compiler_params=LIMIT,
        cost_estimate=busy(0.2),
        name="input_gradient",
    )(grads, *weights, block_input, gain[None, :], d_middle)


def wide(ref, frame, spaces, first, last, count=1):
    return jnp.concatenate(
        [ref[frame * spaces + j, first:last, :] for j in range(spaces * count)], axis=1
    )


def attend(lo, packed, frames):
    devices, _, rows = packed.shape
    spaces = devices // frames
    per_frame = rows * spaces
    dim = HEAD_DIM

    def body(lo_ref, r_ref, o_ref, low_ref, lse_ref, kv, top, total, summed):
        def turn_keys(device, _):
            kv[pl.ds(pl.multiple_of(device * rows, rows), rows), :] = r_ref[device, dim:, :].T
            return 0

        lax.fori_loop(0, devices, turn_keys, 0, unroll=4)

        def group(queries, _):
            first = queries * CLIP
            query = [wide(r_ref, first + i, spaces, 0, dim) for i in range(CLIP)]

            def update(i, keys, scores, fresh):
                fold = lambda op, value: op(value.reshape(-1, 8, per_frame), axis=0)
                new_top = fold(jnp.max, scores[0])
                for part in scores[1:]:
                    new_top = jnp.maximum(new_top, fold(jnp.max, part))
                new_top = jnp.max(new_top, axis=0, keepdims=True)
                if not fresh:
                    old_top = top[i]
                    new_top = jnp.maximum(old_top, new_top)
                new_total, new_sum = 0.0, 0.0
                for j, part in enumerate(scores):
                    weights = jnp.exp(part - new_top)
                    new_total += fold(jnp.sum, weights)
                    values = wide(r_ref, keys * CLIP + j, spaces, 2 * dim, 3 * dim)
                    new_sum += dot(values, weights.astype(jnp.bfloat16), 1, 0)
                new_total = jnp.sum(new_total, axis=0, keepdims=True)
                if not fresh:
                    factor = jnp.exp(old_top - new_top)
                    new_total += total[i] * factor
                    new_sum += summed[i] * factor
                top[i] = new_top
                total[i] = new_total
                summed[i] = new_sum

            def against(keys, counts, fresh):
                scores = []
                for i, count in enumerate(counts):
                    rows_of = [
                        pl.ds(pl.multiple_of((keys * CLIP + j) * per_frame, per_frame), per_frame)
                        for j in range(count)
                    ]
                    scores.append([dot(kv[part, :dim], query[i], 1, 0) for part in rows_of])
                for i in range(CLIP):
                    update(i, keys, scores[i], fresh)

            against(queries, range(1, CLIP + 1), True)

            def earlier(keys, _):
                against(keys, [CLIP] * CLIP, False)
                return 0

            lax.fori_loop(lo_ref[first] // CLIP, queries, earlier, 0)
            for i in range(CLIP):
                out = summed[i] / total[i]
                for j in range(spaces):
                    piece = out[:, j * rows : (j + 1) * rows]
                    o_ref[(first + i) * spaces + j] = piece
                    low_ref[(first + i) * spaces + j] = piece.astype(jnp.bfloat16)
                lse_ref[first + i] = top[i] + jnp.log(total[i])
            return 0

        lax.fori_loop(0, frames // CLIP, group, 0)

    f32 = jnp.float32
    return pl.pallas_call(
        body,
        out_shape=(
            jax.ShapeDtypeStruct((devices, dim, rows), f32),
            jax.ShapeDtypeStruct((devices, dim, rows), jnp.bfloat16),
            jax.ShapeDtypeStruct((frames, 1, per_frame), f32),
            jax.ShapeDtypeStruct((devices * rows, 2 * dim), jnp.bfloat16),
        ),
        in_specs=[SMEM, VMEM],
        out_specs=(VMEM,) * 4,
        scratch_shapes=[
            pltpu.VMEM((CLIP, 1, per_frame), f32),
            pltpu.VMEM((CLIP, 1, per_frame), f32),
            pltpu.VMEM((CLIP, dim, per_frame), f32),
        ],
        compiler_params=LIMIT,
        cost_estimate=busy(28),
        name="attend",
    )(lo, packed)


def attend_back(hi, packed, d_own, lse, kv, tables, rest, frames, start, stop):
    devices, _, rows = packed.shape
    spaces = devices // frames
    per_frame = rows * spaces
    dim = HEAD_DIM
    last = stop * CLIP == frames
    f32 = jnp.float32
    shift = dim if last else 0
    base = 0 if last else start * CLIP * spaces

    def body(hi_ref, r_ref, d_ref, lse_ref, kv_ref, table_ref, *rest):
        if last:
            delta_ref, qd_ref, before, piece, where_ref, near_ref, far_ref, *rest = rest
            out, product_out, acc, left, d_query_ref, product, near, far, sems = rest
        else:
            o_ref, out, d_query_ref, qd_ref, delta_ref, acc, left = rest

        def begin(frame, _):
            d_query_ref[frame] = jnp.zeros((dim, per_frame), f32)
            for j in range(spaces):
                device = frame * spaces + j
                both = jnp.concatenate([r_ref[device, :dim, :], d_ref[device]], axis=0)
                qd_ref[pl.ds(pl.multiple_of(device * rows, rows), rows), :] = both.T
                delta_ref[frame, :, j * rows : (j + 1) * rows] = jnp.sum(
                    d_ref[device].astype(f32) * o_ref[device], axis=0, keepdims=True
                )
            return 0

        def fetch(pair, slot):
            plane = pair // 2
            entry = jnp.where(pair % 2 == 0, plane, frames // 2 - 1 - plane)
            return [
                pltpu.make_async_copy(source.at[pl.ds(2 * entry, 2)], target.at[slot], sems.at[slot, i])
                for i, (source, target) in enumerate(((near_ref, near), (far_ref, far)))
            ]

        if last:
            for copy in fetch(0, 0):
                copy.start()
            pltpu.sync_copy(before, d_query_ref)
        else:
            lax.fori_loop(0, frames, begin, 0, unroll=2)
        if last:
            out[: piece.shape[0], dim:, :] = piece[...]
        first_half = lax.broadcasted_iota(jnp.int32, (per_frame, 2 * dim), 1) < dim

        def group(keys, _):
            first = keys * CLIP
            for i in range(CLIP):
                rows_of = pl.ds(pl.multiple_of((first + i) * per_frame, per_frame), per_frame)
                both = kv_ref[rows_of, :]
                zero = jnp.zeros_like(both)
                left[i, :per_frame] = jnp.where(first_half, both, zero)
                left[i, per_frame:] = jnp.where(first_half, zero, both)

            def against(queries, lead, fresh):
                own = queries * CLIP
                d_scores = [[] for _ in range(CLIP)]
                right = []
                for n in range(CLIP):
                    d_rows = [d_ref[(own + n) * spaces + j] for j in range(spaces)]
                    both = [wide(r_ref, own + n, spaces, 0, dim), jnp.concatenate(d_rows, axis=1)]
                    right.append(jnp.concatenate(both, axis=0))
                for i in range(CLIP):
                    term = 0.0
                    taken = range(i if lead else 0, CLIP)
                    products = [dot(left[i], right[n], 1, 0) for n in taken]
                    pairs = []
                    for n, both in zip(taken, products):
                        weights = jnp.exp(both[:per_frame] - lse_ref[own + n])
                        change = weights * (both[per_frame:] - delta_ref[own + n])
                        d_scores[n].append(change.astype(jnp.bfloat16))
                        pairs.append(
                            jnp.concatenate([weights.astype(jnp.bfloat16), d_scores[n][-1]], axis=0)
                        )
                    for n, pair in zip(taken, pairs):
                        rows_of = pl.ds(pl.multiple_of((own + n) * per_frame, per_frame), per_frame)
                        term += dot(pair, qd_ref[rows_of, :], 1, 0)
                    if fresh:
                        acc[i] = term
                    else:
                        acc[i] += term
                for n in range(CLIP):
                    keys_of = [
                        wide(r_ref, first + i, spaces, dim, 2 * dim) for i in range(len(d_scores[n]))
                    ]
                    d_query_ref[own + n] += dot(
                        jnp.concatenate(keys_of, axis=1), jnp.concatenate(d_scores[n], axis=0), 1, 0
                    )

            against(keys, True, True)

            def later(queries, _):
                against(queries, False, False)
                return 0

            lax.fori_loop(keys + 1, hi_ref[first] // CLIP, later, 0)
            for i in range(CLIP):
                total = acc[i]
                d_key = total[per_frame:].T[:dim]
                d_key = turned(d_key, table_ref[first + i, 0], table_ref[first + i, 1], -1.0)
                d_key = d_key.astype(jnp.bfloat16)
                d_value = total[:per_frame].T[dim:].astype(jnp.bfloat16)
                for j in range(spaces):
                    device = (first + i) * spaces + j - base
                    columns = slice(j * rows, (j + 1) * rows)
                    out[device, shift : shift + dim, :] = d_key[:, columns]
                    out[device, shift + dim : shift + 2 * dim, :] = d_value[:, columns]
            return 0

        lax.fori_loop(start, stop, group, 0)
        if last:

            def finish(frame, _):
                whole_query = d_query_ref[frame] * (1.0 / math.sqrt(dim))
                whole_query = turned(whole_query, table_ref[frame, 0], table_ref[frame, 1], -1.0)
                whole_query = whole_query.astype(jnp.bfloat16)
                for j in range(spaces):
                    out[frame * spaces + j, :dim, :] = whole_query[:, j * rows : (j + 1) * rows]
                return 0

            lax.fori_loop(0, frames, finish, 0)

            core = where_ref[0]
            product[...] = jnp.zeros_like(product)

            def multiply(pair, _):
                slot = lax.rem(pair, 2)

                @pl.when(pair + 1 < frames // 2)
                def _():
                    for copy in fetch(pair + 1, 1 - slot):
                        copy.start()

                for copy in fetch(pair, slot):
                    copy.wait()
                lefts, rights = [], []
                for index in range(2):
                    frame = 2 * pair + index
                    lefts += [out[spaces * frame + core], out[spaces * frame + 1 - core]]
                    rights += [near[slot, index], far[slot, index]]
                product[...] += dot(
                    jnp.concatenate(lefts, axis=1), jnp.concatenate(rights, axis=0), 1, 0
                )
                return 0

            lax.fori_loop(0, frames // 2, multiply, 0)
            product_out[...] = product[...].astype(jnp.bfloat16)

    inputs = [hi, packed, d_own, lse, kv, tables, *rest]
    in_specs = [SMEM] + [VMEM] * 5
    query_sum = jax.ShapeDtypeStruct((frames, dim, per_frame), f32)
    scratch = [
        pltpu.VMEM((CLIP, 2 * per_frame, 2 * dim), f32),
        pltpu.VMEM((CLIP, 2 * per_frame, 2 * dim), jnp.bfloat16),
    ]
    if last:
        width = rest[-1].shape[2]
        in_specs += [VMEM, VMEM, ANY, VMEM, SMEM, ANY, ANY]
        out_shape = (
            jax.ShapeDtypeStruct((devices, 3 * dim, rows), jnp.bfloat16),
            jax.ShapeDtypeStruct((3 * dim, width), jnp.bfloat16),
        )
        scratch += [
            pltpu.VMEM((frames, dim, per_frame), f32),
            pltpu.VMEM((3 * dim, width), f32),
            pltpu.VMEM((2, 2, rows, width), jnp.bfloat16),
            pltpu.VMEM((2, 2, rows, width), jnp.bfloat16),
            pltpu.SemaphoreType.DMA((2, 2)),
        ]
    else:
        shape = ((stop - start) * CLIP * spaces, 2 * dim, rows)
        in_specs += [VMEM]
        out_shape = (
            jax.ShapeDtypeStruct(shape, jnp.bfloat16),
            query_sum,
            jax.ShapeDtypeStruct((devices * rows, 2 * dim), jnp.bfloat16),
            jax.ShapeDtypeStruct((frames, 1, per_frame), f32),
        )
    return pl.pallas_call(
        body,
        out_shape=out_shape,
        in_specs=in_specs,
        out_specs=(VMEM,) * len(out_shape),
        scratch_shapes=scratch,
        compiler_params=LIMIT,
        cost_estimate=busy(20),
        name="attend_back",
    )(*inputs)


def after(value, *others):
    return lax.optimization_barrier((value, *others))[0]


class Ring:
    def __init__(self):
        self.frames = lax.axis_size("frame")
        self.spaces = lax.axis_size("space")
        self.planes = self.frames // 4
        self.frame = lax.axis_index("frame")
        self.core = lax.axis_index("space")
        self.plane = self.frame // 4
        self.spot = self.frame % 4
        bits = (self.frame % 2, (self.frame // 2) % 2)
        self.first_bit = jnp.where(self.core == 0, bits[0], bits[1])
        self.second_bit = jnp.where(self.core == 0, bits[1], bits[0])

    def send(self, value, target):
        moves = []
        for frame in range(self.frames):
            for core in range(self.spaces):
                to_frame, to_core = target(frame, core)
                moves.append((frame * self.spaces + core, to_frame * self.spaces + to_core))
        return lax.ppermute(value, ("frame", "space"), moves)

    def first(self, value):
        return self.send(value, lambda frame, core: (frame ^ (1 if core == 0 else 2), core))

    def second(self, value):
        return self.send(value, lambda frame, core: (frame ^ (2 if core == 0 else 1), core))

    def across(self, value):
        return self.send(value, lambda frame, core: (frame, 1 - core))

    def up(self, value, step):
        size = self.frames
        return self.send(value, lambda frame, core: ((frame + 4 * step) % size, core))

    def send_planes(self, pieces):
        return [self.up(piece, step) for step, piece in enumerate(pieces[1:], 1)]

    def plane_part(self, value):
        groups = [list(range(spot, self.frames, 4)) for spot in range(4)]
        if value.shape[0] % (16 * self.planes):
            return lax.psum(value, "frame", axis_index_groups=groups)
        return lax.psum_scatter(
            value, "frame", scatter_dimension=0, axis_index_groups=groups, tiled=True
        )

    def add_planes(self, own, arrived):
        total = own.astype(jnp.float32)
        for piece in arrived:
            total = total + piece.astype(jnp.float32)
        return total.astype(jnp.bfloat16)

    def spread_planes(self, value, count):
        return [self.up(value, step) for step in range(1, count)]

    def gather_spots(self):
        near = jnp.where(self.core == 0, 2, 1)
        own = jnp.stack([self.spot, self.spot ^ near, self.spot ^ (3 - near), self.spot ^ 3])
        other = jnp.stack([self.spot, self.spot ^ (3 - near), self.spot ^ near, self.spot ^ 3])
        cores = jnp.repeat(jnp.stack([self.core, 1 - self.core]), 4)
        return jnp.concatenate([own, other]), cores

    def halves(self, value, bit):
        rows, columns = value.shape
        cut = value.reshape(2, rows // 2, columns)
        pick = lambda index: lax.dynamic_index_in_dim(cut, index, 0, keepdims=False)
        return pick(bit), pick(1 - bit).astype(jnp.bfloat16)


def frame_limits(clip_frames, frames):
    ends = jnp.cumsum(clip_frames, axis=1, dtype=jnp.int32)
    begins = ends - clip_frames
    index = jnp.arange(frames, dtype=jnp.int32)[None, :, None]
    inside = (index >= begins[:, None, :]) & (index < ends[:, None, :])
    pick = lambda table: jnp.sum(jnp.where(inside, table[:, None, :], 0), axis=2, dtype=jnp.int32)
    return pick(begins), pick(ends)


def local(
    block_input,
    norm1_gain,
    w_query,
    w_key,
    w_value,
    w_out,
    norm2_gain,
    w_up,
    w_down,
    clip_frames,
    cotangent,
):
    streams, rows, width = block_input.shape
    ring = Ring()
    frames, spaces, planes = ring.frames, ring.spaces, ring.planes
    devices = frames * spaces
    per_frame = rows * spaces
    tokens = streams * rows
    axes = ("frame", "space")
    low = jnp.bfloat16
    core = jnp.reshape(ring.core, (1,))
    spots, cores = ring.gather_spots()
    slots = 4 * spaces

    owners = head_owners(frames, spaces)
    w_projections = (w_query, w_key, w_value)
    side = ring.frame % 2

    def swap(value):
        return lax.all_to_all(value, axes, 0, 0, tiled=True)

    spot_of = jnp.stack([ring.frame, ring.core * rows])
    sent, normed = project(
        spot_of, clip_frames, block_input, norm1_gain, *w_projections, owners, devices, per_frame
    )
    packed = swap(sent)

    begin, end = frame_limits(after(clip_frames, sent), frames)
    frame_ids = jnp.arange(frames, dtype=jnp.int32)
    mine = ring.frame * spaces + ring.core
    idle = ~jnp.any(mine == jnp.asarray(owners))
    lo = jnp.where(idle, frame_ids, jnp.where(side == 0, begin[0], begin[1]))
    hi = jnp.where(idle, frame_ids, jnp.where(side == 0, end[0], end[1]))

    neighbour = lambda value: ring.send(value, lambda frame, core: (frame ^ 1, core))
    stream_near = neighbour(lax.dynamic_index_in_dim(normed, 1 - side, 0))
    stream_own = lax.dynamic_index_in_dim(normed, side, 0)
    stream_pair = jnp.where(
        side == 0,
        jnp.concatenate([stream_own, stream_near]),
        jnp.concatenate([stream_near, stream_own]),
    )
    up, down = range(planes), range(planes)[::-1]
    same_side = [
        [4 * plane + bit for plane in up] + [4 * plane + 2 + bit for plane in down] for bit in range(2)
    ]
    stream_mine = lax.all_gather(
        stream_pair, "frame", axis=0, tiled=True, axis_index_groups=same_side
    )
    cot_flat = cotangent.reshape(tokens, width)
    cot_one = ring.second(cot_flat)
    out, out_low, lse, kv = attend(lo, after(packed, stream_pair), frames)
    cot_pair = jnp.stack([cot_flat, after(cot_one, out_low)])
    attended = swap(after(out_low, cot_pair))
    tables = rope_tables(after(lo, out_low), frames, per_frame)
    attended = after(attended, tables)
    cot_far = ring.first(cot_pair)

    middle, two = attention_out(attended, block_input, w_out, norm2_gain, owners)
    chunk, skip = 512, 3
    cot_far = after(cot_far, middle)
    cot_plane = [cot_pair, cot_far, ring.across(cot_pair), ring.across(cot_far)]
    so_far = feed_first(two, cotangent, w_up, w_down, chunk, skip)
    two_pair = jnp.stack([two, ring.second(two)])
    so_far = after(so_far, two_pair, stream_mine)
    two_far = ring.first(two_pair)
    two_pair_other = ring.across(two_pair)
    block_output, d_middle, d_sent, out_keep, out_give = feed_rest(
        core, so_far, attended, middle, two, cotangent, w_out, norm2_gain, w_up, w_down,
        chunk, skip, owners,
    )
    d_own = swap(d_sent)
    two_far, two_pair_other = after((two_far, two_pair_other), d_sent)
    two_plane = [two_pair, two_far, two_pair_other, ring.across(two_far)]
    out_sum = out_keep + ring.across(out_give).astype(jnp.float32)
    out_keep, out_give = ring.halves(out_sum, ring.first_bit)
    out_other = ring.first(out_give)
    pieces = hidden_gradients(
        jnp.stack([ring.spot * spaces + ring.core, ring.plane]),
        after(two_plane, out_give), cot_plane, w_up, w_down, slots, planes,
    )

    arrived = ring.send_planes(pieces)
    out_sum = out_keep + after(out_other, pieces[0]).astype(jnp.float32)
    out_keep, out_give = ring.halves(out_sum, ring.second_bit)
    out_sum = (out_keep + ring.second(out_give).astype(jnp.float32)).astype(low)
    d_own = after(d_own, out_sum)
    out_sum = ring.plane_part(out_sum)
    groups = frames // CLIP
    first_part, d_query, qd, delta = attend_back(
        hi, packed, d_own, lse, kv, tables, (out,), frames, 0, groups // 2
    )
    total = ring.add_planes(pieces[0], after(arrived, first_part))
    stream_other = ring.across(stream_mine)
    grads, product = attend_back(
        hi, packed, d_own, lse, kv, tables,
        (after(delta, total, out_sum), qd, d_query, first_part, jnp.reshape(ring.core, (1,)),
         stream_mine, stream_other),
        frames, groups // 2, groups,
    )
    spread = ring.spread_planes(total, planes)
    own_one, own_two = ring.second(total), ring.first(total)
    spread, own_one, own_two, own_product = lax.optimization_barrier(
        (spread, own_one, own_two, product)
    )
    back = swap(grads)
    heads_sum = own_product.astype(jnp.float32) + neighbour(product).astype(jnp.float32)
    out_other = neighbour(out_sum)
    out_pair = jnp.where(
        side == 0,
        jnp.concatenate([out_sum, out_other], axis=1),
        jnp.concatenate([out_other, out_sum], axis=1),
    )
    heads_sum = jnp.concatenate([heads_sum.astype(low), out_pair])
    heads_mine = lax.all_gather(heads_sum, "frame", axis_index_groups=same_side)
    rest = after(jnp.concatenate(spread), heads_sum)
    one, two = (own_one, ring.second(rest)), (own_two, ring.first(rest))
    three = tuple(ring.first(part) for part in (one[0], after(one[1], back)))
    own = (total, rest)
    both_across = lambda pair: (ring.across(pair[0]), ring.across(pair[1]))
    own_other = both_across(own)
    grad_input = input_gradient(back, w_projections, block_input, norm1_gain, d_middle, owners)
    unit_slots = spots * spaces + cores
    where = jnp.stack([unit_slots, jnp.broadcast_to(ring.plane, cores.shape)])
    places = lambda *entries: jnp.stack([where[:, entry] for entry in entries], axis=1)
    placed = place_hidden(places(0, 4), [own, own_other], None, w_up, norm2_gain, planes, False)
    one, two = after((one, two), placed[0], grad_input)
    pieces = [one, two, both_across(one), both_across(two)]
    heads_other = ring.across(after(heads_mine, pieces))
    pieces = after(pieces, heads_mine)
    placed = place_hidden(places(1, 2, 5, 6), pieces, placed, w_up, norm2_gain, planes, False)
    grad_query, grad_key, grad_value, grad_out, gain_one = place_heads(
        jnp.reshape(ring.core, (1,)), heads_mine, after(heads_other, placed[0]),
        w_projections, norm1_gain, owners,
    )
    three = after(three, grad_query)
    three_other = both_across(three)
    grad_up, grad_down, gain_two = place_hidden(
        places(3, 7), [three, three_other], placed, w_up, norm2_gain, planes, True
    )
    return (
        block_output,
        grad_input,
        gain_one,
        grad_query,
        grad_key,
        grad_value,
        grad_out,
        gain_two,
        grad_up,
        grad_down,
    )


def solution(mesh):
    spread = P(None, ("frame", "space"), None)
    in_specs = (spread,) + (P(),) * 9 + (spread,)
    out_specs = (spread, spread) + (P(),) * 8
    return jax.shard_map(local, mesh=mesh, in_specs=in_specs, out_specs=out_specs, check_vma=False)
```

```python
import functools
import math

import jax
import jax.numpy as jnp
import numpy as np
from jax import lax
from jax.experimental import pallas as pl
from jax.experimental.pallas import tpu as pltpu
from jax.sharding import PartitionSpec as P

HEADS = 12
HEAD_DIM = 64
VMEM = pl.BlockSpec(memory_space=pltpu.VMEM)
ANY = pl.BlockSpec(memory_space=pl.ANY)
SMEM = pl.BlockSpec(memory_space=pltpu.SMEM)
LIMIT = pltpu.CompilerParams(vmem_limit_bytes=56 * 2**20)
FLOPS = 1.15e9


def busy(microseconds):
    return pl.CostEstimate(flops=int(microseconds * FLOPS), transcendentals=0, bytes_accessed=0)


CLIP = 4


def dot(left, right, left_dim, right_dim):
    return lax.dot_general(
        left,
        right,
        (((left_dim,), (right_dim,)), ((), ())),
        preferred_element_type=jnp.float32,
    )


def head_owners(frames, spaces):
    planes = frames // 4
    share = -(-HEADS // planes)
    return [
        [
            ((head // share) * 4 + (head % share) // spaces * 2 + stream) * spaces
            + (head % share) % spaces
            for head in range(HEADS)
        ]
        for stream in range(2)
    ]


def normalize(values):
    average = jnp.mean(values, axis=-1, keepdims=True)
    centred = values - average
    root = lax.rsqrt(jnp.mean(centred * centred, axis=-1, keepdims=True) + 1e-05)
    return centred * root, root


def normalize_back(d_scaled, unit, root, gain):
    d_unit = d_scaled * gain
    mean_one = jnp.mean(d_unit, axis=-1, keepdims=True)
    mean_two = jnp.mean(d_unit * unit, axis=-1, keepdims=True)
    return root * (d_unit - mean_one - unit * mean_two)


def frequencies(columns):
    half = HEAD_DIM // 2
    values = np.exp(np.arange(half) * (-2.0 * math.log(10000.0) / HEAD_DIM))
    return jnp.asarray(np.broadcast_to(values[:, None], (half, columns)), jnp.float32)


def turned(value, cosine, sine, sign):
    half = HEAD_DIM // 2
    first, second = value[:half], value[half:]
    return jnp.concatenate(
        [first * cosine - sign * second * sine, second * cosine + sign * first * sine], axis=0
    )


def project(place, clips, block_input, gain, w_query, w_key, w_value, owners, devices, per_frame):
    streams, rows, width = block_input.shape
    half = HEAD_DIM // 2
    low = jnp.bfloat16
    scale = 1.0 / math.sqrt(HEAD_DIM)
    owned = {device for row in owners for device in row}

    def body(place_ref, clips_ref, freq_ref, x_ref, gain_ref, wq, wk, wv, out, normed_out, table):
        frame, first_row = place_ref[0], place_ref[1]
        for stream in range(streams):
            begin = jnp.int32(0)
            running = jnp.int32(0)
            for clip in range(clips_ref.shape[1]):
                length = clips_ref[stream, clip]
                begin = jnp.where((frame >= running) & (frame < running + length), running, begin)
                running = running + length
            row = lax.broadcasted_iota(jnp.int32, (half, rows), 1)
            position = ((frame - begin) * per_frame + first_row + row).astype(jnp.float32)
            angles = position * freq_ref[...]
            table[0, stream] = jnp.cos(angles)
            table[1, stream] = jnp.sin(angles)
        values = x_ref[...].astype(jnp.float32).reshape(streams * rows, width)
        normed = (normalize(values)[0] * gain_ref[...][None, :]).astype(low)
        normed_out[...] = normed.reshape(streams, rows, width)
        for kind, weight in enumerate((wq, wk, wv)):
            product = dot(normed, weight[...], 1, 0).T
            for stream in range(streams):
                columns = slice(stream * rows, (stream + 1) * rows)
                for head in range(HEADS):
                    piece = product[head * HEAD_DIM : (head + 1) * HEAD_DIM, columns]
                    if kind < 2:
                        piece = turned(piece, table[0, stream], table[1, stream], 1.0)
                    if kind == 0:
                        piece = piece * scale
                    out[
                        owners[stream][head], kind * HEAD_DIM : (kind + 1) * HEAD_DIM, :
                    ] = piece.astype(low)
        for spare in range(devices):
            if spare not in owned:
                out[spare] = jnp.zeros((3 * HEAD_DIM, rows), low)

    return pl.pallas_call(
        body,
        out_shape=(
            jax.ShapeDtypeStruct((devices, 3 * HEAD_DIM, rows), low),
            jax.ShapeDtypeStruct((streams, rows, width), low),
        ),
        in_specs=[SMEM, SMEM] + [VMEM] * 6,
        out_specs=(VMEM, VMEM),
        scratch_shapes=[pltpu.VMEM((2, streams, half, rows), jnp.float32)],
        compiler_params=LIMIT,
        cost_estimate=busy(5),
        name="project",
    )(place, clips, frequencies(rows), block_input, gain, w_query, w_key, w_value)


def rope_tables(lo, frames, per_frame):
    half = HEAD_DIM // 2

    def body(lo_ref, freq_ref, out):
        def one(frame, _):
            row = lax.broadcasted_iota(jnp.int32, (half, per_frame), 1)
            position = ((frame - lo_ref[frame]) * per_frame + row).astype(jnp.float32)
            angles = position * freq_ref[...]
            out[frame, 0] = jnp.cos(angles)
            out[frame, 1] = jnp.sin(angles)
            return 0

        lax.fori_loop(0, frames, one, 0)

    return pl.pallas_call(
        body,
        out_shape=jax.ShapeDtypeStruct((frames, 2, half, per_frame), jnp.float32),
        in_specs=[SMEM, VMEM],
        out_specs=VMEM,
        compiler_params=LIMIT,
        cost_estimate=busy(4),
        name="rope_tables",
    )(lo, frequencies(per_frame))


GELU = math.sqrt(2.0 / math.pi)


def gelu_pair(value):
    square = value * value
    bent = jnp.tanh(GELU * value * (1.0 + 0.044715 * square))
    side = 0.5 * (1.0 + bent)
    slope = side + 0.5 * value * (1.0 - bent * bent) * (GELU * (1.0 + 3 * 0.044715 * square))
    return value * side, slope


def attention_out(attended, block_input, w_out, gain, owners):
    streams, rows, width = block_input.shape
    low = jnp.bfloat16

    def body(att, x_ref, wo, gain_ref, middle, two_ref):
        for stream in range(streams):
            rows_of = slice(stream * rows, (stream + 1) * rows)
            flat = jnp.concatenate([att[owner] for owner in owners[stream]], axis=0)
            values = x_ref[stream].astype(jnp.float32) + dot(flat.T, wo[...], 1, 0)
            middle[rows_of] = values
            two_ref[rows_of] = (normalize(values)[0] * gain_ref[...]).astype(low)

    return pl.pallas_call(
        body,
        out_shape=(
            jax.ShapeDtypeStruct((streams * rows, width), jnp.float32),
            jax.ShapeDtypeStruct((streams * rows, width), low),
        ),
        in_specs=[VMEM] * 4,
        out_specs=(VMEM, VMEM),
        compiler_params=LIMIT,
        cost_estimate=busy(3),
        name="attention_out",
    )(attended, block_input, w_out, gain[None, :])


def as_row(column):
    return jnp.broadcast_to(column, (column.shape[0], 128)).T[:1]


def whole(shape):
    return pl.BlockSpec(shape, lambda *indices: (0,) * len(shape))


def feed_first(two, cotangent, w_up, w_down, chunk, steps):
    tokens, width = two.shape
    low = jnp.bfloat16

    def body(two_ref, cot, up, down, result, d_two):
        cot_flat = cot[...].reshape(tokens, width)
        active, slope = gelu_pair(dot(two_ref[...], up[...], 1, 0))
        d_hidden = (dot(cot_flat, down[...], 1, 1) * slope).astype(low)
        forward = dot(active.astype(low), down[...], 1, 0)
        backward = dot(d_hidden, up[...], 1, 1)

        @pl.when(pl.program_id(0) == 0)
        def _():
            result[...] = forward
            d_two[...] = backward

        @pl.when(pl.program_id(0) > 0)
        def _():
            result[...] += forward
            d_two[...] += backward

    return pl.pallas_call(
        body,
        grid=(steps,),
        out_shape=(jax.ShapeDtypeStruct((tokens, width), jnp.float32),) * 2,
        in_specs=[
            whole(two.shape), whole(cotangent.shape),
            pl.BlockSpec((width, chunk), lambda i: (0, i)),
            pl.BlockSpec((chunk, width), lambda i: (i, 0)),
        ],
        out_specs=(whole((tokens, width)),) * 2,
        compiler_params=LIMIT,
        cost_estimate=busy(7),
        name="feed_first",
    )(two, cotangent, w_up, w_down)


def feed_rest(core, so_far, attended, middle, two, cotangent, w_out, gain, w_up, w_down, chunk, skip, owners):
    devices, head_width, rows = attended.shape
    streams, _, width = cotangent.shape
    tokens = streams * rows
    half = width // 2
    steps = w_up.shape[1] // chunk - skip
    low = jnp.bfloat16
    f32 = jnp.float32
    owned = {device for row in owners for device in row}

    def body(
        core_ref, first_result, first_two, att, middle, two_ref, cot, wo, gain_ref, up, down,
        result_ref, d_middle_ref, d_own, keep, give,
        result, d_two,
    ):
        step = pl.program_id(0)
        cot_flat = cot[...].reshape(tokens, width)
        active, slope = gelu_pair(dot(two_ref[...], up[...], 1, 0))
        d_hidden = (dot(cot_flat, down[...], 1, 1) * slope).astype(low)
        forward = dot(active.astype(low), down[...], 1, 0)
        backward = dot(d_hidden, up[...], 1, 1)

        @pl.when(step == 0)
        def _():
            result[...] = first_result[...] + forward
            d_two[...] = first_two[...] + backward

        @pl.when(step > 0)
        def _():
            result[...] += forward
            d_two[...] += backward

        @pl.when(step == steps - 1)
        def _():
            result_ref[...] = (middle[...] + result[...]).astype(low).reshape(streams, rows, width)
            unit, root = normalize(middle[...])
            d_middle = cot_flat.astype(f32) + normalize_back(
                d_two[...], unit, root, gain_ref[...]
            )
            d_middle_ref[...] = d_middle
            branch = d_middle.astype(low)
            d_att = dot(branch, wo[...], 1, 1).T.astype(low)
            total = jnp.zeros((width, width), f32)
            for stream in range(streams):
                rows_of = slice(stream * rows, (stream + 1) * rows)
                for head, owner in enumerate(owners[stream]):
                    d_own[owner] = d_att[head * HEAD_DIM : (head + 1) * HEAD_DIM, rows_of]
                flat = jnp.concatenate([att[owner] for owner in owners[stream]], axis=0)
                total += dot(flat, branch[rows_of], 1, 0)
            for spare in range(devices):
                if spare not in owned:
                    d_own[spare] = jnp.zeros((head_width, rows), low)
            first = core_ref[0] == 0
            keep[...] = jnp.where(first, total[:, :half], total[:, half:])
            give[...] = jnp.where(first, total[:, half:], total[:, :half]).astype(low)

    shapes = (
        ((streams, rows, width), low),
        ((tokens, width), f32),
        ((devices, head_width, rows), low),
        ((width, half), f32),
        ((width, half), low),
    )
    return pl.pallas_call(
        body,
        grid=(steps,),
        out_shape=tuple(jax.ShapeDtypeStruct(*entry) for entry in shapes),
        in_specs=[
            SMEM, whole((tokens, width)), whole((tokens, width)),
            whole(attended.shape), whole(middle.shape), whole(two.shape),
            whole(cotangent.shape), whole(w_out.shape), whole((1, width)),
            pl.BlockSpec((width, chunk), lambda i: (0, i + skip)),
            pl.BlockSpec((chunk, width), lambda i: (i + skip, 0)),
        ],
        out_specs=tuple(whole(shape) for shape, _ in shapes),
        scratch_shapes=[pltpu.VMEM((tokens, width), f32), pltpu.VMEM((tokens, width), f32)],
        compiler_params=LIMIT,
        cost_estimate=busy(10),
        name="feed_rest",
    )(core, *so_far, attended, middle, two, cotangent, w_out, gain[None, :], w_up, w_down)


def hidden_gradients(where, two, cot, w_up, w_down, slots, planes):
    _, tokens, width = two[0].shape
    count = len(two)
    hidden = w_up.shape[1] // slots
    rows = width // planes
    height = 2 * rows
    low = jnp.bfloat16

    def body(where_ref, *rest):
        two_refs, cot_refs, (up, down) = rest[:count], rest[count : 2 * count], rest[2 * count :][:2]
        rest = rest[2 * count + 2 :]
        outs, (up_sum, down_sum) = rest[:planes], rest[planes:]
        step = pl.program_id(0)

        def run(two_ref, cot_ref):
            two = two_ref[...].reshape(2 * tokens, width)
            cot = cot_ref[...].reshape(2 * tokens, width)
            active, slope = gelu_pair(dot(two, up[...], 1, 0))
            d_hidden = (dot(cot, down[...], 1, 1) * slope).astype(low)
            up_term = dot(two, d_hidden, 0, 0)
            down_term = dot(active.astype(low), cot, 0, 0)

            @pl.when(step == 0)
            def _():
                up_sum[...] = up_term
                down_sum[:hidden] = down_term[:, :hidden]
                down_sum[hidden:] = down_term[:, hidden:]

            @pl.when(step > 0)
            def _():
                up_sum[...] += up_term
                down_sum[:hidden] += down_term[:, :hidden]
                down_sum[hidden:] += down_term[:, hidden:]

        for index, refs in enumerate(zip(two_refs, cot_refs)):
            pl.when(step == index)(functools.partial(run, *refs))

        @pl.when(step == count - 1)
        def _():
            for index, out in enumerate(outs):
                plane = lax.rem(where_ref[1] + index, planes)
                rows_of = pl.ds(pl.multiple_of(plane * rows, rows), rows)
                out[:rows] = up_sum[rows_of, :].astype(low)
                out[rows:] = down_sum[rows_of, :].astype(low)

    return pl.pallas_call(
        body,
        grid_spec=pltpu.PrefetchScalarGridSpec(
            num_scalar_prefetch=1,
            grid=(count,),
            in_specs=[
                *[whole(two[0].shape)] * (2 * count),
                pl.BlockSpec((width, hidden), lambda i, where: (0, where[0])),
                pl.BlockSpec((hidden, width), lambda i, where: (where[0], 0)),
            ],
            out_specs=[whole((height, hidden))] * planes,
            scratch_shapes=[
                pltpu.VMEM((width, hidden), jnp.float32),
                pltpu.VMEM((width, hidden), jnp.float32),
            ],
        ),
        out_shape=[jax.ShapeDtypeStruct((height, hidden), low)] * planes,
        compiler_params=LIMIT,
        cost_estimate=busy(12),
        name="hidden_gradients",
    )(where, *two, *cot, w_up, w_down)


def place_hidden(where, pieces, placed, w_up, gain, planes, last):
    count = len(pieces)
    hidden = pieces[0][0].shape[1]
    width = w_up.shape[0]
    rows = width // planes
    f32 = jnp.float32
    second = placed is not None

    def body(where_ref, *rest):
        refs, (up_ref, gain_ref), rest = rest[: 2 * count], rest[2 * count :][:2], rest[2 * count + 2 :]
        gain_before = rest[2] if second else None
        up_out, down_out, gain_out, sums = rest[3:] if second else rest
        step = pl.program_id(0)

        def put(first_ref, others_ref):
            for index in range(planes):
                plane = lax.rem(where_ref[1, 0] + planes - index, planes)
                rows_of = pl.ds(pl.multiple_of(plane * rows, rows), rows)
                ref, first = (others_ref, 2 * rows * (index - 1)) if index else (first_ref, 0)
                up_out[rows_of, :] = ref[first : first + rows].astype(f32)
                down = ref[first + rows : first + 2 * rows].astype(f32)
                row = plane * rows
                held = pl.ds(pl.multiple_of(lax.rem(row, hidden), rows), rows)

                @pl.when(row < hidden)
                def _():
                    down_out[held, :hidden] = down

                @pl.when(row >= hidden)
                def _():
                    down_out[held, hidden:] = down

        for index in range(count):
            pl.when(step == index)(functools.partial(put, *refs[2 * index : 2 * index + 2]))
        terms = jnp.sum(up_out[...] * up_ref[...].astype(f32), axis=1, keepdims=True)

        @pl.when(step == 0)
        def _():
            sums[...] = terms

        @pl.when(step > 0)
        def _():
            sums[...] += terms

        @pl.when(step == count - 1)
        def _():
            row = as_row(sums[...])
            row = row + gain_before[...][None, :] if second else row
            gain_out[...] = (row / gain_ref[...])[0] if last else row[0]

    unused = [pl.BlockSpec(memory_space=pl.ANY)] * 2 + [whole((width,))]
    return pl.pallas_call(
        body,
        grid_spec=pltpu.PrefetchScalarGridSpec(
            num_scalar_prefetch=1,
            grid=(count,),
            in_specs=[whole(part.shape) for pair in pieces for part in pair]
            + [
                pl.BlockSpec((width, hidden), lambda i, where: (0, where[0, i])),
                whole((1, width)),
            ]
            + (unused if second else []),
            out_specs=[
                pl.BlockSpec((width, hidden), lambda i, where: (0, where[0, i])),
                pl.BlockSpec((hidden, width), lambda i, where: (where[0, i], 0)),
                whole((width,)),
            ],
            scratch_shapes=[pltpu.VMEM((width, 1), f32)],
        ),
        out_shape=[
            jax.ShapeDtypeStruct(w_up.shape, f32),
            jax.ShapeDtypeStruct(w_up.shape[::-1], f32),
            jax.ShapeDtypeStruct((width,), f32),
        ],
        input_output_aliases={2 * count + 3: 0, 2 * count + 4: 1} if second else {},
        compiler_params=LIMIT,
        cost_estimate=busy(0.2),
        name="place_hidden",
    )(where, *[part for pair in pieces for part in pair], w_up, gain[None, :], *(placed or []))


def place_heads(core, mine, other, weights, gain, owners):
    chips, height, width = mine.shape
    half = width // 2
    quarter = width // 4
    size = height - 3 * HEAD_DIM
    f32 = jnp.float32

    def body(core_ref, mine_ref, other_ref, wq, wk, wv, gain_ref, dq, dk, dv, out, gain_out):
        def rows_of_device(plane, row, core, rows):
            entry = chips - 1 - plane if row else plane
            own = core_ref[0] == core
            return jnp.where(own, mine_ref[entry, rows], other_ref[entry, rows])

        for spot in range(4):
            for core in range(2):
                first = (spot if core else spot % 2 * 2 + spot // 2) * quarter
                columns = slice(core * half, (core + 1) * half)
                held = slice(spot % 2 * half, (spot % 2 + 1) * half)
                for plane in range(quarter // size):
                    piece = rows_of_device(plane, spot // 2, core, slice(3 * HEAD_DIM, height))
                    rows_of = slice(first + plane * size, first + (plane + 1) * size)
                    out[rows_of, columns] = piece[:, held].astype(f32)
        terms = jnp.zeros((width, 1), f32)
        for kind, (weight, target) in enumerate(((wq, dq), (wk, dk), (wv, dv))):
            rows = slice(kind * HEAD_DIM, (kind + 1) * HEAD_DIM)
            pieces = [
                rows_of_device(owner // 8, owner // 4 % 2, owner % 2, rows) for owner in owners[0]
            ]
            grad = jnp.concatenate(pieces, axis=0).T.astype(f32)
            target[...] = grad
            terms += jnp.sum(grad * weight[...].astype(f32), axis=1, keepdims=True)
        gain_out[...] = (as_row(terms) / gain_ref[...])[0]

    return pl.pallas_call(
        body,
        out_shape=[jax.ShapeDtypeStruct((width, width), f32)] * 4
        + [jax.ShapeDtypeStruct((width,), f32)],
        in_specs=[SMEM] + [VMEM] * 6,
        out_specs=[VMEM] * 5,
        compiler_params=LIMIT,
        cost_estimate=busy(0.2),
        name="place_heads",
    )(core, mine, other, *weights, gain[None, :])


def input_gradient(grads, weights, block_input, gain, d_middle, owners):
    streams, rows, width = block_input.shape

    def body(d_ref, wq, wk, wv, x_ref, gain_ref, d_middle_ref, out):
        for stream in range(streams):
            d_normed = jnp.zeros((rows, width), jnp.float32)
            for kind, weight in enumerate((wq, wk, wv)):
                rows_of = slice(kind * HEAD_DIM, (kind + 1) * HEAD_DIM)
                flat = jnp.concatenate([d_ref[owner, rows_of] for owner in owners[stream]], axis=0)
                d_normed += dot(flat.T, weight[...], 1, 1)
            unit, root = normalize(x_ref[stream].astype(jnp.float32))
            d_values = normalize_back(d_normed, unit, root, gain_ref[...])
            out[stream] = d_middle_ref[stream * rows : (stream + 1) * rows] + d_values

    return pl.pallas_call(
        body,
        out_shape=jax.ShapeDtypeStruct(block_input.shape, jnp.float32),
        in_specs=[VMEM] * 7,
        out_specs=VMEM,
        compiler_params=LIMIT,
        cost_estimate=busy(0.2),
        name="input_gradient",
    )(grads, *weights, block_input, gain[None, :], d_middle)


def wide(ref, frame, spaces, first, last, count=1):
    return jnp.concatenate(
        [ref[frame * spaces + j, first:last, :] for j in range(spaces * count)], axis=1
    )


def attend(lo, packed, frames):
    devices, _, rows = packed.shape
    spaces = devices // frames
    per_frame = rows * spaces
    dim = HEAD_DIM

    def body(lo_ref, r_ref, o_ref, low_ref, lse_ref, kv, top, total, summed):
        def turn_keys(device, _):
            kv[pl.ds(pl.multiple_of(device * rows, rows), rows), :] = r_ref[device, dim:, :].T
            return 0

        lax.fori_loop(0, devices, turn_keys, 0, unroll=4)

        def group(queries, _):
            first = queries * CLIP
            query = [wide(r_ref, first + i, spaces, 0, dim) for i in range(CLIP)]

            def update(i, keys, scores, fresh):
                fold = lambda op, value: op(value.reshape(-1, 8, per_frame), axis=0)
                new_top = fold(jnp.max, scores[0])
                for part in scores[1:]:
                    new_top = jnp.maximum(new_top, fold(jnp.max, part))
                new_top = jnp.max(new_top, axis=0, keepdims=True)
                if not fresh:
                    old_top = top[i]
                    new_top = jnp.maximum(old_top, new_top)
                new_total, new_sum = 0.0, 0.0
                for j, part in enumerate(scores):
                    weights = jnp.exp(part - new_top)
                    new_total += fold(jnp.sum, weights)
                    values = wide(r_ref, keys * CLIP + j, spaces, 2 * dim, 3 * dim)
                    new_sum += dot(values, weights.astype(jnp.bfloat16), 1, 0)
                new_total = jnp.sum(new_total, axis=0, keepdims=True)
                if not fresh:
                    factor = jnp.exp(old_top - new_top)
                    new_total += total[i] * factor
                    new_sum += summed[i] * factor
                top[i] = new_top
                total[i] = new_total
                summed[i] = new_sum

            def against(keys, counts, fresh):
                scores = []
                for i, count in enumerate(counts):
                    rows_of = [
                        pl.ds(pl.multiple_of((keys * CLIP + j) * per_frame, per_frame), per_frame)
                        for j in range(count)
                    ]
                    scores.append([dot(kv[part, :dim], query[i], 1, 0) for part in rows_of])
                for i in range(CLIP):
                    update(i, keys, scores[i], fresh)

            against(queries, range(1, CLIP + 1), True)

            def earlier(keys, _):
                against(keys, [CLIP] * CLIP, False)
                return 0

            lax.fori_loop(lo_ref[first] // CLIP, queries, earlier, 0)
            for i in range(CLIP):
                out = summed[i] / total[i]
                for j in range(spaces):
                    piece = out[:, j * rows : (j + 1) * rows]
                    o_ref[(first + i) * spaces + j] = piece
                    low_ref[(first + i) * spaces + j] = piece.astype(jnp.bfloat16)
                lse_ref[first + i] = top[i] + jnp.log(total[i])
            return 0

        lax.fori_loop(0, frames // CLIP, group, 0)

    f32 = jnp.float32
    return pl.pallas_call(
        body,
        out_shape=(
            jax.ShapeDtypeStruct((devices, dim, rows), f32),
            jax.ShapeDtypeStruct((devices, dim, rows), jnp.bfloat16),
            jax.ShapeDtypeStruct((frames, 1, per_frame), f32),
            jax.ShapeDtypeStruct((devices * rows, 2 * dim), jnp.bfloat16),
        ),
        in_specs=[SMEM, VMEM],
        out_specs=(VMEM,) * 4,
        scratch_shapes=[
            pltpu.VMEM((CLIP, 1, per_frame), f32),
            pltpu.VMEM((CLIP, 1, per_frame), f32),
            pltpu.VMEM((CLIP, dim, per_frame), f32),
        ],
        compiler_params=LIMIT,
        cost_estimate=busy(28),
        name="attend",
    )(lo, packed)


def attend_back(hi, packed, d_own, lse, kv, tables, rest, frames, start, stop):
    devices, _, rows = packed.shape
    spaces = devices // frames
    per_frame = rows * spaces
    dim = HEAD_DIM
    last = stop * CLIP == frames
    f32 = jnp.float32
    shift = dim if last else 0
    base = 0 if last else start * CLIP * spaces

    def body(hi_ref, r_ref, d_ref, lse_ref, kv_ref, table_ref, *rest):
        if last:
            delta_ref, qd_ref, before, piece, where_ref, near_ref, far_ref, *rest = rest
            out, product_out, acc, left, d_query_ref, product, near, far, sems = rest
        else:
            o_ref, out, d_query_ref, qd_ref, delta_ref, acc, left = rest

        def begin(frame, _):
            d_query_ref[frame] = jnp.zeros((dim, per_frame), f32)
            for j in range(spaces):
                device = frame * spaces + j
                both = jnp.concatenate([r_ref[device, :dim, :], d_ref[device]], axis=0)
                qd_ref[pl.ds(pl.multiple_of(device * rows, rows), rows), :] = both.T
                delta_ref[frame, :, j * rows : (j + 1) * rows] = jnp.sum(
                    d_ref[device].astype(f32) * o_ref[device], axis=0, keepdims=True
                )
            return 0

        def fetch(pair, slot):
            plane = pair // 2
            entry = jnp.where(pair % 2 == 0, plane, frames // 2 - 1 - plane)
            return [
                pltpu.make_async_copy(source.at[pl.ds(2 * entry, 2)], target.at[slot], sems.at[slot, i])
                for i, (source, target) in enumerate(((near_ref, near), (far_ref, far)))
            ]

        if last:
            for copy in fetch(0, 0):
                copy.start()
            pltpu.sync_copy(before, d_query_ref)
        else:
            lax.fori_loop(0, frames, begin, 0, unroll=2)
        if last:
            out[: piece.shape[0], dim:, :] = piece[...]
        first_half = lax.broadcasted_iota(jnp.int32, (per_frame, 2 * dim), 1) < dim

        def group(keys, _):
            first = keys * CLIP
            for i in range(CLIP):
                rows_of = pl.ds(pl.multiple_of((first + i) * per_frame, per_frame), per_frame)
                both = kv_ref[rows_of, :]
                zero = jnp.zeros_like(both)
                left[i, :per_frame] = jnp.where(first_half, both, zero)
                left[i, per_frame:] = jnp.where(first_half, zero, both)

            def against(queries, lead, fresh):
                own = queries * CLIP
                d_scores = [[] for _ in range(CLIP)]
                right = []
                for n in range(CLIP):
                    d_rows = [d_ref[(own + n) * spaces + j] for j in range(spaces)]
                    both = [wide(r_ref, own + n, spaces, 0, dim), jnp.concatenate(d_rows, axis=1)]
                    right.append(jnp.concatenate(both, axis=0))
                for i in range(CLIP):
                    term = 0.0
                    taken = range(i if lead else 0, CLIP)
                    products = [dot(left[i], right[n], 1, 0) for n in taken]
                    pairs = []
                    for n, both in zip(taken, products):
                        weights = jnp.exp(both[:per_frame] - lse_ref[own + n])
                        change = weights * (both[per_frame:] - delta_ref[own + n])
                        d_scores[n].append(change.astype(jnp.bfloat16))
                        pairs.append(
                            jnp.concatenate([weights.astype(jnp.bfloat16), d_scores[n][-1]], axis=0)
                        )
                    for n, pair in zip(taken, pairs):
                        rows_of = pl.ds(pl.multiple_of((own + n) * per_frame, per_frame), per_frame)
                        term += dot(pair, qd_ref[rows_of, :], 1, 0)
                    if fresh:
                        acc[i] = term
                    else:
                        acc[i] += term
                for n in range(CLIP):
                    keys_of = [
                        wide(r_ref, first + i, spaces, dim, 2 * dim) for i in range(len(d_scores[n]))
                    ]
                    d_query_ref[own + n] += dot(
                        jnp.concatenate(keys_of, axis=1), jnp.concatenate(d_scores[n], axis=0), 1, 0
                    )

            against(keys, True, True)

            def later(queries, _):
                against(queries, False, False)
                return 0

            lax.fori_loop(keys + 1, hi_ref[first] // CLIP, later, 0)
            for i in range(CLIP):
                total = acc[i]
                d_key = total[per_frame:].T[:dim]
                d_key = turned(d_key, table_ref[first + i, 0], table_ref[first + i, 1], -1.0)
                d_key = d_key.astype(jnp.bfloat16)
                d_value = total[:per_frame].T[dim:].astype(jnp.bfloat16)
                for j in range(spaces):
                    device = (first + i) * spaces + j - base
                    columns = slice(j * rows, (j + 1) * rows)
                    out[device, shift : shift + dim, :] = d_key[:, columns]
                    out[device, shift + dim : shift + 2 * dim, :] = d_value[:, columns]
            return 0

        lax.fori_loop(start, stop, group, 0)
        if last:

            def finish(frame, _):
                whole_query = d_query_ref[frame] * (1.0 / math.sqrt(dim))
                whole_query = turned(whole_query, table_ref[frame, 0], table_ref[frame, 1], -1.0)
                whole_query = whole_query.astype(jnp.bfloat16)
                for j in range(spaces):
                    out[frame * spaces + j, :dim, :] = whole_query[:, j * rows : (j + 1) * rows]
                return 0

            lax.fori_loop(0, frames, finish, 0)

            core = where_ref[0]
            product[...] = jnp.zeros_like(product)

            def multiply(pair, _):
                slot = lax.rem(pair, 2)

                @pl.when(pair + 1 < frames // 2)
                def _():
                    for copy in fetch(pair + 1, 1 - slot):
                        copy.start()

                for copy in fetch(pair, slot):
                    copy.wait()
                lefts, rights = [], []
                for index in range(2):
                    frame = 2 * pair + index
                    lefts += [out[spaces * frame + core], out[spaces * frame + 1 - core]]
                    rights += [near[slot, index], far[slot, index]]
                product[...] += dot(
                    jnp.concatenate(lefts, axis=1), jnp.concatenate(rights, axis=0), 1, 0
                )
                return 0

            lax.fori_loop(0, frames // 2, multiply, 0)
            product_out[...] = product[...].astype(jnp.bfloat16)

    inputs = [hi, packed, d_own, lse, kv, tables, *rest]
    in_specs = [SMEM] + [VMEM] * 5
    query_sum = jax.ShapeDtypeStruct((frames, dim, per_frame), f32)
    scratch = [
        pltpu.VMEM((CLIP, 2 * per_frame, 2 * dim), f32),
        pltpu.VMEM((CLIP, 2 * per_frame, 2 * dim), jnp.bfloat16),
    ]
    if last:
        width = rest[-1].shape[2]
        in_specs += [VMEM, VMEM, ANY, VMEM, SMEM, ANY, ANY]
        out_shape = (
            jax.ShapeDtypeStruct((devices, 3 * dim, rows), jnp.bfloat16),
            jax.ShapeDtypeStruct((3 * dim, width), jnp.bfloat16),
        )
        scratch += [
            pltpu.VMEM((frames, dim, per_frame), f32),
            pltpu.VMEM((3 * dim, width), f32),
            pltpu.VMEM((2, 2, rows, width), jnp.bfloat16),
            pltpu.VMEM((2, 2, rows, width), jnp.bfloat16),
            pltpu.SemaphoreType.DMA((2, 2)),
        ]
    else:
        shape = ((stop - start) * CLIP * spaces, 2 * dim, rows)
        in_specs += [VMEM]
        out_shape = (
            jax.ShapeDtypeStruct(shape, jnp.bfloat16),
            query_sum,
            jax.ShapeDtypeStruct((devices * rows, 2 * dim), jnp.bfloat16),
            jax.ShapeDtypeStruct((frames, 1, per_frame), f32),
        )
    return pl.pallas_call(
        body,
        out_shape=out_shape,
        in_specs=in_specs,
        out_specs=(VMEM,) * len(out_shape),
        scratch_shapes=scratch,
        compiler_params=LIMIT,
        cost_estimate=busy(20),
        name="attend_back",
    )(*inputs)


def after(value, *others):
    return lax.optimization_barrier((value, *others))[0]


class Ring:
    def __init__(self):
        self.frames = lax.axis_size("frame")
        self.spaces = lax.axis_size("space")
        self.planes = self.frames // 4
        self.frame = lax.axis_index("frame")
        self.core = lax.axis_index("space")
        self.plane = self.frame // 4
        self.spot = self.frame % 4
        bits = (self.frame % 2, (self.frame // 2) % 2)
        self.first_bit = jnp.where(self.core == 0, bits[0], bits[1])
        self.second_bit = jnp.where(self.core == 0, bits[1], bits[0])

    def send(self, value, target):
        moves = []
        for frame in range(self.frames):
            for core in range(self.spaces):
                to_frame, to_core = target(frame, core)
                moves.append((frame * self.spaces + core, to_frame * self.spaces + to_core))
        return lax.ppermute(value, ("frame", "space"), moves)

    def first(self, value):
        return self.send(value, lambda frame, core: (frame ^ (1 if core == 0 else 2), core))

    def second(self, value):
        return self.send(value, lambda frame, core: (frame ^ (2 if core == 0 else 1), core))

    def across(self, value):
        return self.send(value, lambda frame, core: (frame, 1 - core))

    def up(self, value, step):
        size = self.frames
        return self.send(value, lambda frame, core: ((frame + 4 * step) % size, core))

    def send_planes(self, pieces):
        return [self.up(piece, step) for step, piece in enumerate(pieces[1:], 1)]

    def plane_part(self, value):
        groups = [list(range(spot, self.frames, 4)) for spot in range(4)]
        if value.shape[0] % (16 * self.planes):
            return lax.psum(value, "frame", axis_index_groups=groups)
        return lax.psum_scatter(
            value, "frame", scatter_dimension=0, axis_index_groups=groups, tiled=True
        )

    def add_planes(self, own, arrived):
        total = own.astype(jnp.float32)
        for piece in arrived:
            total = total + piece.astype(jnp.float32)
        return total.astype(jnp.bfloat16)

    def spread_planes(self, value, count):
        return [self.up(value, step) for step in range(1, count)]

    def gather_spots(self):
        near = jnp.where(self.core == 0, 2, 1)
        own = jnp.stack([self.spot, self.spot ^ near, self.spot ^ (3 - near), self.spot ^ 3])
        other = jnp.stack([self.spot, self.spot ^ (3 - near), self.spot ^ near, self.spot ^ 3])
        cores = jnp.repeat(jnp.stack([self.core, 1 - self.core]), 4)
        return jnp.concatenate([own, other]), cores

    def halves(self, value, bit):
        rows, columns = value.shape
        cut = value.reshape(2, rows // 2, columns)
        pick = lambda index: lax.dynamic_index_in_dim(cut, index, 0, keepdims=False)
        return pick(bit), pick(1 - bit).astype(jnp.bfloat16)


def frame_limits(clip_frames, frames):
    ends = jnp.cumsum(clip_frames, axis=1, dtype=jnp.int32)
    begins = ends - clip_frames
    index = jnp.arange(frames, dtype=jnp.int32)[None, :, None]
    inside = (index >= begins[:, None, :]) & (index < ends[:, None, :])
    pick = lambda table: jnp.sum(jnp.where(inside, table[:, None, :], 0), axis=2, dtype=jnp.int32)
    return pick(begins), pick(ends)


def local(
    block_input,
    norm1_gain,
    w_query,
    w_key,
    w_value,
    w_out,
    norm2_gain,
    w_up,
    w_down,
    clip_frames,
    cotangent,
):
    streams, rows, width = block_input.shape
    ring = Ring()
    frames, spaces, planes = ring.frames, ring.spaces, ring.planes
    devices = frames * spaces
    per_frame = rows * spaces
    tokens = streams * rows
    axes = ("frame", "space")
    low = jnp.bfloat16
    core = jnp.reshape(ring.core, (1,))
    spots, cores = ring.gather_spots()
    slots = 4 * spaces

    owners = head_owners(frames, spaces)
    w_projections = (w_query, w_key, w_value)
    side = ring.frame % 2

    def swap(value):
        return lax.all_to_all(value, axes, 0, 0, tiled=True)

    spot_of = jnp.stack([ring.frame, ring.core * rows])
    sent, normed = project(
        spot_of, clip_frames, block_input, norm1_gain, *w_projections, owners, devices, per_frame
    )
    packed = swap(sent)

    begin, end = frame_limits(after(clip_frames, sent), frames)
    frame_ids = jnp.arange(frames, dtype=jnp.int32)
    mine = ring.frame * spaces + ring.core
    idle = ~jnp.any(mine == jnp.asarray(owners))
    lo = jnp.where(idle, frame_ids, jnp.where(side == 0, begin[0], begin[1]))
    hi = jnp.where(idle, frame_ids, jnp.where(side == 0, end[0], end[1]))

    neighbour = lambda value: ring.send(value, lambda frame, core: (frame ^ 1, core))
    stream_near = neighbour(lax.dynamic_index_in_dim(normed, 1 - side, 0))
    stream_own = lax.dynamic_index_in_dim(normed, side, 0)
    stream_pair = jnp.where(
        side == 0,
        jnp.concatenate([stream_own, stream_near]),
        jnp.concatenate([stream_near, stream_own]),
    )
    up, down = range(planes), range(planes)[::-1]
    same_side = [
        [4 * plane + bit for plane in up] + [4 * plane + 2 + bit for plane in down] for bit in range(2)
    ]
    stream_mine = lax.all_gather(
        stream_pair, "frame", axis=0, tiled=True, axis_index_groups=same_side
    )
    cot_flat = cotangent.reshape(tokens, width)
    cot_one = ring.second(cot_flat)
    out, out_low, lse, kv = attend(lo, after(packed, stream_pair), frames)
    cot_pair = jnp.stack([cot_flat, after(cot_one, out_low)])
    attended = swap(after(out_low, cot_pair))
    tables = rope_tables(after(lo, out_low), frames, per_frame)
    attended = after(attended, tables)
    cot_far = ring.first(cot_pair)

    middle, two = attention_out(attended, block_input, w_out, norm2_gain, owners)
    chunk, skip = 768, 2
    cot_far = after(cot_far, middle)
    cot_plane = [cot_pair, cot_far, ring.across(cot_pair), ring.across(cot_far)]
    so_far = feed_first(two, cotangent, w_up, w_down, chunk, skip)
    two_pair = jnp.stack([two, ring.second(two)])
    so_far = after(so_far, two_pair, stream_mine)
    two_far = ring.first(two_pair)
    two_pair_other = ring.across(two_pair)
    block_output, d_middle, d_sent, out_keep, out_give = feed_rest(
        core, so_far, attended, middle, two, cotangent, w_out, norm2_gain, w_up, w_down,
        chunk, skip, owners,
    )
    d_own = swap(d_sent)
    two_far, two_pair_other = after((two_far, two_pair_other), d_sent)
    two_plane = [two_pair, two_far, two_pair_other, ring.across(two_far)]
    out_sum = out_keep + ring.across(out_give).astype(jnp.float32)
    out_keep, out_give = ring.halves(out_sum, ring.first_bit)
    out_other = ring.first(out_give)
    pieces = hidden_gradients(
        jnp.stack([ring.spot * spaces + ring.core, ring.plane]),
        after(two_plane, out_give), cot_plane, w_up, w_down, slots, planes,
    )

    arrived = ring.send_planes(pieces)
    out_sum = out_keep + after(out_other, pieces[0]).astype(jnp.float32)
    out_keep, out_give = ring.halves(out_sum, ring.second_bit)
    out_sum = (out_keep + ring.second(out_give).astype(jnp.float32)).astype(low)
    d_own = after(d_own, out_sum)
    out_sum = ring.plane_part(out_sum)
    groups = frames // CLIP
    first_part, d_query, qd, delta = attend_back(
        hi, packed, d_own, lse, kv, tables, (out,), frames, 0, groups // 2
    )
    total = ring.add_planes(pieces[0], after(arrived, first_part))
    stream_other = ring.across(stream_mine)
    grads, product = attend_back(
        hi, packed, d_own, lse, kv, tables,
        (after(delta, total, out_sum), qd, d_query, first_part, jnp.reshape(ring.core, (1,)),
         stream_mine, stream_other),
        frames, groups // 2, groups,
    )
    spread = ring.spread_planes(total, planes)
    own_one, own_two = ring.second(total), ring.first(total)
    spread, own_one, own_two, own_product = lax.optimization_barrier(
        (spread, own_one, own_two, product)
    )
    back = swap(grads)
    heads_sum = own_product.astype(jnp.float32) + neighbour(product).astype(jnp.float32)
    out_other = neighbour(out_sum)
    out_pair = jnp.where(
        side == 0,
        jnp.concatenate([out_sum, out_other], axis=1),
        jnp.concatenate([out_other, out_sum], axis=1),
    )
    heads_sum = jnp.concatenate([heads_sum.astype(low), out_pair])
    heads_mine = lax.all_gather(heads_sum, "frame", axis_index_groups=same_side)
    rest = after(jnp.concatenate(spread), heads_sum)
    one, two = (own_one, ring.second(rest)), (own_two, ring.first(rest))
    three = tuple(ring.first(part) for part in (one[0], after(one[1], back)))
    own = (total, rest)
    both_across = lambda pair: (ring.across(pair[0]), ring.across(pair[1]))
    own_other = both_across(own)
    grad_input = input_gradient(back, w_projections, block_input, norm1_gain, d_middle, owners)
    unit_slots = spots * spaces + cores
    where = jnp.stack([unit_slots, jnp.broadcast_to(ring.plane, cores.shape)])
    places = lambda *entries: jnp.stack([where[:, entry] for entry in entries], axis=1)
    placed = place_hidden(places(0, 4), [own, own_other], None, w_up, norm2_gain, planes, False)
    one, two = after((one, two), placed[0], grad_input)
    pieces = [both_across(one), both_across(two)]
    placed = place_hidden(places(1, 2), [one, two], placed, w_up, norm2_gain, planes, False)
    pieces, heads_mine = after((pieces, heads_mine), placed[0])
    heads_other = ring.across(after(heads_mine, pieces))
    pieces = after(pieces, heads_mine)
    placed = place_hidden(places(5, 6), pieces, placed, w_up, norm2_gain, planes, False)
    grad_query, grad_key, grad_value, grad_out, gain_one = place_heads(
        jnp.reshape(ring.core, (1,)), heads_mine, after(heads_other, placed[0]),
        w_projections, norm1_gain, owners,
    )
    three = after(three, grad_query)
    three_other = both_across(three)
    grad_up, grad_down, gain_two = place_hidden(
        places(3, 7), [three, three_other], placed, w_up, norm2_gain, planes, True
    )
    return (
        block_output,
        grad_input,
        gain_one,
        grad_query,
        grad_key,
        grad_value,
        grad_out,
        gain_two,
        grad_up,
        grad_down,
    )


def solution(mesh):
    spread = P(None, ("frame", "space"), None)
    in_specs = (spread,) + (P(),) * 9 + (spread,)
    out_specs = (spread, spread) + (P(),) * 8
    return jax.shard_map(local, mesh=mesh, in_specs=in_specs, out_specs=out_specs, check_vma=False)
```

```python
import functools
import math

import jax
import jax.numpy as jnp
import numpy as np
from jax import lax
from jax.experimental import pallas as pl
from jax.experimental.pallas import tpu as pltpu
from jax.sharding import PartitionSpec as P

HEADS = 12
HEAD_DIM = 64
VMEM = pl.BlockSpec(memory_space=pltpu.VMEM)
ANY = pl.BlockSpec(memory_space=pl.ANY)
SMEM = pl.BlockSpec(memory_space=pltpu.SMEM)
LIMIT = pltpu.CompilerParams(vmem_limit_bytes=56 * 2**20)
FLOPS = 1.15e9


def busy(microseconds):
    return pl.CostEstimate(flops=int(microseconds * FLOPS), transcendentals=0, bytes_accessed=0)


CLIP = 4


def dot(left, right, left_dim, right_dim):
    return lax.dot_general(
        left,
        right,
        (((left_dim,), (right_dim,)), ((), ())),
        preferred_element_type=jnp.float32,
    )


def head_owners(frames, spaces):
    planes = frames // 4
    share = -(-HEADS // planes)
    return [
        [
            ((head // share) * 4 + (head % share) // spaces * 2 + stream) * spaces
            + (head % share) % spaces
            for head in range(HEADS)
        ]
        for stream in range(2)
    ]


def normalize(values):
    average = jnp.mean(values, axis=-1, keepdims=True)
    centred = values - average
    root = lax.rsqrt(jnp.mean(centred * centred, axis=-1, keepdims=True) + 1e-05)
    return centred * root, root


def normalize_back(d_scaled, unit, root, gain):
    d_unit = d_scaled * gain
    mean_one = jnp.mean(d_unit, axis=-1, keepdims=True)
    mean_two = jnp.mean(d_unit * unit, axis=-1, keepdims=True)
    return root * (d_unit - mean_one - unit * mean_two)


def frequencies(columns):
    half = HEAD_DIM // 2
    values = np.exp(np.arange(half) * (-2.0 * math.log(10000.0) / HEAD_DIM))
    return jnp.asarray(np.broadcast_to(values[:, None], (half, columns)), jnp.float32)


def turned(value, cosine, sine, sign):
    half = HEAD_DIM // 2
    first, second = value[:half], value[half:]
    return jnp.concatenate(
        [first * cosine - sign * second * sine, second * cosine + sign * first * sine], axis=0
    )


def project(place, clips, block_input, gain, w_query, w_key, w_value, owners, devices, per_frame):
    streams, rows, width = block_input.shape
    half = HEAD_DIM // 2
    low = jnp.bfloat16
    scale = 1.0 / math.sqrt(HEAD_DIM)
    owned = {device for row in owners for device in row}

    def body(place_ref, clips_ref, freq_ref, x_ref, gain_ref, wq, wk, wv, out, normed_out, table):
        frame, first_row = place_ref[0], place_ref[1]
        for stream in range(streams):
            begin = jnp.int32(0)
            running = jnp.int32(0)
            for clip in range(clips_ref.shape[1]):
                length = clips_ref[stream, clip]
                begin = jnp.where((frame >= running) & (frame < running + length), running, begin)
                running = running + length
            row = lax.broadcasted_iota(jnp.int32, (half, rows), 1)
            position = ((frame - begin) * per_frame + first_row + row).astype(jnp.float32)
            angles = position * freq_ref[...]
            table[0, stream] = jnp.cos(angles)
            table[1, stream] = jnp.sin(angles)
        values = x_ref[...].astype(jnp.float32).reshape(streams * rows, width)
        normed = (normalize(values)[0] * gain_ref[...][None, :]).astype(low)
        normed_out[...] = normed.reshape(streams, rows, width)
        for kind, weight in enumerate((wq, wk, wv)):
            product = dot(normed, weight[...], 1, 0).T
            for stream in range(streams):
                columns = slice(stream * rows, (stream + 1) * rows)
                for head in range(HEADS):
                    piece = product[head * HEAD_DIM : (head + 1) * HEAD_DIM, columns]
                    if kind < 2:
                        piece = turned(piece, table[0, stream], table[1, stream], 1.0)
                    if kind == 0:
                        piece = piece * scale
                    out[
                        owners[stream][head], kind * HEAD_DIM : (kind + 1) * HEAD_DIM, :
                    ] = piece.astype(low)
        for spare in range(devices):
            if spare not in owned:
                out[spare] = jnp.zeros((3 * HEAD_DIM, rows), low)

    return pl.pallas_call(
        body,
        out_shape=(
            jax.ShapeDtypeStruct((devices, 3 * HEAD_DIM, rows), low),
            jax.ShapeDtypeStruct((streams, rows, width), low),
        ),
        in_specs=[SMEM, SMEM] + [VMEM] * 6,
        out_specs=(VMEM, VMEM),
        scratch_shapes=[pltpu.VMEM((2, streams, half, rows), jnp.float32)],
        compiler_params=LIMIT,
        cost_estimate=busy(5),
        name="project",
    )(place, clips, frequencies(rows), block_input, gain, w_query, w_key, w_value)


def rope_tables(lo, frames, per_frame):
    half = HEAD_DIM // 2

    def body(lo_ref, freq_ref, out):
        def one(frame, _):
            row = lax.broadcasted_iota(jnp.int32, (half, per_frame), 1)
            position = ((frame - lo_ref[frame]) * per_frame + row).astype(jnp.float32)
            angles = position * freq_ref[...]
            out[frame, 0] = jnp.cos(angles)
            out[frame, 1] = jnp.sin(angles)
            return 0

        lax.fori_loop(0, frames, one, 0)

    return pl.pallas_call(
        body,
        out_shape=jax.ShapeDtypeStruct((frames, 2, half, per_frame), jnp.float32),
        in_specs=[SMEM, VMEM],
        out_specs=VMEM,
        compiler_params=LIMIT,
        cost_estimate=busy(4),
        name="rope_tables",
    )(lo, frequencies(per_frame))


GELU = math.sqrt(2.0 / math.pi)


def gelu_pair(value):
    square = value * value
    bent = jnp.tanh(GELU * value * (1.0 + 0.044715 * square))
    side = 0.5 * (1.0 + bent)
    slope = side + 0.5 * value * (1.0 - bent * bent) * (GELU * (1.0 + 3 * 0.044715 * square))
    return value * side, slope


def attention_out(attended, block_input, w_out, gain, owners):
    streams, rows, width = block_input.shape
    low = jnp.bfloat16

    def body(att, x_ref, wo, gain_ref, middle, two_ref):
        for stream in range(streams):
            rows_of = slice(stream * rows, (stream + 1) * rows)
            flat = jnp.concatenate([att[owner] for owner in owners[stream]], axis=0)
            values = x_ref[stream].astype(jnp.float32) + dot(flat.T, wo[...], 1, 0)
            middle[rows_of] = values
            two_ref[rows_of] = (normalize(values)[0] * gain_ref[...]).astype(low)

    return pl.pallas_call(
        body,
        out_shape=(
            jax.ShapeDtypeStruct((streams * rows, width), jnp.float32),
            jax.ShapeDtypeStruct((streams * rows, width), low),
        ),
        in_specs=[VMEM] * 4,
        out_specs=(VMEM, VMEM),
        compiler_params=LIMIT,
        cost_estimate=busy(3),
        name="attention_out",
    )(attended, block_input, w_out, gain[None, :])


def as_row(column):
    return jnp.broadcast_to(column, (column.shape[0], 128)).T[:1]


def whole(shape):
    return pl.BlockSpec(shape, lambda *indices: (0,) * len(shape))


def feed_first(two, cotangent, w_up, w_down, chunk, steps):
    tokens, width = two.shape
    low = jnp.bfloat16

    def body(two_ref, cot, up, down, result, d_two):
        cot_flat = cot[...].reshape(tokens, width)
        active, slope = gelu_pair(dot(two_ref[...], up[...], 1, 0))
        d_hidden = (dot(cot_flat, down[...], 1, 1) * slope).astype(low)
        forward = dot(active.astype(low), down[...], 1, 0)
        backward = dot(d_hidden, up[...], 1, 1)

        @pl.when(pl.program_id(0) == 0)
        def _():
            result[...] = forward
            d_two[...] = backward

        @pl.when(pl.program_id(0) > 0)
        def _():
            result[...] += forward
            d_two[...] += backward

    return pl.pallas_call(
        body,
        grid=(steps,),
        out_shape=(jax.ShapeDtypeStruct((tokens, width), jnp.float32),) * 2,
        in_specs=[
            whole(two.shape), whole(cotangent.shape),
            pl.BlockSpec((width, chunk), lambda i: (0, i)),
            pl.BlockSpec((chunk, width), lambda i: (i, 0)),
        ],
        out_specs=(whole((tokens, width)),) * 2,
        compiler_params=LIMIT,
        cost_estimate=busy(7),
        name="feed_first",
    )(two, cotangent, w_up, w_down)


def feed_rest(core, so_far, attended, middle, two, cotangent, w_out, gain, w_up, w_down, chunk, skip, owners):
    devices, head_width, rows = attended.shape
    streams, _, width = cotangent.shape
    tokens = streams * rows
    half = width // 2
    steps = w_up.shape[1] // chunk - skip
    low = jnp.bfloat16
    f32 = jnp.float32
    owned = {device for row in owners for device in row}

    def body(
        core_ref, first_result, first_two, att, middle, two_ref, cot, wo, gain_ref, up, down,
        result_ref, d_middle_ref, d_own, keep, give,
        result, d_two,
    ):
        step = pl.program_id(0)
        cot_flat = cot[...].reshape(tokens, width)
        active, slope = gelu_pair(dot(two_ref[...], up[...], 1, 0))
        d_hidden = (dot(cot_flat, down[...], 1, 1) * slope).astype(low)
        forward = dot(active.astype(low), down[...], 1, 0)
        backward = dot(d_hidden, up[...], 1, 1)

        @pl.when(step == 0)
        def _():
            result[...] = first_result[...] + forward
            d_two[...] = first_two[...] + backward

        @pl.when(step > 0)
        def _():
            result[...] += forward
            d_two[...] += backward

        @pl.when(step == steps - 1)
        def _():
            result_ref[...] = (middle[...] + result[...]).astype(low).reshape(streams, rows, width)
            unit, root = normalize(middle[...])
            d_middle = cot_flat.astype(f32) + normalize_back(
                d_two[...], unit, root, gain_ref[...]
            )
            d_middle_ref[...] = d_middle
            branch = d_middle.astype(low)
            d_att = dot(branch, wo[...], 1, 1).T.astype(low)
            total = jnp.zeros((width, width), f32)
            for stream in range(streams):
                rows_of = slice(stream * rows, (stream + 1) * rows)
                for head, owner in enumerate(owners[stream]):
                    d_own[owner] = d_att[head * HEAD_DIM : (head + 1) * HEAD_DIM, rows_of]
                flat = jnp.concatenate([att[owner] for owner in owners[stream]], axis=0)
                total += dot(flat, branch[rows_of], 1, 0)
            for spare in range(devices):
                if spare not in owned:
                    d_own[spare] = jnp.zeros((head_width, rows), low)
            first = core_ref[0] == 0
            keep[...] = jnp.where(first, total[:, :half], total[:, half:])
            give[...] = jnp.where(first, total[:, half:], total[:, :half]).astype(low)

    shapes = (
        ((streams, rows, width), low),
        ((tokens, width), f32),
        ((devices, head_width, rows), low),
        ((width, half), f32),
        ((width, half), low),
    )
    return pl.pallas_call(
        body,
        grid=(steps,),
        out_shape=tuple(jax.ShapeDtypeStruct(*entry) for entry in shapes),
        in_specs=[
            SMEM, whole((tokens, width)), whole((tokens, width)),
            whole(attended.shape), whole(middle.shape), whole(two.shape),
            whole(cotangent.shape), whole(w_out.shape), whole((1, width)),
            pl.BlockSpec((width, chunk), lambda i: (0, i + skip)),
            pl.BlockSpec((chunk, width), lambda i: (i + skip, 0)),
        ],
        out_specs=tuple(whole(shape) for shape, _ in shapes),
        scratch_shapes=[pltpu.VMEM((tokens, width), f32), pltpu.VMEM((tokens, width), f32)],
        compiler_params=LIMIT,
        cost_estimate=busy(10),
        name="feed_rest",
    )(core, *so_far, attended, middle, two, cotangent, w_out, gain[None, :], w_up, w_down)


def hidden_gradients(where, two, cot, w_up, w_down, slots, planes):
    _, tokens, width = two[0].shape
    count = len(two)
    hidden = w_up.shape[1] // slots
    rows = width // planes
    height = 2 * rows
    low = jnp.bfloat16

    def body(where_ref, *rest):
        two_refs, cot_refs, (up, down) = rest[:count], rest[count : 2 * count], rest[2 * count :][:2]
        rest = rest[2 * count + 2 :]
        outs, (up_sum, down_sum) = rest[:planes], rest[planes:]
        step = pl.program_id(0)

        def run(two_ref, cot_ref):
            two = two_ref[...].reshape(2 * tokens, width)
            cot = cot_ref[...].reshape(2 * tokens, width)
            active, slope = gelu_pair(dot(two, up[...], 1, 0))
            d_hidden = (dot(cot, down[...], 1, 1) * slope).astype(low)
            up_term = dot(two, d_hidden, 0, 0)
            down_term = dot(active.astype(low), cot, 0, 0)

            @pl.when(step == 0)
            def _():
                up_sum[...] = up_term
                down_sum[:hidden] = down_term[:, :hidden]
                down_sum[hidden:] = down_term[:, hidden:]

            @pl.when(step > 0)
            def _():
                up_sum[...] += up_term
                down_sum[:hidden] += down_term[:, :hidden]
                down_sum[hidden:] += down_term[:, hidden:]

        for index, refs in enumerate(zip(two_refs, cot_refs)):
            pl.when(step == index)(functools.partial(run, *refs))

        @pl.when(step == count - 1)
        def _():
            for index, out in enumerate(outs):
                plane = lax.rem(where_ref[1] + index, planes)
                rows_of = pl.ds(pl.multiple_of(plane * rows, rows), rows)
                out[:rows] = up_sum[rows_of, :].astype(low)
                out[rows:] = down_sum[rows_of, :].astype(low)

    return pl.pallas_call(
        body,
        grid_spec=pltpu.PrefetchScalarGridSpec(
            num_scalar_prefetch=1,
            grid=(count,),
            in_specs=[
                *[whole(two[0].shape)] * (2 * count),
                pl.BlockSpec((width, hidden), lambda i, where: (0, where[0])),
                pl.BlockSpec((hidden, width), lambda i, where: (where[0], 0)),
            ],
            out_specs=[whole((height, hidden))] * planes,
            scratch_shapes=[
                pltpu.VMEM((width, hidden), jnp.float32),
                pltpu.VMEM((width, hidden), jnp.float32),
            ],
        ),
        out_shape=[jax.ShapeDtypeStruct((height, hidden), low)] * planes,
        compiler_params=LIMIT,
        cost_estimate=busy(12),
        name="hidden_gradients",
    )(where, *two, *cot, w_up, w_down)


def place_hidden(where, pieces, placed, w_up, gain, planes, last):
    count = len(pieces)
    hidden = pieces[0][0].shape[1]
    width = w_up.shape[0]
    rows = width // planes
    f32 = jnp.float32
    second = placed is not None

    def body(where_ref, *rest):
        refs, (up_ref, gain_ref), rest = rest[: 2 * count], rest[2 * count :][:2], rest[2 * count + 2 :]
        gain_before = rest[2] if second else None
        up_out, down_out, gain_out, sums = rest[3:] if second else rest
        step = pl.program_id(0)

        def put(first_ref, others_ref):
            for index in range(planes):
                plane = lax.rem(where_ref[1, 0] + planes - index, planes)
                rows_of = pl.ds(pl.multiple_of(plane * rows, rows), rows)
                ref, first = (others_ref, 2 * rows * (index - 1)) if index else (first_ref, 0)
                up_out[rows_of, :] = ref[first : first + rows].astype(f32)
                down = ref[first + rows : first + 2 * rows].astype(f32)
                row = plane * rows
                held = pl.ds(pl.multiple_of(lax.rem(row, hidden), rows), rows)

                @pl.when(row < hidden)
                def _():
                    down_out[held, :hidden] = down

                @pl.when(row >= hidden)
                def _():
                    down_out[held, hidden:] = down

        for index in range(count):
            pl.when(step == index)(functools.partial(put, *refs[2 * index : 2 * index + 2]))
        terms = jnp.sum(up_out[...] * up_ref[...].astype(f32), axis=1, keepdims=True)

        @pl.when(step == 0)
        def _():
            sums[...] = terms

        @pl.when(step > 0)
        def _():
            sums[...] += terms

        @pl.when(step == count - 1)
        def _():
            row = as_row(sums[...])
            row = row + gain_before[...][None, :] if second else row
            gain_out[...] = (row / gain_ref[...])[0] if last else row[0]

    unused = [pl.BlockSpec(memory_space=pl.ANY)] * 2 + [whole((width,))]
    return pl.pallas_call(
        body,
        grid_spec=pltpu.PrefetchScalarGridSpec(
            num_scalar_prefetch=1,
            grid=(count,),
            in_specs=[whole(part.shape) for pair in pieces for part in pair]
            + [
                pl.BlockSpec((width, hidden), lambda i, where: (0, where[0, i])),
                whole((1, width)),
            ]
            + (unused if second else []),
            out_specs=[
                pl.BlockSpec((width, hidden), lambda i, where: (0, where[0, i])),
                pl.BlockSpec((hidden, width), lambda i, where: (where[0, i], 0)),
                whole((width,)),
            ],
            scratch_shapes=[pltpu.VMEM((width, 1), f32)],
        ),
        out_shape=[
            jax.ShapeDtypeStruct(w_up.shape, f32),
            jax.ShapeDtypeStruct(w_up.shape[::-1], f32),
            jax.ShapeDtypeStruct((width,), f32),
        ],
        input_output_aliases={2 * count + 3: 0, 2 * count + 4: 1} if second else {},
        compiler_params=LIMIT,
        cost_estimate=busy(0.2),
        name="place_hidden",
    )(where, *[part for pair in pieces for part in pair], w_up, gain[None, :], *(placed or []))


def place_heads(core, mine, other, weights, gain, owners):
    chips, height, width = mine.shape
    half = width // 2
    quarter = width // 4
    size = height - 3 * HEAD_DIM
    f32 = jnp.float32

    def body(core_ref, mine_ref, other_ref, wq, wk, wv, gain_ref, dq, dk, dv, out, gain_out):
        def rows_of_device(plane, row, core, rows):
            entry = chips - 1 - plane if row else plane
            own = core_ref[0] == core
            return jnp.where(own, mine_ref[entry, rows], other_ref[entry, rows])

        for spot in range(4):
            for core in range(2):
                first = (spot if core else spot % 2 * 2 + spot // 2) * quarter
                columns = slice(core * half, (core + 1) * half)
                held = slice(spot % 2 * half, (spot % 2 + 1) * half)
                for plane in range(quarter // size):
                    piece = rows_of_device(plane, spot // 2, core, slice(3 * HEAD_DIM, height))
                    rows_of = slice(first + plane * size, first + (plane + 1) * size)
                    out[rows_of, columns] = piece[:, held].astype(f32)
        terms = jnp.zeros((width, 1), f32)
        for kind, (weight, target) in enumerate(((wq, dq), (wk, dk), (wv, dv))):
            rows = slice(kind * HEAD_DIM, (kind + 1) * HEAD_DIM)
            pieces = [
                rows_of_device(owner // 8, owner // 4 % 2, owner % 2, rows) for owner in owners[0]
            ]
            grad = jnp.concatenate(pieces, axis=0).T.astype(f32)
            target[...] = grad
            terms += jnp.sum(grad * weight[...].astype(f32), axis=1, keepdims=True)
        gain_out[...] = (as_row(terms) / gain_ref[...])[0]

    return pl.pallas_call(
        body,
        out_shape=[jax.ShapeDtypeStruct((width, width), f32)] * 4
        + [jax.ShapeDtypeStruct((width,), f32)],
        in_specs=[SMEM] + [VMEM] * 6,
        out_specs=[VMEM] * 5,
        compiler_params=LIMIT,
        cost_estimate=busy(0.2),
        name="place_heads",
    )(core, mine, other, *weights, gain[None, :])


def input_gradient(grads, weights, block_input, gain, d_middle, owners):
    streams, rows, width = block_input.shape

    def body(d_ref, wq, wk, wv, x_ref, gain_ref, d_middle_ref, out):
        for stream in range(streams):
            d_normed = jnp.zeros((rows, width), jnp.float32)
            for kind, weight in enumerate((wq, wk, wv)):
                rows_of = slice(kind * HEAD_DIM, (kind + 1) * HEAD_DIM)
                flat = jnp.concatenate([d_ref[owner, rows_of] for owner in owners[stream]], axis=0)
                d_normed += dot(flat.T, weight[...], 1, 1)
            unit, root = normalize(x_ref[stream].astype(jnp.float32))
            d_values = normalize_back(d_normed, unit, root, gain_ref[...])
            out[stream] = d_middle_ref[stream * rows : (stream + 1) * rows] + d_values

    return pl.pallas_call(
        body,
        out_shape=jax.ShapeDtypeStruct(block_input.shape, jnp.float32),
        in_specs=[VMEM] * 7,
        out_specs=VMEM,
        compiler_params=LIMIT,
        cost_estimate=busy(0.2),
        name="input_gradient",
    )(grads, *weights, block_input, gain[None, :], d_middle)


def wide(ref, frame, spaces, first, last, count=1):
    return jnp.concatenate(
        [ref[frame * spaces + j, first:last, :] for j in range(spaces * count)], axis=1
    )


def attend(lo, packed, frames):
    devices, _, rows = packed.shape
    spaces = devices // frames
    per_frame = rows * spaces
    dim = HEAD_DIM

    def body(lo_ref, r_ref, o_ref, low_ref, lse_ref, kv, top, total, summed):
        def turn_keys(device, _):
            kv[pl.ds(pl.multiple_of(device * rows, rows), rows), :] = r_ref[device, dim:, :].T
            return 0

        lax.fori_loop(0, devices, turn_keys, 0, unroll=4)

        def group(queries, _):
            first = queries * CLIP
            query = [wide(r_ref, first + i, spaces, 0, dim) for i in range(CLIP)]

            def update(i, keys, scores, fresh):
                fold = lambda op, value: op(value.reshape(-1, 8, per_frame), axis=0)
                new_top = fold(jnp.max, scores[0])
                for part in scores[1:]:
                    new_top = jnp.maximum(new_top, fold(jnp.max, part))
                new_top = jnp.max(new_top, axis=0, keepdims=True)
                if not fresh:
                    old_top = top[i]
                    new_top = jnp.maximum(old_top, new_top)
                new_total, new_sum = 0.0, 0.0
                for j, part in enumerate(scores):
                    weights = jnp.exp(part - new_top)
                    new_total += fold(jnp.sum, weights)
                    values = wide(r_ref, keys * CLIP + j, spaces, 2 * dim, 3 * dim)
                    new_sum += dot(values, weights.astype(jnp.bfloat16), 1, 0)
                new_total = jnp.sum(new_total, axis=0, keepdims=True)
                if not fresh:
                    factor = jnp.exp(old_top - new_top)
                    new_total += total[i] * factor
                    new_sum += summed[i] * factor
                top[i] = new_top
                total[i] = new_total
                summed[i] = new_sum

            def against(keys, counts, fresh):
                scores = []
                for i, count in enumerate(counts):
                    rows_of = [
                        pl.ds(pl.multiple_of((keys * CLIP + j) * per_frame, per_frame), per_frame)
                        for j in range(count)
                    ]
                    scores.append([dot(kv[part, :dim], query[i], 1, 0) for part in rows_of])
                for i in range(CLIP):
                    update(i, keys, scores[i], fresh)

            against(queries, range(1, CLIP + 1), True)

            def earlier(keys, _):
                against(keys, [CLIP] * CLIP, False)
                return 0

            lax.fori_loop(lo_ref[first] // CLIP, queries, earlier, 0)
            for i in range(CLIP):
                out = summed[i] / total[i]
                for j in range(spaces):
                    piece = out[:, j * rows : (j + 1) * rows]
                    o_ref[(first + i) * spaces + j] = piece
                    low_ref[(first + i) * spaces + j] = piece.astype(jnp.bfloat16)
                lse_ref[first + i] = top[i] + jnp.log(total[i])
            return 0

        lax.fori_loop(0, frames // CLIP, group, 0)

    f32 = jnp.float32
    return pl.pallas_call(
        body,
        out_shape=(
            jax.ShapeDtypeStruct((devices, dim, rows), f32),
            jax.ShapeDtypeStruct((devices, dim, rows), jnp.bfloat16),
            jax.ShapeDtypeStruct((frames, 1, per_frame), f32),
            jax.ShapeDtypeStruct((devices * rows, 2 * dim), jnp.bfloat16),
        ),
        in_specs=[SMEM, VMEM],
        out_specs=(VMEM,) * 4,
        scratch_shapes=[
            pltpu.VMEM((CLIP, 1, per_frame), f32),
            pltpu.VMEM((CLIP, 1, per_frame), f32),
            pltpu.VMEM((CLIP, dim, per_frame), f32),
        ],
        compiler_params=LIMIT,
        cost_estimate=busy(28),
        name="attend",
    )(lo, packed)


def attend_back(hi, packed, d_own, lse, kv, tables, rest, frames, start, stop):
    devices, _, rows = packed.shape
    spaces = devices // frames
    per_frame = rows * spaces
    dim = HEAD_DIM
    last = stop * CLIP == frames
    f32 = jnp.float32
    shift = dim if last else 0
    base = 0 if last else start * CLIP * spaces

    def body(hi_ref, r_ref, d_ref, lse_ref, kv_ref, table_ref, *rest):
        if last:
            delta_ref, qd_ref, before, piece, where_ref, near_ref, far_ref, *rest = rest
            out, product_out, acc, left, d_query_ref, product, near, far, sems = rest
        else:
            o_ref, out, d_query_ref, qd_ref, delta_ref, acc, left = rest

        def begin(frame, _):
            d_query_ref[frame] = jnp.zeros((dim, per_frame), f32)
            for j in range(spaces):
                device = frame * spaces + j
                both = jnp.concatenate([r_ref[device, :dim, :], d_ref[device]], axis=0)
                qd_ref[pl.ds(pl.multiple_of(device * rows, rows), rows), :] = both.T
                delta_ref[frame, :, j * rows : (j + 1) * rows] = jnp.sum(
                    d_ref[device].astype(f32) * o_ref[device], axis=0, keepdims=True
                )
            return 0

        def fetch(pair, slot):
            plane = pair // 2
            entry = jnp.where(pair % 2 == 0, plane, frames // 2 - 1 - plane)
            return [
                pltpu.make_async_copy(source.at[pl.ds(2 * entry, 2)], target.at[slot], sems.at[slot, i])
                for i, (source, target) in enumerate(((near_ref, near), (far_ref, far)))
            ]

        if last:
            for copy in fetch(0, 0):
                copy.start()
            pltpu.sync_copy(before, d_query_ref)
        else:
            lax.fori_loop(0, frames, begin, 0, unroll=2)
        if last:
            out[: piece.shape[0], dim:, :] = piece[...]
        first_half = lax.broadcasted_iota(jnp.int32, (per_frame, 2 * dim), 1) < dim

        def group(keys, _):
            first = keys * CLIP
            for i in range(CLIP):
                rows_of = pl.ds(pl.multiple_of((first + i) * per_frame, per_frame), per_frame)
                both = kv_ref[rows_of, :]
                zero = jnp.zeros_like(both)
                left[i, :per_frame] = jnp.where(first_half, both, zero)
                left[i, per_frame:] = jnp.where(first_half, zero, both)

            def against(queries, lead, fresh):
                own = queries * CLIP
                d_scores = [[] for _ in range(CLIP)]
                right = []
                for n in range(CLIP):
                    d_rows = [d_ref[(own + n) * spaces + j] for j in range(spaces)]
                    both = [wide(r_ref, own + n, spaces, 0, dim), jnp.concatenate(d_rows, axis=1)]
                    right.append(jnp.concatenate(both, axis=0))
                for i in range(CLIP):
                    term = 0.0
                    taken = range(i if lead else 0, CLIP)
                    products = [dot(left[i], right[n], 1, 0) for n in taken]
                    pairs = []
                    for n, both in zip(taken, products):
                        weights = jnp.exp(both[:per_frame] - lse_ref[own + n])
                        change = weights * (both[per_frame:] - delta_ref[own + n])
                        d_scores[n].append(change.astype(jnp.bfloat16))
                        pairs.append(
                            jnp.concatenate([weights.astype(jnp.bfloat16), d_scores[n][-1]], axis=0)
                        )
                    for n, pair in zip(taken, pairs):
                        rows_of = pl.ds(pl.multiple_of((own + n) * per_frame, per_frame), per_frame)
                        term += dot(pair, qd_ref[rows_of, :], 1, 0)
                    if fresh:
                        acc[i] = term
                    else:
                        acc[i] += term
                for n in range(CLIP):
                    keys_of = [
                        wide(r_ref, first + i, spaces, dim, 2 * dim) for i in range(len(d_scores[n]))
                    ]
                    d_query_ref[own + n] += dot(
                        jnp.concatenate(keys_of, axis=1), jnp.concatenate(d_scores[n], axis=0), 1, 0
                    )

            against(keys, True, True)

            def later(queries, _):
                against(queries, False, False)
                return 0

            lax.fori_loop(keys + 1, hi_ref[first] // CLIP, later, 0)
            for i in range(CLIP):
                total = acc[i]
                d_key = total[per_frame:].T[:dim]
                d_key = turned(d_key, table_ref[first + i, 0], table_ref[first + i, 1], -1.0)
                d_key = d_key.astype(jnp.bfloat16)
                d_value = total[:per_frame].T[dim:].astype(jnp.bfloat16)
                for j in range(spaces):
                    device = (first + i) * spaces + j - base
                    columns = slice(j * rows, (j + 1) * rows)
                    out[device, shift : shift + dim, :] = d_key[:, columns]
                    out[device, shift + dim : shift + 2 * dim, :] = d_value[:, columns]
            return 0

        lax.fori_loop(start, stop, group, 0)
        if last:

            def finish(frame, _):
                whole_query = d_query_ref[frame] * (1.0 / math.sqrt(dim))
                whole_query = turned(whole_query, table_ref[frame, 0], table_ref[frame, 1], -1.0)
                whole_query = whole_query.astype(jnp.bfloat16)
                for j in range(spaces):
                    out[frame * spaces + j, :dim, :] = whole_query[:, j * rows : (j + 1) * rows]
                return 0

            lax.fori_loop(0, frames, finish, 0)

            core = where_ref[0]
            product[...] = jnp.zeros_like(product)

            def multiply(pair, _):
                slot = lax.rem(pair, 2)

                @pl.when(pair + 1 < frames // 2)
                def _():
                    for copy in fetch(pair + 1, 1 - slot):
                        copy.start()

                for copy in fetch(pair, slot):
                    copy.wait()
                lefts, rights = [], []
                for index in range(2):
                    frame = 2 * pair + index
                    lefts += [out[spaces * frame + core], out[spaces * frame + 1 - core]]
                    rights += [near[slot, index], far[slot, index]]
                product[...] += dot(
                    jnp.concatenate(lefts, axis=1), jnp.concatenate(rights, axis=0), 1, 0
                )
                return 0

            lax.fori_loop(0, frames // 2, multiply, 0)
            product_out[...] = product[...].astype(jnp.bfloat16)

    inputs = [hi, packed, d_own, lse, kv, tables, *rest]
    in_specs = [SMEM] + [VMEM] * 5
    query_sum = jax.ShapeDtypeStruct((frames, dim, per_frame), f32)
    scratch = [
        pltpu.VMEM((CLIP, 2 * per_frame, 2 * dim), f32),
        pltpu.VMEM((CLIP, 2 * per_frame, 2 * dim), jnp.bfloat16),
    ]
    if last:
        width = rest[-1].shape[2]
        in_specs += [VMEM, VMEM, ANY, VMEM, SMEM, ANY, ANY]
        out_shape = (
            jax.ShapeDtypeStruct((devices, 3 * dim, rows), jnp.bfloat16),
            jax.ShapeDtypeStruct((3 * dim, width), jnp.bfloat16),
        )
        scratch += [
            pltpu.VMEM((frames, dim, per_frame), f32),
            pltpu.VMEM((3 * dim, width), f32),
            pltpu.VMEM((2, 2, rows, width), jnp.bfloat16),
            pltpu.VMEM((2, 2, rows, width), jnp.bfloat16),
            pltpu.SemaphoreType.DMA((2, 2)),
        ]
    else:
        shape = ((stop - start) * CLIP * spaces, 2 * dim, rows)
        in_specs += [VMEM]
        out_shape = (
            jax.ShapeDtypeStruct(shape, jnp.bfloat16),
            query_sum,
            jax.ShapeDtypeStruct((devices * rows, 2 * dim), jnp.bfloat16),
            jax.ShapeDtypeStruct((frames, 1, per_frame), f32),
        )
    return pl.pallas_call(
        body,
        out_shape=out_shape,
        in_specs=in_specs,
        out_specs=(VMEM,) * len(out_shape),
        scratch_shapes=scratch,
        compiler_params=LIMIT,
        cost_estimate=busy(20),
        name="attend_back",
    )(*inputs)


def after(value, *others):
    return lax.optimization_barrier((value, *others))[0]


class Ring:
    def __init__(self):
        self.frames = lax.axis_size("frame")
        self.spaces = lax.axis_size("space")
        self.planes = self.frames // 4
        self.frame = lax.axis_index("frame")
        self.core = lax.axis_index("space")
        self.plane = self.frame // 4
        self.spot = self.frame % 4
        bits = (self.frame % 2, (self.frame // 2) % 2)
        self.first_bit = jnp.where(self.core == 0, bits[0], bits[1])
        self.second_bit = jnp.where(self.core == 0, bits[1], bits[0])

    def send(self, value, target):
        moves = []
        for frame in range(self.frames):
            for core in range(self.spaces):
                to_frame, to_core = target(frame, core)
                moves.append((frame * self.spaces + core, to_frame * self.spaces + to_core))
        return lax.ppermute(value, ("frame", "space"), moves)

    def first(self, value):
        return self.send(value, lambda frame, core: (frame ^ (1 if core == 0 else 2), core))

    def second(self, value):
        return self.send(value, lambda frame, core: (frame ^ (2 if core == 0 else 1), core))

    def across(self, value):
        return self.send(value, lambda frame, core: (frame, 1 - core))

    def up(self, value, step):
        size = self.frames
        return self.send(value, lambda frame, core: ((frame + 4 * step) % size, core))

    def send_planes(self, pieces):
        return [self.up(piece, step) for step, piece in enumerate(pieces[1:], 1)]

    def plane_part(self, value):
        groups = [list(range(spot, self.frames, 4)) for spot in range(4)]
        if value.shape[0] % (16 * self.planes):
            return lax.psum(value, "frame", axis_index_groups=groups)
        return lax.psum_scatter(
            value, "frame", scatter_dimension=0, axis_index_groups=groups, tiled=True
        )

    def add_planes(self, own, arrived):
        total = own.astype(jnp.float32)
        for piece in arrived:
            total = total + piece.astype(jnp.float32)
        return total.astype(jnp.bfloat16)

    def spread_planes(self, value, count):
        return [self.up(value, step) for step in range(1, count)]

    def gather_spots(self):
        near = jnp.where(self.core == 0, 2, 1)
        own = jnp.stack([self.spot, self.spot ^ near, self.spot ^ (3 - near), self.spot ^ 3])
        other = jnp.stack([self.spot, self.spot ^ (3 - near), self.spot ^ near, self.spot ^ 3])
        cores = jnp.repeat(jnp.stack([self.core, 1 - self.core]), 4)
        return jnp.concatenate([own, other]), cores

    def halves(self, value, bit):
        rows, columns = value.shape
        cut = value.reshape(2, rows // 2, columns)
        pick = lambda index: lax.dynamic_index_in_dim(cut, index, 0, keepdims=False)
        return pick(bit), pick(1 - bit).astype(jnp.bfloat16)


def frame_limits(clip_frames, frames):
    ends = jnp.cumsum(clip_frames, axis=1, dtype=jnp.int32)
    begins = ends - clip_frames
    index = jnp.arange(frames, dtype=jnp.int32)[None, :, None]
    inside = (index >= begins[:, None, :]) & (index < ends[:, None, :])
    pick = lambda table: jnp.sum(jnp.where(inside, table[:, None, :], 0), axis=2, dtype=jnp.int32)
    return pick(begins), pick(ends)


def local(
    block_input,
    norm1_gain,
    w_query,
    w_key,
    w_value,
    w_out,
    norm2_gain,
    w_up,
    w_down,
    clip_frames,
    cotangent,
):
    streams, rows, width = block_input.shape
    ring = Ring()
    frames, spaces, planes = ring.frames, ring.spaces, ring.planes
    devices = frames * spaces
    per_frame = rows * spaces
    tokens = streams * rows
    axes = ("frame", "space")
    low = jnp.bfloat16
    core = jnp.reshape(ring.core, (1,))
    spots, cores = ring.gather_spots()
    slots = 4 * spaces

    owners = head_owners(frames, spaces)
    w_projections = (w_query, w_key, w_value)
    side = ring.frame % 2

    def swap(value):
        return lax.all_to_all(value, axes, 0, 0, tiled=True)

    spot_of = jnp.stack([ring.frame, ring.core * rows])
    sent, normed = project(
        spot_of, clip_frames, block_input, norm1_gain, *w_projections, owners, devices, per_frame
    )
    packed = swap(sent)

    begin, end = frame_limits(after(clip_frames, sent), frames)
    frame_ids = jnp.arange(frames, dtype=jnp.int32)
    mine = ring.frame * spaces + ring.core
    idle = ~jnp.any(mine == jnp.asarray(owners))
    lo = jnp.where(idle, frame_ids, jnp.where(side == 0, begin[0], begin[1]))
    hi = jnp.where(idle, frame_ids, jnp.where(side == 0, end[0], end[1]))

    neighbour = lambda value: ring.send(value, lambda frame, core: (frame ^ 1, core))
    stream_near = neighbour(lax.dynamic_index_in_dim(normed, 1 - side, 0))
    stream_own = lax.dynamic_index_in_dim(normed, side, 0)
    stream_pair = jnp.where(
        side == 0,
        jnp.concatenate([stream_own, stream_near]),
        jnp.concatenate([stream_near, stream_own]),
    )
    up, down = range(planes), range(planes)[::-1]
    same_side = [
        [4 * plane + bit for plane in up] + [4 * plane + 2 + bit for plane in down] for bit in range(2)
    ]
    stream_mine = lax.all_gather(
        stream_pair, "frame", axis=0, tiled=True, axis_index_groups=same_side
    )
    cot_flat = cotangent.reshape(tokens, width)
    cot_one = ring.second(cot_flat)
    out, out_low, lse, kv = attend(lo, after(packed, stream_pair), frames)
    cot_pair = jnp.stack([cot_flat, after(cot_one, out_low)])
    attended = swap(after(out_low, cot_pair))
    tables = rope_tables(after(lo, out_low), frames, per_frame)
    attended = after(attended, tables)
    cot_far = ring.first(cot_pair)

    middle, two = attention_out(attended, block_input, w_out, norm2_gain, owners)
    chunk, skip = 768, 2
    cot_far = after(cot_far, middle)
    cot_plane = [cot_pair, cot_far, ring.across(cot_pair), ring.across(cot_far)]
    so_far = feed_first(two, cotangent, w_up, w_down, chunk, skip)
    two_pair = jnp.stack([two, ring.second(two)])
    so_far = after(so_far, two_pair, stream_mine)
    two_far = ring.first(two_pair)
    two_pair_other = ring.across(two_pair)
    block_output, d_middle, d_sent, out_keep, out_give = feed_rest(
        core, so_far, attended, middle, two, cotangent, w_out, norm2_gain, w_up, w_down,
        chunk, skip, owners,
    )
    d_own = swap(d_sent)
    two_far, two_pair_other = after((two_far, two_pair_other), d_sent)
    two_plane = [two_pair, two_far, two_pair_other, ring.across(two_far)]
    out_sum = out_keep + ring.across(out_give).astype(jnp.float32)
    out_keep, out_give = ring.halves(out_sum, ring.first_bit)
    out_other = ring.first(out_give)
    pieces = hidden_gradients(
        jnp.stack([ring.spot * spaces + ring.core, ring.plane]),
        after(two_plane, out_give), cot_plane, w_up, w_down, slots, planes,
    )

    arrived = ring.send_planes(pieces)
    out_sum = out_keep + after(out_other, pieces[0]).astype(jnp.float32)
    out_keep, out_give = ring.halves(out_sum, ring.second_bit)
    out_sum = (out_keep + ring.second(out_give).astype(jnp.float32)).astype(low)
    d_own = after(d_own, out_sum)
    out_sum = ring.plane_part(out_sum)
    groups = frames // CLIP
    first_part, d_query, qd, delta = attend_back(
        hi, packed, d_own, lse, kv, tables, (out,), frames, 0, groups // 2
    )
    total = ring.add_planes(pieces[0], after(arrived, first_part))
    stream_other = ring.across(stream_mine)
    grads, product = attend_back(
        hi, packed, d_own, lse, kv, tables,
        (after(delta, total, out_sum), qd, d_query, first_part, jnp.reshape(ring.core, (1,)),
         stream_mine, stream_other),
        frames, groups // 2, groups,
    )
    spread = ring.spread_planes(total, planes)
    own_one, own_two = ring.second(total), ring.first(total)
    spread, own_one, own_two, own_product = lax.optimization_barrier(
        (spread, own_one, own_two, product)
    )
    back = swap(grads)
    heads_sum = own_product.astype(jnp.float32) + neighbour(product).astype(jnp.float32)
    out_other = neighbour(out_sum)
    out_pair = jnp.where(
        side == 0,
        jnp.concatenate([out_sum, out_other], axis=1),
        jnp.concatenate([out_other, out_sum], axis=1),
    )
    heads_sum = jnp.concatenate([heads_sum.astype(low), out_pair])
    heads_mine = lax.all_gather(heads_sum, "frame", axis_index_groups=same_side)
    rest = after(jnp.concatenate(spread), heads_sum)
    one, two = (own_one, ring.second(rest)), (own_two, ring.first(rest))
    three = tuple(ring.first(part) for part in (one[0], after(one[1], back)))
    own = (total, rest)
    both_across = lambda pair: (ring.across(pair[0]), ring.across(pair[1]))
    own_other = both_across(own)
    grad_input = input_gradient(back, w_projections, block_input, norm1_gain, d_middle, owners)
    unit_slots = spots * spaces + cores
    where = jnp.stack([unit_slots, jnp.broadcast_to(ring.plane, cores.shape)])
    places = lambda *entries: jnp.stack([where[:, entry] for entry in entries], axis=1)
    placed = place_hidden(places(0, 4), [own, own_other], None, w_up, norm2_gain, planes, False)
    one, two = after((one, two), placed[0], grad_input)
    pieces = [both_across(one), both_across(two)]
    placed = place_hidden(places(1, 2), [one, two], placed, w_up, norm2_gain, planes, False)
    pieces, heads_mine = after((pieces, heads_mine), placed[0])
    heads_other = ring.across(after(heads_mine, pieces))
    pieces = after(pieces, heads_mine)
    placed = place_hidden(places(5, 6), pieces, placed, w_up, norm2_gain, planes, False)
    grad_query, grad_key, grad_value, grad_out, gain_one = place_heads(
        jnp.reshape(ring.core, (1,)), heads_mine, after(heads_other, placed[0]),
        w_projections, norm1_gain, owners,
    )
    three = after(three, placed[0])
    three_other = after(both_across(three), grad_query)
    grad_up, grad_down, gain_two = place_hidden(
        places(3, 7), [three, three_other], placed, w_up, norm2_gain, planes, True
    )
    return (
        block_output,
        grad_input,
        gain_one,
        grad_query,
        grad_key,
        grad_value,
        grad_out,
        gain_two,
        grad_up,
        grad_down,
    )


def solution(mesh):
    spread = P(None, ("frame", "space"), None)
    in_specs = (spread,) + (P(),) * 9 + (spread,)
    out_specs = (spread, spread) + (P(),) * 8
    return jax.shard_map(local, mesh=mesh, in_specs=in_specs, out_specs=out_specs, check_vma=False)
```
